128 devices in a mesh: gx: 8 (over z_lo, y), gy: 8 (over x, core), gz: 2 (over z_hi).
Axes of the slice: x: 4, y: 4, z: 4 (z_hi: 2, z_lo: 2; z = z_hi * 2 + z_lo), core: 2. Of those that a mesh axis runs over, the one named last changes fastest.
Arguments:
- features: float32 [192, 192, 1536], P('gx', 'gy', 'gz'), may hold values from -6 to 6
- cotangent: float32 [192, 192, 1536], P('gx', 'gy', 'gz'), may hold values from -6 to 6
- skip_weight: float32 [32, 32], replicated, may hold values from -1 to 1
- bias_vector: float32 [32], replicated, may hold values from -3 to 3
- mode_factors: float32 [3, 3, 16, 64], replicated, may hold values from -4 to 4
- in_factors: float32 [3, 32, 64], replicated, may hold values from -1 to 1
- out_factors: float32 [3, 64, 32], replicated, may hold values from -0.75 to 0.75
Outputs:
- output: float32 [192, 192, 1536], P('gx', 'gy', 'gz')
- grad_skip: float32 [32, 32], replicated
- grad_bias: float32 [32], replicated
- grad_modes: float32 [3, 3, 16, 64], replicated
- grad_in: float32 [3, 32, 64], replicated
- grad_out: float32 [3, 64, 32], replicated
The draws below stay inside these ranges and needn't reach their ends.
All inputs are finite; a program needn't handle non-finite values.
Results may differ from the reference program's by a relative error of at most 0.0003.
Values sent between devices are 32-bit elements; how exact they have to be, the bound alone decides.
A program may use at most 256 MiB of HBM per device.

```python
import math
import jax
import jax.numpy as jnp
from jax import lax

C = 32
MODES = 16
RANK = 64
LEVELS = 3
P_SIZE = 24
NX = 192
NY = 192
NZ = 48
N_GX = 8
N_GY = 8
N_GZ = 2


def shard_levels(rng, dims, cuts, smallest, high):
    level, own = 1.0, jax.random.fold_in(rng, 6)
    for position, parts in cuts:
        draws = jnp.exp(jax.random.uniform(jax.random.fold_in(own, position), (parts,), jnp.float32, smallest / len(cuts), high / len(cuts)))
        level = level * jnp.repeat(draws, dims[position] // parts).reshape([-1 if axis == position else 1 for axis in range(len(dims))])
    return level


def noise(own_key, extent, width, bound, shards=(), held_as=jnp.bfloat16):
    drawn = jax.random.normal(own_key, extent, jnp.float32) * width
    if len(shards) > 0:
        drawn = shard_levels(own_key, extent, shards, -0.22, 0.18) * drawn
    return jnp.clip(drawn, min=-bound, max=bound).astype(held_as)


def setup_inputs(seed: int = 0) -> dict:
    key_of = jax.random.split(jax.random.key(seed), 8)
    features = noise(key_of[0], (NX, NY, NZ * C), 1.0, 6.0, ((0, 8), (1, 8), (2, 2)), jnp.float32)
    cotangent = noise(key_of[1], (NX, NY, NZ * C), 1.0, 6.0, ((0, 8), (1, 8), (2, 2)), jnp.float32)
    skip_weight = noise(key_of[2], (C, C), C ** -0.5, 1.0, (), jnp.float32)
    bias_vector = noise(key_of[3], (C,), 0.5, 3.0, (), jnp.float32)
    mode_factors = noise(key_of[4], (LEVELS, 3, MODES, RANK), 1.0, 4.0, (), jnp.float32)
    in_factors = noise(key_of[5], (LEVELS, C, RANK), C ** -0.5, 1.0, (), jnp.float32)
    out_factors = noise(key_of[6], (LEVELS, RANK, C), RANK ** -0.5, 0.75, (), jnp.float32)
    return {"features": features, "cotangent": cotangent, "skip_weight": skip_weight, "bias_vector": bias_vector, "mode_factors": mode_factors, "in_factors": in_factors, "out_factors": out_factors}


HIGHEST = lax.Precision.HIGHEST

def basis_table(length, modes):
    half_count = modes // 2
    mode_rows = jnp.arange(modes)
    frequency = jnp.where(mode_rows < half_count, mode_rows, mode_rows - half_count + 1).astype(jnp.float32)
    positions = jnp.arange(length).astype(jnp.float32)
    phases = 2.0 * math.pi / length * frequency[:, None] * positions[None, :]
    is_cosine = (mode_rows < half_count)[:, None]
    return jnp.where(is_cosine, jnp.cos(phases), jnp.sin(phases)) * math.sqrt(2.0 / length)

def spectral(grid, factor_modes, factor_in, factor_out):
    length = grid.shape[0]
    table = basis_table(length, factor_modes.shape[1])
    coeffs = jnp.einsum('ax,xyzi->ayzi', table, grid, precision=HIGHEST)
    coeffs = jnp.einsum('by,ayzi->abzi', table, coeffs, precision=HIGHEST)
    coeffs = jnp.einsum('cz,abzi->abci', table, coeffs, precision=HIGHEST)
    ranked = jnp.einsum('abci,ir->abcr', coeffs, factor_in, precision=HIGHEST)
    weights = factor_modes[0][:, None, None, :] * factor_modes[1][None, :, None, :] * factor_modes[2][None, None, :, :]
    result = jnp.einsum('abcr,ro->abco', ranked * weights, factor_out, precision=HIGHEST)
    result = jnp.einsum('ax,abco->xbco', table, result, precision=HIGHEST)
    result = jnp.einsum('by,xbco->xyco', table, result, precision=HIGHEST)
    return jnp.einsum('cz,xyco->xyzo', table, result, precision=HIGHEST)

def upsample(block, factor):
    block = jnp.repeat(block, factor, axis=0)
    block = jnp.repeat(block, factor, axis=1)
    return jnp.repeat(block, factor, axis=2)

def coarsen(field, factor):
    shape = field.shape
    split = field.reshape(shape[0] // factor, factor, shape[1] // factor, factor, shape[2] // factor, factor, shape[3])
    return lax.optimization_barrier(jnp.mean(split, axis=(1, 3, 5)))

def layer(params, fine_patch, half_grid, quarter_grid):
    skip_weight, bias_vector, mode_factors, in_factors, out_factors = params
    patch = fine_patch.shape[0]
    start = patch // 4
    preact = jnp.einsum('xyzi,io->xyzo', fine_patch, skip_weight, precision=HIGHEST) + bias_vector
    preact = preact + spectral(fine_patch, mode_factors[0], in_factors[0], out_factors[0])
    half_out = spectral(half_grid, mode_factors[1], in_factors[1], out_factors[1])
    half_out = half_out[start:start + patch // 2, start:start + patch // 2, start:start + patch // 2]
    preact = preact + upsample(half_out, 2)
    quarter_out = spectral(quarter_grid, mode_factors[2], in_factors[2], out_factors[2])
    quarter_out = quarter_out[start:start + patch // 4, start:start + patch // 4, start:start + patch // 4]
    preact = preact + upsample(quarter_out, 4)
    return jax.nn.gelu(preact)

def reference(features, cotangent, skip_weight, bias_vector, mode_factors, in_factors, out_factors):
    channels = skip_weight.shape[0]
    fine_field = features.reshape(NX, NY, NZ, channels)
    cot_field = cotangent.reshape(NX, NY, NZ, channels)
    half_field = coarsen(fine_field, 2)
    quarter_field = coarsen(half_field, 2)
    margin = P_SIZE // 4
    pad_spec = ((margin, margin), (margin, margin), (margin, margin), (0, 0))
    half_padded = jnp.pad(half_field, pad_spec)
    quarter_padded = jnp.pad(quarter_field, pad_spec)
    scale = 1.0 / math.sqrt(NX * NY * NZ)
    params = (skip_weight, bias_vector, mode_factors, in_factors, out_factors)
    zero_grads = jax.tree.map(jnp.zeros_like, params)
    quarter_len = 3 * P_SIZE // 4

    def visit(totals, patch_index):
        block_x = patch_index // (N_GY * N_GZ)
        block_y = patch_index // N_GZ % N_GY
        block_z = patch_index % N_GZ
        anchor = jnp.zeros((), jnp.int32)
        fine_patch = lax.dynamic_slice(fine_field, (block_x * P_SIZE, block_y * P_SIZE, block_z * P_SIZE, anchor), (P_SIZE, P_SIZE, P_SIZE, channels))
        cot_patch = lax.dynamic_slice(cot_field, (block_x * P_SIZE, block_y * P_SIZE, block_z * P_SIZE, anchor), (P_SIZE, P_SIZE, P_SIZE, channels))
        half_grid = lax.dynamic_slice(half_padded, (block_x * (P_SIZE // 2), block_y * (P_SIZE // 2), block_z * (P_SIZE // 2), anchor), (P_SIZE, P_SIZE, P_SIZE, channels))
        quarter_grid = lax.dynamic_slice(quarter_padded, (block_x * (P_SIZE // 4), block_y * (P_SIZE // 4), block_z * (P_SIZE // 4), anchor), (quarter_len, quarter_len, quarter_len, channels))
        result, pullback = jax.vjp(lambda values: layer(values, fine_patch, half_grid, quarter_grid), params)
        grads = pullback(cot_patch * scale)[0]
        return (jax.tree.map(jnp.add, totals, grads), result)
    totals, outputs = lax.scan(visit, zero_grads, jnp.arange(N_GX * N_GY * N_GZ, dtype=jnp.int32))
    outputs = outputs.reshape(N_GX, N_GY, N_GZ, P_SIZE, P_SIZE, P_SIZE, channels)
    outputs = outputs.transpose(0, 3, 1, 4, 2, 5, 6).reshape(NX, NY, NZ * channels)
    return (outputs, totals[0], totals[1], totals[2], totals[3], totals[4])
```

```python
import math

import jax
import jax.numpy as jnp
import ml_dtypes
import numpy as np
from jax import lax
from jax.experimental import pallas as pl
from jax.experimental.pallas import tpu as pltpu
from jax.sharding import PartitionSpec as P

MESH = pl.DeviceIdType.MESH
BF = jnp.bfloat16
F32 = jnp.float32
CH, RK, MD, NP = 32, 64, 16, 24
NN = (((1,), (0,)), ((), ()))
NT = (((1,), (1,)), ((), ()))
TN = (((0,), (0,)), ((), ()))
PAY = 192


def basis(length):
    rows = np.arange(MD)
    freq = np.where(rows < MD // 2, rows, rows - MD // 2 + 1).astype(np.float64)
    phase = 2.0 * math.pi / length * freq[:, None] * np.arange(length)[None, :]
    wave = np.where((rows < MD // 2)[:, None], np.cos(phase), np.sin(phase))
    return wave * math.sqrt(2.0 / length)


def halves(x):
    x = np.asarray(x, np.float32)
    hi = x.astype(ml_dtypes.bfloat16)
    lo = (x - hi.astype(np.float32)).astype(ml_dtypes.bfloat16)
    return hi, lo


def left(x):
    hi, lo = halves(x)
    return np.concatenate([hi, hi, lo], axis=1)


def right(x):
    hi, lo = halves(x)
    return np.concatenate([hi, lo], axis=0)


def exact(x, times, axis):
    x = np.asarray(x, np.float32).astype(ml_dtypes.bfloat16)
    return np.concatenate([x] * times, axis=axis)


def channel_eye(b):
    return np.kron(b, np.eye(CH))


def make_tables():
    b24, b18 = basis(24), basis(18)
    pool = np.zeros((208, 12, 24))
    for j in range(2):
        for i in range(2):
            for r in range(36):
                x, y = i * 6 + r // 6, 2 * (j * 6 + r % 6)
                pool[(j * 2 + i) * 40 + r, x, y : y + 2] = 1 / 8
    for r in range(36):
        x, y = 2 * (r // 6), 4 * (r % 6)
        pool[160 + r, x : x + 2, y : y + 4] = 1 / 64
    pool = pool.reshape(208, 288)
    pair = channel_eye(np.kron(np.eye(4), np.ones((2, 1))))
    quad = np.zeros((24, 8))
    for z in range(24):
        quad[z, z // 4] = 1
    quad = channel_eye(quad)
    xy0 = np.kron(b24, b24)
    xy1 = np.zeros((256, 4, 4, 40))
    for j in range(4):
        for i in range(4):
            for r in range(36):
                xy1[:, j, i, r] = np.kron(b24[:, i * 6 + r // 6], b24[:, j * 6 + r % 6])
    xy2 = np.zeros((256, 368))
    for j in range(3):
        for i in range(3):
            for r in range(36):
                xy2[:, (j * 3 + i) * 40 + r] = np.kron(
                    b18[:, i * 6 + r // 6], b18[:, j * 6 + r % 6]
                )
    z0 = channel_eye(b24.T)
    z1s, z2s = [], []
    for gz in range(2):
        z1 = np.zeros((20, 16))
        z1[0:12] = b24[:, 6:18].T
        if gz == 0:
            z1[12:18] = b24[:, 18:24].T
        else:
            z1[14:20] = b24[:, 0:6].T
        z1s.append(right(channel_eye(z1)))
        z2 = np.zeros((16, 16))
        z2[0:6] = b18[:, 6:12].T
        z2[8:14] = b18[:, 12:18].T if gz == 0 else b18[:, 0:6].T
        z2s.append(right(channel_eye(z2)))
    z1c = channel_eye(b24[:, 6:18])
    z2c = channel_eye(np.repeat(b18[:, 6:12], 2, axis=1))
    c1 = b24[:, 6:18]
    c2 = np.repeat(b18[:, 6:12], 2, axis=1)
    xy12 = np.concatenate([np.kron(c1, c1), np.kron(c2, c2)], axis=0)
    return {
        "pool": exact(pool, 2, 1),
        "pair": exact(pair, 2, 0),
        "quad": exact(quad, 2, 0),
        "unpair": exact(pair.T, 2, 0),
        "xy0": left(xy0),
        "z0": right(z0),
        "z0t": right(z0.T),
        "inv": left(xy0.T),
        "xy1": left(xy1.reshape(256, 640)),
        "z1": np.concatenate(z1s, axis=0),
        "xy2": left(xy2),
        "z2": np.concatenate(z2s, axis=0),
        "z1c": right(z1c),
        "z2c": right(z2c),
        "xy12": left(xy12.T),
        "xy12t": left(xy12),
        "z2ct": right(z2c.T),
    }


TABLES = make_tables()
NAMES = list(TABLES)


def table_shape(name):
    rows, cols = TABLES[name].shape
    return (rows // 2 if name in ("z1", "z2") else rows), cols


def dot(a, b, dims=NN):
    return lax.dot_general(a, b, dims, preferred_element_type=F32)


def split(x):
    hi = x.astype(BF)
    return hi, (x - hi.astype(F32)).astype(BF)


def rows_cat(*parts):
    return jnp.concatenate(parts, axis=0)


def lanes_cat(*parts):
    return jnp.concatenate(parts, axis=1)


def iota(shape, dim):
    return lax.broadcasted_iota(jnp.int32, shape, dim)


def fold_lanes(x):
    total = x[:, 0:128]
    for k in range(1, x.shape[1] // 128):
        total = total + x[:, 128 * k : 128 * (k + 1)]
    return total + pltpu.roll(total, 64, 1)


def layer_kernel(sizes, *refs):
    ngx, ngy, ngz = sizes
    refs = list(refs)
    take = lambda n: [refs.pop(0) for _ in range(n)]
    feat_hbm, cot_hbm, skip_ref, bias_ref, modes_ref, in_ref, out_ref = take(7)
    hbm = dict(zip(NAMES, take(len(NAMES))))
    result_hbm, red_ref = take(2)
    tab = dict(zip(NAMES, take(len(NAMES))))
    (feat, cot, result, fs, half, quart, hs, qs, kh, kl, pr, rh, rl, qh, ql, th, tl, bs, t12, pre, gs, gqh, gql, ghh, ghl,
     wide, down, g12h, g12l, um, m2r, m0t, m1t, inw, outw, outt, skw, biast, gskip, gbias, pay, ra, rb, acc, red) = take(45)
    table_sem, local_sem, halo_send, halo_recv, red_send, red_recv = take(6)

    gx, gy, gz = lax.axis_index("gx"), lax.axis_index("gy"), lax.axis_index("gz")
    me = gx * ngz + gz
    group = ngx * ngz

    load_f = pltpu.make_async_copy(feat_hbm, feat, local_sem.at[0])
    load_f.start()
    load_c = pltpu.make_async_copy(cot_hbm, cot, local_sem.at[1])
    loads = {}
    for k, name in enumerate(NAMES):
        rows = table_shape(name)[0]
        src = hbm[name].at[pl.ds(pl.multiple_of(gz * rows, 16), rows)] if name in ("z1", "z2") else hbm[name]
        loads[name] = pltpu.make_async_copy(src, tab[name], table_sem.at[k])
        if k < 3:
            loads[name].start()

    barrier = pltpu.get_barrier_semaphore()

    def greet_row(k, carry):
        pl.semaphore_signal(
            barrier, inc=1, device_id=(gx, lax.rem(gy + k, ngy), gz), device_id_type=MESH
        )
        return carry

    lax.fori_loop(1, ngy, greet_row, 0)

    def greet_plane(k, carry):
        q = lax.rem(me + k, group)
        pl.semaphore_signal(
            barrier, inc=1, device_id=(q // ngz, gy, lax.rem(q, ngz)), device_id_type=MESH
        )
        return carry

    lax.fori_loop(1, group, greet_plane, 0)

    @pl.when(gx == 0)
    def _():
        for j in (1, 2):
            half[j, 0] = jnp.zeros((40, 640), F32)
        quart[1, 0] = jnp.zeros((40, 512), F32)

    @pl.when(gx == ngx - 1)
    def _():
        for j in (1, 2):
            half[j, 3] = jnp.zeros((40, 640), F32)
        quart[1, 2] = jnp.zeros((40, 512), F32)

    @pl.when(gy == 0)
    def _():
        for i in range(4):
            half[0, i] = jnp.zeros((40, 640), F32)
        for i in range(3):
            quart[0, i] = jnp.zeros((40, 512), F32)

    @pl.when(gy == ngy - 1)
    def _():
        for i in range(4):
            half[3, i] = jnp.zeros((40, 640), F32)
        for i in range(3):
            quart[2, i] = jnp.zeros((40, 512), F32)

    load_f.wait()
    for name in NAMES[3:]:
        loads[name].start()
        if name == "xy2":
            load_c.start()
    cells = feat[...].reshape(12, 2, 24, 768)
    hi, lo = split((cells[:, 0] + cells[:, 1]).reshape(288, 768))
    gs[0:288] = hi
    gs[288:576] = lo
    loads["pool"].wait()
    for n in range(3):
        pre[0:208, 256 * n : 256 * (n + 1)] = dot(tab["pool"][...], gs[0:576, 256 * n : 256 * (n + 1)])
    hi, lo = split(pre[0:208])
    loads["pair"].wait()
    for n in range(3):
        cols = slice(256 * n, 256 * (n + 1))
        cells = dot(lanes_cat(hi[0:160, cols], lo[0:160, cols]), tab["pair"][...])
        for j in range(2):
            for i in range(2):
                r = (j * 2 + i) * 40
                half[j + 1, i + 1, :, 128 * n : 128 * (n + 1)] = cells[r : r + 40]
    loads["quad"].wait()
    cells = dot(lanes_cat(hi[160:208], lo[160:208]), tab["quad"][...])
    quart[1, 1, :, 0:256] = cells[0:40]

    pl.semaphore_wait(barrier, ngy - 1 + group - 1)

    def remote(k, src, dst, to):
        return pltpu.make_async_remote_copy(
            src_ref=src,
            dst_ref=dst,
            send_sem=halo_send.at[k],
            recv_sem=halo_recv.at[k],
            device_id=to,
            device_id_type=MESH,
        )

    first = pl.multiple_of(128 * (1 - gz), 128)
    own, far = pl.ds(0, 384), pl.ds(384, 256)
    up_x, down_x = (gx + 1, gy, gz), (gx - 1, gy, gz)
    up_y, down_y = (gx, gy + 1, gz), (gx, gy - 1, gz)
    across = (gx, gy, 1 - gz)
    mid = pl.ds(1, 2)
    z_half = remote(0, half.at[mid, mid, :, pl.ds(first, 256)], half.at[mid, mid, :, far], across)
    z_quart = remote(1, quart.at[1, 1, :, pl.ds(0, 256)], quart.at[1, 1, :, pl.ds(256, 256)], across)
    x_up = [
        remote(2, half.at[mid, 2, :, own], half.at[mid, 0, :, own], up_x),
        remote(3, half.at[mid, 2, :, far], half.at[mid, 0, :, far], up_x),
        remote(4, quart.at[1, 1], quart.at[1, 0], up_x),
    ]
    x_down = [
        remote(5, half.at[mid, 1, :, own], half.at[mid, 3, :, own], down_x),
        remote(6, half.at[mid, 1, :, far], half.at[mid, 3, :, far], down_x),
        remote(7, quart.at[1, 1], quart.at[1, 2], down_x),
    ]
    y_up = [
        remote(8, half.at[2, mid, :, own], half.at[0, mid, :, own], up_y),
        remote(9, half.at[2, mid, :, far], half.at[0, mid, :, far], up_y),
        remote(10, half.at[2, 0], half.at[0, 0], up_y),
        remote(11, half.at[2, 3], half.at[0, 3], up_y),
        remote(12, quart.at[1], quart.at[0], up_y),
    ]
    y_down = [
        remote(13, half.at[1, mid, :, own], half.at[3, mid, :, own], down_y),
        remote(14, half.at[1, mid, :, far], half.at[3, mid, :, far], down_y),
        remote(15, half.at[1, 0], half.at[3, 0], down_y),
        remote(16, half.at[1, 3], half.at[3, 3], down_y),
        remote(17, quart.at[1], quart.at[2], down_y),
    ]

    def each(copies, which, to_up, to_down, act):
        @pl.when(to_up)
        def _():
            for k in which:
                act(copies[0][k])

        @pl.when(to_down)
        def _():
            for k in which:
                act(copies[1][k])

    has_ux, has_dx, has_uy, has_dy = gx < ngx - 1, gx > 0, gy < ngy - 1, gy > 0
    xs, ys = (x_up, x_down), (y_up, y_down)
    start = lambda c: c.start()
    recv = lambda c: c.wait_recv()
    sent = lambda c: c.wait_send()

    z_half.start()
    z_quart.start()
    each(xs, (0,), has_ux, has_dx, start)
    each(ys, (0,), has_uy, has_dy, start)

    def dup64(x):
        eye = (iota((64, 128), 0) == iota((64, 128), 1) % 64).astype(BF)
        return dot(x, eye)

    def dup32(x):
        eye = (iota((32, 128), 0) == iota((32, 128), 1) % 32).astype(BF)
        return dot(x, eye)

    diag_ir = iota((128, 256), 0) // 32 == iota((128, 256), 1) // 64
    diag_ro = iota((256, 128), 0) // 64 == iota((256, 128), 1) // 32
    diag_io = iota((128, 128), 0) // 32 == iota((128, 128), 1) // 32
    eye64 = (iota((64, 64), 0) == iota((64, 64), 1)).astype(BF)

    b0, b1 = split(jnp.broadcast_to(bias_ref[...], (16, 32)))
    biast[...] = (dup32(b0) + dup32(b1))[0:8]
    w0, w1 = [jnp.where(diag_io, rows_cat(*[dup32(w)] * 4), 0.0).astype(BF) for w in split(skip_ref[...])]
    w0 = lanes_cat(w0, w1)
    skw[...] = rows_cat(w0, w0)

    def spread(l, carry):
        i0, i1 = split(in_ref[l])
        o0, o1 = split(out_ref[l])

        def wide(w):
            t = dup64(w)
            return jnp.where(diag_ir, rows_cat(*[lanes_cat(t, t)] * 4), 0.0).astype(BF)

        def tall(w):
            t = dup32(dot(eye64, w, NT).astype(BF))
            return jnp.where(diag_ro, rows_cat(*[t] * 4), 0.0).astype(BF)

        w0 = wide(i0)
        inw[l] = rows_cat(w0, w0, wide(i1))
        w0 = wide(o0)
        outt[l] = rows_cat(w0, w0, wide(o1))
        w0 = lanes_cat(tall(o0), tall(o1))
        outw[l] = rows_cat(w0, w0)
        dup = []
        for d in range(3):
            m = modes_ref[l, d]
            hi, lo = split(m)
            rest = (m - hi.astype(F32) - lo.astype(F32)).astype(BF)
            dup.append(dup64(hi) + dup64(lo) + dup64(rest))
        m0t[l] = dup[0]
        m1t[l] = dup[1]
        um[l] = (dup[0][:, None, :] * dup[1][None, :, :]).reshape(256, 128)
        line = lanes_cat(*[dup[2]] * 8)
        line = jnp.where(iota((16, 1024), 0) == iota((16, 1024), 1) // 64, line, 0.0)
        m2r[l] = jnp.broadcast_to(jnp.sum(line, axis=0, keepdims=True), (8, 1024))
        return carry

    lax.fori_loop(0, 3, spread, 0)

    hi, lo = split(feat[...])
    fs[0:576] = hi
    fs[576:1152] = lo

    def stacked(ref):
        parts = [slice(128 * n, 128 * (n + 1)) for n in range(6)]
        return rows_cat(*[lanes_cat(ref[0:576, c], ref[576:1152, c]) for c in parts])

    def xy_transform(table, hi_lo, rows, chunks, wide):
        for n in range(chunks):
            cols = slice(wide * n, wide * (n + 1))
            data = rows_cat(hi_lo[0 : 2 * rows, cols], hi_lo[0:rows, cols])
            hi, lo = split(dot(table[...], data))
            th[:, cols] = hi
            tl[:, cols] = lo

    def z_transform(hi, lo, table, depth, into_h, into_l, l, parts=None):
        a = lanes_cat(hi, lo, hi)
        zh, zl = (0, depth) if parts is None else parts
        for n in range(2):
            cols = slice(256 * n, 256 * (n + 1))
            tz = rows_cat(table[zh : zh + depth, cols], table[zh : zh + depth, cols], table[zl : zl + depth, cols])
            vh, vl = split(dot(a, tz))
            into_h[l, :, cols] = vh
            into_l[l, :, cols] = vl

    quads = [(slice(128 * c, 128 * (c + 1)), slice(256 * c, 256 * (c + 1))) for c in range(4)]

    def modes_forward(l):
        data = [(kh[l, :, c], kl[l, :, c]) for c, _ in quads]
        p = dot(rows_cat(*[lanes_cat(a, b, a) for a, b in data]), inw[l])
        u = um[l]
        u = lanes_cat(u, u)
        data = []
        for k, (_, cols) in enumerate(quads):
            pk = p[256 * k : 256 * (k + 1)]
            pr[l, :, cols] = pk
            a, b = split(pk * u * m2r[l, 0:1, cols])
            rh[l, :, cols] = a
            rl[l, :, cols] = b
            data.append(lanes_cat(a, b))
        q = dot(rows_cat(*data), outw[l])
        q = q[:, 0:128] + q[:, 128:256]
        for k, (cols, _) in enumerate(quads):
            a, b = split(q[256 * k : 256 * (k + 1)])
            qh[l, :, cols] = a
            ql[l, :, cols] = b

    v = dot(stacked(fs), skw[...])
    v = v[:, 0:128] + v[:, 128:256] + biast[0:1]
    for n in range(6):
        pre[:, 128 * n : 128 * (n + 1)] = v[576 * n : 576 * (n + 1)]
    loads["xy0"].wait()
    xy_transform(tab["xy0"], fs, 576, 3, 256)

    z_half.wait_recv()
    z_quart.wait_recv()
    each(xs, (1, 2), has_ux, has_dx, start)
    each(ys, (1,), has_uy, has_dy, start)

    loads["z0"].wait()
    z_transform(th[...], tl[...], tab["z0"], 768, kh, kl, 0)
    modes_forward(0)

    each(xs, (0, 1, 2), has_dx, has_ux, recv)
    each(ys, (2, 3, 4), has_uy, has_dy, start)

    loads["z0t"].wait()
    a = lanes_cat(qh[0], ql[0], qh[0])
    for n in range(3):
        cols = slice(256 * n, 256 * (n + 1))
        tz = rows_cat(tab["z0t"][0:512, cols], tab["z0t"][0:512, cols], tab["z0t"][512:1024, cols])
        hi, lo = split(dot(a, tz))
        bs[0:256, cols] = hi
        bs[256:512, cols] = lo
    loads["inv"].wait()
    for n in range(3):
        cols = slice(256 * n, 256 * (n + 1))
        pre[:, cols] = pre[:, cols] + dot(tab["inv"][...], rows_cat(bs[0:512, cols], bs[0:256, cols]))

    each(ys, (0, 1, 2, 3, 4), has_dy, has_uy, recv)
    for j in range(4):
        hi, lo = split(half[j].reshape(160, 640))
        hs[160 * j : 160 * (j + 1)] = hi
        hs[640 + 160 * j : 640 + 160 * (j + 1)] = lo
    cells = rows_cat(quart[...].reshape(360, 512), jnp.zeros((8, 512), F32))
    hi, lo = split(cells)
    qs[0:368] = hi
    qs[368:736] = lo
    loads["xy1"].wait()
    xy_transform(tab["xy1"], hs, 640, 2, 256)
    data = rows_cat(hs[:, 512:640], hs[0:640, 512:640])
    hi, lo = split(dot(tab["xy1"][...], data))
    th[:, 512:640] = hi
    tl[:, 512:640] = lo
    loads["z1"].wait()
    z_transform(th[:, 0:640], tl[:, 0:640], tab["z1"], 640, kh, kl, 1)
    loads["xy2"].wait()
    xy_transform(tab["xy2"], qs, 368, 2, 256)
    loads["z2"].wait()
    z_transform(th[:, 0:512], tl[:, 0:512], tab["z2"], 512, kh, kl, 2)
    lax.fori_loop(1, 3, lambda l, c: (modes_forward(l), c)[1], 0)

    loads["z1c"].wait()
    loads["z2c"].wait()
    for l, name in ((1, "z1c"), (2, "z2c")):
        tz = tab[name]
        v = dot(lanes_cat(qh[l], ql[l], qh[l]), rows_cat(tz[0:512], tz[0:512], tz[512:1024]))
        hi, lo = split(v)
        t12[256 * (l - 1) : 256 * l] = hi
        t12[512 + 256 * (l - 1) : 512 + 256 * l] = lo
    loads["xy12"].wait()
    loads["unpair"].wait()
    s = dot(tab["xy12"][...], rows_cat(t12[...], t12[0:512]))
    for n in range(3):
        hi, lo = split(s[:, 128 * n : 128 * (n + 1)])
        v = dot(lanes_cat(hi, lo), tab["unpair"][...])
        for k in range(2):
            for step in range(2):
                wide[2 * n + k, pl.ds(step, 144, stride=2), :] = v[:, 128 * k : 128 * (k + 1)]

    load_c.wait()
    scale = 1.0 / math.sqrt(ngx * ngy * ngz * NP**3)
    c0 = math.sqrt(2.0 / math.pi)
    store = pltpu.make_async_copy(result, result_hbm, local_sem.at[2])

    def activate(m, carry):
        rows = pl.ds(pl.multiple_of(m * 48, 48), 48)
        v = lanes_cat(*[wide[n, pl.ds(pl.multiple_of(m * 24, 24), 24), :] for n in range(6)])
        x = pre[rows, :] + rows_cat(v, v)
        x2 = x * x
        t = jnp.tanh(c0 * (x * (1.0 + 0.044715 * x2)))
        half_t = 0.5 * (1.0 + t)
        result[rows, :] = x * half_t
        slope = half_t + 0.5 * x * (1.0 - t * t) * (c0 * (1.0 + (3 * 0.044715) * x2))
        g = cot[rows, :] * scale * slope
        hi, lo = split(g)
        gs[rows, :] = hi
        gs[pl.ds(pl.multiple_of(576 + m * 48, 48), 48), :] = lo
        g2 = g[0:24] + g[24:48]
        for n in range(6):
            down[n, pl.ds(pl.multiple_of(m * 24, 24), 24), :] = g2[:, 128 * n : 128 * (n + 1)]
        return carry + jnp.sum(g.reshape(6, 8, 768), axis=0)

    colsum = lax.fori_loop(0, 12, activate, jnp.zeros((8, 768), F32))
    store.start()
    gbias[...] = fold_lanes(colsum)

    xy_transform(tab["xy0"], gs, 576, 3, 256)
    z_transform(th[...], tl[...], tab["z0"], 768, gqh, gql, 0)
    for n in range(3):
        v = [down[2 * n + k, pl.ds(0, 144, stride=2), :] + down[2 * n + k, pl.ds(1, 144, stride=2), :] for k in range(2)]
        hi, lo = split(lanes_cat(*v))
        hi, lo = split(dot(lanes_cat(hi, lo), tab["pair"][...]))
        ghh[:, 128 * n : 128 * (n + 1)] = hi
        ghl[:, 128 * n : 128 * (n + 1)] = lo
    loads["xy12t"].wait()
    hi, lo = split(dot(tab["xy12t"][...], rows_cat(ghh[...], ghl[...], ghh[...])))
    g12h[...] = hi
    g12l[...] = lo
    loads["z2ct"].wait()
    z_transform(g12h[0:256], g12l[0:256], tab["z1"], 384, gqh, gql, 1, (0, 640))
    z_transform(g12h[256:512], g12l[256:512], tab["z2ct"], 384, gqh, gql, 2)

    total = dot(stacked(fs), stacked(gs), TN)
    total = total[0:128] + total[128:256]
    total = jnp.where(diag_io, total[:, 0:128] + total[:, 128:256], 0.0)
    s = total[0:32] + total[32:64] + total[64:96] + total[96:128]
    s = s + pltpu.roll(s, 64, 1)
    gskip[...] = s + pltpu.roll(s, 32, 1)

    def gram(ah, al, bh, bl):
        a, b = [], []
        for ca, cb in quads:
            x, y = ah[:, ca], al[:, ca]
            v, w = bh[:, cb], bl[:, cb]
            a += [x, y, x]
            b += [v, v, w]
        g = jnp.where(diag_ir, dot(rows_cat(*a), rows_cat(*b), TN), 0.0)
        return fold_lanes(g[0:32] + g[32:64] + g[64:96] + g[96:128])

    low = iota((32, 128), 1) < 64

    def modes_backward(l, carry):
        u = um[l]
        u = lanes_cat(u, u)
        e = jnp.zeros((256, 128), F32)
        g2 = []
        g_out = gram(gqh.at[l], gql.at[l], rh.at[l], rl.at[l])
        data = [(gqh[l, :, c], gql[l, :, c]) for c, _ in quads]
        g = dot(rows_cat(*[lanes_cat(a, b, a) for a, b in data]), outt[l])
        for k, (_, cols) in enumerate(quads):
            gr = g[256 * k : 256 * (k + 1)]
            d = gr * pr[l, :, cols]
            m2 = m2r[l, 0:1, cols]
            dm = d * m2
            e = e + dm[:, 0:128] + dm[:, 128:256]
            g2.append(jnp.sum((d * u).reshape(32, 8, 256), axis=0))
            hi, lo = split(gr * (u * m2))
            rh[l, :, cols] = hi
            rl[l, :, cols] = lo
        g_in = gram(kh.at[l], kl.at[l], rh.at[l], rl.at[l])
        e = (e + pltpu.roll(e, 64, 1)).reshape(16, 16, 128)
        g0 = jnp.sum(e * m1t[l][None, :, :], axis=1)
        g1 = jnp.sum(e * m0t[l][:, None, :], axis=0)
        g2 = jnp.sum(lanes_cat(*g2), axis=0, keepdims=True)
        g2 = jnp.where(iota((16, 1024), 0) == iota((16, 1024), 1) // 64, g2, 0.0)
        g2 = fold_lanes(g2)
        row = pl.multiple_of(l * 64, 64)
        pay[pl.ds(row, 32), :] = jnp.where(low, g_in, g_out)
        pay[pl.ds(row + 32, 16), :] = jnp.where(low[0:16], g0, g1)
        pay[pl.ds(row + 48, 16), :] = jnp.where(low[0:16], g2, 0.0)
        return carry

    lax.fori_loop(0, 3, modes_backward, 0)
    s = gskip[...]
    s = jnp.where(iota((16, 128), 1) < 96, s[0:16], s[16:32])
    pay[48:64] = jnp.where(low[0:16], pay[48:64], s)
    b = gbias[...] + pltpu.roll(gbias[...], 32, 1)
    b = jnp.broadcast_to(jnp.sum(b, axis=0, keepdims=True), (16, 128))
    pay[112:128] = jnp.where(low[0:16], pay[112:128], b)

    size = PAY // ngy

    def pushes(count, make, act):
        def body(k, carry):
            act(make(k))
            return carry

        lax.fori_loop(1, count, body, 0)

    def scatter(k):
        t = lax.rem(gy + k, ngy)
        return pltpu.make_async_remote_copy(
            src_ref=pay.at[pl.ds(pl.multiple_of(t * size, 8), size)],
            dst_ref=ra.at[k],
            send_sem=red_send.at[k],
            recv_sem=red_recv.at[k],
            device_id=(gx, t, gz),
            device_id_type=MESH,
        )

    def exchange(k):
        q = lax.rem(me + k, group)
        return pltpu.make_async_remote_copy(
            src_ref=acc,
            dst_ref=rb.at[me],
            send_sem=red_send.at[ngy + k],
            recv_sem=red_recv.at[ngy + k],
            device_id=(q // ngz, gy, lax.rem(q, ngz)),
            device_id_type=MESH,
        )

    mine = pl.ds(pl.multiple_of(gy * size, 8), size)

    def gather(k):
        t = lax.rem(gy + k, ngy)
        return pltpu.make_async_remote_copy(
            src_ref=red.at[mine],
            dst_ref=red.at[mine],
            send_sem=red_send.at[ngy + group + k],
            recv_sem=red_recv.at[ngy + group + k],
            device_id=(gx, t, gz),
            device_id_type=MESH,
        )

    pushes(ngy, scatter, start)
    pushes(ngy, scatter, recv)
    total = pay[mine]
    for k in range(1, ngy):
        total = total + ra[k]
    acc[...] = total
    rb[me] = total
    pushes(group, exchange, start)
    pushes(group, exchange, recv)
    total = rb[0]
    for k in range(1, group):
        total = total + rb[k]
    red[mine] = total
    pushes(ngy, gather, start)
    pushes(ngy, gather, recv)
    red_ref[...] = red[...]

    pushes(ngy, scatter, sent)
    pushes(group, exchange, sent)
    pushes(ngy, gather, sent)
    z_half.wait_send()
    z_quart.wait_send()
    each(xs, (0, 1, 2), has_ux, has_dx, sent)
    each(ys, (0, 1, 2, 3, 4), has_uy, has_dy, sent)
    store.wait()


def unpack_kernel(result_in, red, result_out, skip, bias, modes, fin, fout, held, sem):
    parts = [pl.ds(144 * k, 144) for k in range(4)]
    fetch = [pltpu.make_async_copy(result_in.at[p], held.at[p], sem.at[k]) for k, p in enumerate(parts)]
    store = [pltpu.make_async_copy(held.at[p], result_out.at[p], sem.at[4 + k]) for k, p in enumerate(parts)]
    for copy in fetch:
        copy.start()
    skip[0:16] = red[48:64, 64:96]
    skip[16:32] = red[48:64, 96:128]
    bias[...] = red[112:113, 64:96]
    for l in range(3):
        row = 64 * l
        fin[l] = red[row : row + 32, 0:64]
        fout[l] = red[row : row + 32, 64:128]
        modes[l, 0] = red[row + 32 : row + 48, 0:64]
        modes[l, 1] = red[row + 32 : row + 48, 64:128]
        modes[l, 2] = red[row + 48 : row + 64, 0:64]
    for a, b in zip(fetch, store):
        a.wait()
        b.start()
    for copy in store:
        copy.wait()


def solution(mesh):
    sizes = tuple(mesh.shape[name] for name in ("gx", "gy", "gz"))
    ngx, ngy, ngz = sizes
    group = ngx * ngz
    size = PAY // ngy
    any_spec = pl.BlockSpec(memory_space=pl.ANY)
    vmem_spec = pl.BlockSpec(memory_space=pltpu.VMEM)
    scratch = [pltpu.VMEM(table_shape(n), BF) for n in NAMES] + [
        pltpu.VMEM((576, 768), F32),
        pltpu.VMEM((576, 768), F32),
        pltpu.VMEM((576, 768), F32),
        pltpu.VMEM((1152, 768), BF),
        pltpu.VMEM((4, 4, 40, 640), F32),
        pltpu.VMEM((3, 3, 40, 512), F32),
        pltpu.VMEM((1280, 640), BF),
        pltpu.VMEM((736, 512), BF),
        pltpu.VMEM((3, 256, 512), BF),
        pltpu.VMEM((3, 256, 512), BF),
        pltpu.VMEM((3, 256, 1024), F32),
        pltpu.VMEM((3, 256, 1024), BF),
        pltpu.VMEM((3, 256, 1024), BF),
        pltpu.VMEM((3, 256, 512), BF),
        pltpu.VMEM((3, 256, 512), BF),
        pltpu.VMEM((256, 768), BF),
        pltpu.VMEM((256, 768), BF),
        pltpu.VMEM((512, 768), BF),
        pltpu.VMEM((1024, 384), BF),
        pltpu.VMEM((576, 768), F32),
        pltpu.VMEM((1152, 768), BF),
        pltpu.VMEM((3, 256, 512), BF),
        pltpu.VMEM((3, 256, 512), BF),
        pltpu.VMEM((144, 384), BF),
        pltpu.VMEM((144, 384), BF),
        pltpu.VMEM((6, 288, 128), F32),
        pltpu.VMEM((6, 288, 128), F32),
        pltpu.VMEM((512, 384), BF),
        pltpu.VMEM((512, 384), BF),
        pltpu.VMEM((3, 256, 128), F32),
        pltpu.VMEM((3, 8, 1024), F32),
        pltpu.VMEM((3, 16, 128), F32),
        pltpu.VMEM((3, 16, 128), F32),
        pltpu.VMEM((3, 384, 256), BF),
        pltpu.VMEM((3, 512, 256), BF),
        pltpu.VMEM((3, 384, 256), BF),
        pltpu.VMEM((256, 256), BF),
        pltpu.VMEM((8, 128), F32),
        pltpu.VMEM((32, 128), F32),
        pltpu.VMEM((8, 128), F32),
        pltpu.VMEM((PAY, 128), F32),
        pltpu.VMEM((ngy, size, 128), F32),
        pltpu.VMEM((group, size, 128), F32),
        pltpu.VMEM((size, 128), F32),
        pltpu.VMEM((PAY, 128), F32),
        pltpu.SemaphoreType.DMA((len(NAMES),)),
        pltpu.SemaphoreType.DMA((3,)),
        pltpu.SemaphoreType.DMA((18,)),
        pltpu.SemaphoreType.DMA((18,)),
        pltpu.SemaphoreType.DMA((2 * ngy + group,)),
        pltpu.SemaphoreType.DMA((2 * ngy + group,)),
    ]

    def per_device(features, cotangent, skip_weight, bias_vector, mode_factors, in_factors, out_factors):
        tables = [jnp.asarray(TABLES[n]) for n in NAMES]
        result, red = pl.pallas_call(
            lambda *refs: layer_kernel(sizes, *refs),
            name="layer",
            out_shape=(jax.ShapeDtypeStruct((576, 768), F32), jax.ShapeDtypeStruct((PAY, 128), F32)),
            in_specs=[any_spec] * 2 + [vmem_spec] * 5 + [any_spec] * len(NAMES),
            out_specs=(any_spec, vmem_spec),
            scratch_shapes=scratch,
            compiler_params=pltpu.CompilerParams(
                collective_id=0, has_side_effects=True, vmem_limit_bytes=60 * 1024 * 1024
            ),
            cost_estimate=pl.CostEstimate(flops=32 * 10**9, bytes_accessed=20 * 10**6, transcendentals=442368),
        )(
            features.reshape(576, 768),
            cotangent.reshape(576, 768),
            skip_weight,
            bias_vector.reshape(1, CH),
            mode_factors,
            in_factors,
            jnp.swapaxes(out_factors, 1, 2),
            *tables,
        )
        outs = pl.pallas_call(
            unpack_kernel,
            name="unpack",
            out_shape=(
                jax.ShapeDtypeStruct((576, 768), F32),
                jax.ShapeDtypeStruct((CH, CH), F32),
                jax.ShapeDtypeStruct((1, CH), F32),
                jax.ShapeDtypeStruct((3, 3, MD, RK), F32),
                jax.ShapeDtypeStruct((3, CH, RK), F32),
                jax.ShapeDtypeStruct((3, CH, RK), F32),
            ),
            in_specs=[any_spec, vmem_spec],
            out_specs=(any_spec,) + (vmem_spec,) * 5,
            scratch_shapes=[pltpu.VMEM((576, 768), F32), pltpu.SemaphoreType.DMA((8,))],
        )(result, red)
        return (outs[0].reshape(NP, NP, NP * CH), outs[1], outs[2].reshape(CH), outs[3], outs[4], jnp.swapaxes(outs[5], 1, 2))

    placed = (P("gx", "gy", "gz"), P("gx", "gy", "gz"), P(), P(), P(), P(), P())
    return jax.shard_map(
        per_device,
        mesh=mesh,
        in_specs=placed,
        out_specs=(P("gx", "gy", "gz"), P(), P(), P(), P(), P()),
        check_vma=False,
    )
```

```python
import math

import jax
import jax.numpy as jnp
import ml_dtypes
import numpy as np
from jax import lax
from jax.experimental import pallas as pl
from jax.experimental.pallas import tpu as pltpu
from jax.sharding import PartitionSpec as P

MESH = pl.DeviceIdType.MESH
BF = jnp.bfloat16
F32 = jnp.float32
CH, RK, MD, NP = 32, 64, 16, 24
NN = (((1,), (0,)), ((), ()))
NT = (((1,), (1,)), ((), ()))
TN = (((0,), (0,)), ((), ()))
PAY = 192


def basis(length):
    rows = np.arange(MD)
    freq = np.where(rows < MD // 2, rows, rows - MD // 2 + 1).astype(np.float64)
    phase = 2.0 * math.pi / length * freq[:, None] * np.arange(length)[None, :]
    wave = np.where((rows < MD // 2)[:, None], np.cos(phase), np.sin(phase))
    return wave * math.sqrt(2.0 / length)


def halves(x):
    x = np.asarray(x, np.float32)
    hi = x.astype(ml_dtypes.bfloat16)
    lo = (x - hi.astype(np.float32)).astype(ml_dtypes.bfloat16)
    return hi, lo


def left(x):
    hi, lo = halves(x)
    return np.concatenate([hi, hi, lo], axis=1)


def right(x):
    hi, lo = halves(x)
    return np.concatenate([hi, lo], axis=0)


def exact(x, times, axis):
    x = np.asarray(x, np.float32).astype(ml_dtypes.bfloat16)
    return np.concatenate([x] * times, axis=axis)


def channel_eye(b):
    return np.kron(b, np.eye(CH))


def make_tables():
    b24, b18 = basis(24), basis(18)
    pool = np.zeros((208, 12, 24))
    for j in range(2):
        for i in range(2):
            for r in range(36):
                x, y = i * 6 + r // 6, 2 * (j * 6 + r % 6)
                pool[(j * 2 + i) * 40 + r, x, y : y + 2] = 1 / 8
    for r in range(36):
        x, y = 2 * (r // 6), 4 * (r % 6)
        pool[160 + r, x : x + 2, y : y + 4] = 1 / 64
    pool = pool.reshape(208, 288)
    pair = channel_eye(np.kron(np.eye(4), np.ones((2, 1))))
    quad = np.zeros((24, 8))
    for z in range(24):
        quad[z, z // 4] = 1
    quad = channel_eye(quad)
    xy0 = np.kron(b24, b24)
    xy1 = np.zeros((256, 4, 4, 40))
    for j in range(4):
        for i in range(4):
            for r in range(36):
                xy1[:, j, i, r] = np.kron(b24[:, i * 6 + r // 6], b24[:, j * 6 + r % 6])
    xy2 = np.zeros((256, 368))
    for j in range(3):
        for i in range(3):
            for r in range(36):
                xy2[:, (j * 3 + i) * 40 + r] = np.kron(
                    b18[:, i * 6 + r // 6], b18[:, j * 6 + r % 6]
                )
    z0 = channel_eye(b24.T)
    z1s, z2s = [], []
    for gz in range(2):
        z1 = np.zeros((20, 16))
        z1[0:12] = b24[:, 6:18].T
        if gz == 0:
            z1[12:18] = b24[:, 18:24].T
        else:
            z1[14:20] = b24[:, 0:6].T
        z1s.append(right(channel_eye(z1)))
        z2 = np.zeros((16, 16))
        z2[0:6] = b18[:, 6:12].T
        z2[8:14] = b18[:, 12:18].T if gz == 0 else b18[:, 0:6].T
        z2s.append(right(channel_eye(z2)))
    z1c = channel_eye(b24[:, 6:18])
    z2c = channel_eye(np.repeat(b18[:, 6:12], 2, axis=1))
    c1 = b24[:, 6:18]
    c2 = np.repeat(b18[:, 6:12], 2, axis=1)
    xy12 = np.concatenate([np.kron(c1, c1), np.kron(c2, c2)], axis=0)
    return {
        "pool": exact(pool, 2, 1),
        "pair": exact(pair, 2, 0),
        "quad": exact(quad, 2, 0),
        "unpair": exact(pair.T, 2, 0),
        "xy0": left(xy0),
        "z0": right(z0),
        "z0t": right(z0.T),
        "inv": left(xy0.T),
        "xy1": left(xy1.reshape(256, 640)),
        "z1": np.concatenate(z1s, axis=0),
        "xy2": left(xy2),
        "z2": np.concatenate(z2s, axis=0),
        "z1c": right(z1c),
        "z2c": right(z2c),
        "xy12": left(xy12.T),
        "xy12t": left(xy12),
        "z2ct": right(z2c.T),
    }


TABLES = make_tables()
NAMES = list(TABLES)


FED = ("hs", "qs", "pre", "fs", "kh0", "kl0", "pr0", "rh0", "rl0")
SHAPES = {
    "feat": ((576, 768), F32),
    "cot": ((576, 768), F32),
    "result": ((576, 768), F32),
    "fs": ((1152, 768), BF),
    "half": ((4, 4, 40, 640), F32),
    "quart": ((3, 3, 40, 512), F32),
    "hs": ((1280, 640), BF),
    "qs": ((736, 512), BF),
    "kh": ((3, 256, 512), BF),
    "kl": ((3, 256, 512), BF),
    "pr": ((3, 256, 1024), F32),
    "rh": ((3, 256, 1024), BF),
    "rl": ((3, 256, 1024), BF),
    "qh": ((3, 256, 512), BF),
    "ql": ((3, 256, 512), BF),
    "th": ((256, 768), BF),
    "tl": ((256, 768), BF),
    "bs": ((512, 768), BF),
    "t12": ((1024, 384), BF),
    "pre": ((576, 768), F32),
    "gs": ((1152, 768), BF),
    "gqh": ((3, 256, 512), BF),
    "gql": ((3, 256, 512), BF),
    "ghh": ((144, 384), BF),
    "ghl": ((144, 384), BF),
    "wide": ((6, 288, 128), F32),
    "down": ((6, 288, 128), F32),
    "g12h": ((512, 384), BF),
    "g12l": ((512, 384), BF),
    "um": ((3, 256, 128), F32),
    "m2r": ((3, 8, 1024), F32),
    "m0t": ((3, 16, 128), F32),
    "m1t": ((3, 16, 128), F32),
    "inw": ((3, 384, 256), BF),
    "outw": ((3, 512, 256), BF),
    "outt": ((3, 384, 256), BF),
    "skw": ((256, 256), BF),
    "biast": ((8, 128), F32),
    "gskip": ((32, 128), F32),
    "gbias": ((8, 128), F32),
    "pay": ((PAY, 128), F32),
    "red": ((PAY, 128), F32),
    "pooled": ((576, 768), BF),
    "strips": ((208, 768), F32),
    "result_hbm": ((576, 768), F32),
    "red_ref": ((PAY, 128), F32),
}
WEIGHTS = ("skip_ref", "bias_ref", "modes_ref", "in_ref", "out_ref")
SPREAD = ("um", "m2r", "m0t", "m1t", "inw", "outw", "outt")
KERNELS = {
    "A": {
        "ins": ("feat_hbm",) + WEIGHTS,
        "tables": ("pool", "pair", "quad", "xy0", "z0", "z0t", "inv"),
        "outs": tuple(n.rstrip("0") for n in FED),
        "scratch": ("feat", "pooled", "strips", "half", "quart", "qh", "ql", "th", "tl", "bs", "skw", "biast") + SPREAD,
    },
    "B": {
        "ins": ("cot_hbm",) + WEIGHTS + tuple(n + "_hbm" for n in FED),
        "tables": ("xy1", "z1", "xy2", "z2", "z1c", "z2c", "xy12", "unpair", "xy0", "z0", "pair", "xy12t", "z2ct"),
        "outs": ("result_hbm", "pay"),
        "scratch": ("cot", "result", "hs", "qs", "pre", "fs", "kh", "kl", "pr", "rh", "rl", "qh", "ql", "th", "tl", "t12", "gs")
        + ("gqh", "gql", "ghh", "ghl", "wide", "down", "g12h", "g12l", "gskip", "gbias")
        + SPREAD,
    },
    "C": {"ins": ("pay",), "tables": (), "outs": ("red_ref",), "scratch": ("ra", "rb", "acc", "red")},
}


def table_shape(name):
    rows, cols = TABLES[name].shape
    return (rows // 2 if name in ("z1", "z2") else rows), cols


def dot(a, b, dims=NN):
    return lax.dot_general(a, b, dims, preferred_element_type=F32)


def split(x):
    hi = x.astype(BF)
    return hi, (x - hi.astype(F32)).astype(BF)


def rows_cat(*parts):
    return jnp.concatenate(parts, axis=0)


def lanes_cat(*parts):
    return jnp.concatenate(parts, axis=1)


def iota(shape, dim):
    return lax.broadcasted_iota(jnp.int32, shape, dim)


def fold_lanes(x):
    total = x[:, 0:128]
    for k in range(1, x.shape[1] // 128):
        total = total + x[:, 128 * k : 128 * (k + 1)]
    return total + pltpu.roll(total, 64, 1)


def layer_kernel(sizes, parts, *refs):
    ngx, ngy, ngz = sizes
    names = KERNELS[parts]
    refs = list(refs)
    take = lambda which: dict(zip(which, [refs.pop(0) for _ in which]))
    used = names["tables"]
    R = take(names["ins"])
    hbm = take(used)
    R.update(take(names["outs"]))
    tab = take(used)
    R.update(take(names["scratch"]))
    table_sem, local_sem, halo_send, halo_recv, red_send, red_recv = refs

    gx, gy, gz = lax.axis_index("gx"), lax.axis_index("gy"), lax.axis_index("gz")
    me = gx * ngz + gz
    group = ngx * ngz

    loads = {}
    for k, name in enumerate(used):
        rows = table_shape(name)[0]
        src = hbm[name].at[pl.ds(pl.multiple_of(gz * rows, 16), rows)] if name in ("z1", "z2") else hbm[name]
        loads[name] = pltpu.make_async_copy(src, tab[name], table_sem.at[k])
    local = lambda k, src, dst: pltpu.make_async_copy(src, dst, local_sem.at[k])
    start = lambda c: c.start()
    recv = lambda c: c.wait_recv()
    sent = lambda c: c.wait_send()

    feat, fs, kh, kl, pr, rh, rl, qh = (R.get(n) for n in ("feat", "fs", "kh", "kl", "pr", "rh", "rl", "qh"))
    ql, th, tl, wide, um, m2r, m0t, m1t = (R.get(n) for n in ("ql", "th", "tl", "wide", "um", "m2r", "m0t", "m1t"))
    inw, outw, outt, skw, biast, skip_ref, bias_ref, modes_ref = (R.get(n) for n in ("inw", "outw", "outt", "skw", "biast", "skip_ref", "bias_ref", "modes_ref"))
    in_ref, out_ref = (R.get(n) for n in ("in_ref", "out_ref"))
    barrier = pltpu.get_barrier_semaphore() if parts != "B" else None

    def greet():
        def greet_row(k, carry):
            pl.semaphore_signal(
                barrier, inc=1, device_id=(gx, lax.rem(gy + k, ngy), gz), device_id_type=MESH
            )
            return carry

        lax.fori_loop(1, ngy, greet_row, 0)

        def greet_plane(k, carry):
            q = lax.rem(me + k, group)
            pl.semaphore_signal(
                barrier, inc=1, device_id=(q // ngz, gy, lax.rem(q, ngz)), device_id_type=MESH
            )
            return carry

        lax.fori_loop(1, group, greet_plane, 0)

    def dup64(x):
        eye = (iota((64, 128), 0) == iota((64, 128), 1) % 64).astype(BF)
        return dot(x, eye)

    def dup32(x):
        eye = (iota((32, 128), 0) == iota((32, 128), 1) % 32).astype(BF)
        return dot(x, eye)

    diag_ir = iota((128, 256), 0) // 32 == iota((128, 256), 1) // 64
    diag_ro = iota((256, 128), 0) // 64 == iota((256, 128), 1) // 32
    diag_io = iota((128, 128), 0) // 32 == iota((128, 128), 1) // 32
    eye64 = (iota((64, 64), 0) == iota((64, 64), 1)).astype(BF)

    def skip_weights():
        b0, b1 = split(jnp.broadcast_to(bias_ref[...], (16, 32)))
        biast[...] = (dup32(b0) + dup32(b1))[0:8]
        w0, w1 = [jnp.where(diag_io, rows_cat(*[dup32(w)] * 4), 0.0).astype(BF) for w in split(skip_ref[...])]
        w0 = lanes_cat(w0, w1)
        skw[...] = rows_cat(w0, w0)

    def spread_weights():
        def spread(l, carry):
            i0, i1 = split(in_ref[l])
            o0, o1 = split(out_ref[l])

            def wide(w):
                t = dup64(w)
                return jnp.where(diag_ir, rows_cat(*[lanes_cat(t, t)] * 4), 0.0).astype(BF)

            def tall(w):
                t = dup32(dot(eye64, w, NT).astype(BF))
                return jnp.where(diag_ro, rows_cat(*[t] * 4), 0.0).astype(BF)

            w0 = wide(i0)
            inw[l] = rows_cat(w0, w0, wide(i1))
            w0 = wide(o0)
            outt[l] = rows_cat(w0, w0, wide(o1))
            w0 = lanes_cat(tall(o0), tall(o1))
            outw[l] = rows_cat(w0, w0)
            dup = []
            for d in range(3):
                m = modes_ref[l, d]
                hi, lo = split(m)
                rest = (m - hi.astype(F32) - lo.astype(F32)).astype(BF)
                dup.append(dup64(hi) + dup64(lo) + dup64(rest))
            m0t[l] = dup[0]
            m1t[l] = dup[1]
            um[l] = (dup[0][:, None, :] * dup[1][None, :, :]).reshape(256, 128)
            line = lanes_cat(*[dup[2]] * 8)
            line = jnp.where(iota((16, 1024), 0) == iota((16, 1024), 1) // 64, line, 0.0)
            m2r[l] = jnp.broadcast_to(jnp.sum(line, axis=0, keepdims=True), (8, 1024))
            return carry

        lax.fori_loop(0, 3, spread, 0)

    def stacked(ref):
        parts = [slice(128 * n, 128 * (n + 1)) for n in range(6)]
        return rows_cat(*[lanes_cat(ref[0:576, c], ref[576:1152, c]) for c in parts])

    def xy_transform(table, hi_lo, rows, chunks, wide):
        for n in range(chunks):
            cols = slice(wide * n, wide * (n + 1))
            data = rows_cat(hi_lo[0 : 2 * rows, cols], hi_lo[0:rows, cols])
            hi, lo = split(dot(table[...], data))
            th[:, cols] = hi
            tl[:, cols] = lo

    def z_transform(hi, lo, table, depth, into_h, into_l, l, parts=None):
        a = lanes_cat(hi, lo, hi)
        zh, zl = (0, depth) if parts is None else parts
        for n in range(2):
            cols = slice(256 * n, 256 * (n + 1))
            tz = rows_cat(table[zh : zh + depth, cols], table[zh : zh + depth, cols], table[zl : zl + depth, cols])
            vh, vl = split(dot(a, tz))
            into_h[l, :, cols] = vh
            into_l[l, :, cols] = vl

    quads = [(slice(128 * c, 128 * (c + 1)), slice(256 * c, 256 * (c + 1))) for c in range(4)]

    def modes_forward(l):
        data = [(kh[l, :, c], kl[l, :, c]) for c, _ in quads]
        p = dot(rows_cat(*[lanes_cat(a, b, a) for a, b in data]), inw[l])
        u = um[l]
        u = lanes_cat(u, u)
        data = []
        for k, (_, cols) in enumerate(quads):
            pk = p[256 * k : 256 * (k + 1)]
            pr[l, :, cols] = pk
            a, b = split(pk * u * m2r[l, 0:1, cols])
            rh[l, :, cols] = a
            rl[l, :, cols] = b
            data.append(lanes_cat(a, b))
        q = dot(rows_cat(*data), outw[l])
        q = q[:, 0:128] + q[:, 128:256]
        for k, (cols, _) in enumerate(quads):
            a, b = split(q[256 * k : 256 * (k + 1)])
            qh[l, :, cols] = a
            ql[l, :, cols] = b

    def fine_part():
        feat, fs, half, quart, hs, qs, kh, kl = (R.get(n) for n in ("feat", "fs", "half", "quart", "hs", "qs", "kh", "kl"))
        qh, ql, th, tl, bs, pre, skw, biast = (R.get(n) for n in ("qh", "ql", "th", "tl", "bs", "pre", "skw", "biast"))
        pooled, strips = (R.get(n) for n in ("pooled", "strips"))
        load_f = local(0, R["feat_hbm"], feat)
        load_f.start()
        for name in used[:3]:
            loads[name].start()
        greet()
        @pl.when(gx == 0)
        def _():
            for j in (1, 2):
                half[j, 0] = jnp.zeros((40, 640), F32)
            quart[1, 0] = jnp.zeros((40, 512), F32)

        @pl.when(gx == ngx - 1)
        def _():
            for j in (1, 2):
                half[j, 3] = jnp.zeros((40, 640), F32)
            quart[1, 2] = jnp.zeros((40, 512), F32)

        @pl.when(gy == 0)
        def _():
            for i in range(4):
                half[0, i] = jnp.zeros((40, 640), F32)
            for i in range(3):
                quart[0, i] = jnp.zeros((40, 512), F32)

        @pl.when(gy == ngy - 1)
        def _():
            for i in range(4):
                half[3, i] = jnp.zeros((40, 640), F32)
            for i in range(3):
                quart[2, i] = jnp.zeros((40, 512), F32)

        load_f.wait()
        for name in used[3:]:
            loads[name].start()
        cells = feat[...].reshape(12, 2, 24, 768)
        hi, lo = split((cells[:, 0] + cells[:, 1]).reshape(288, 768))
        pooled[0:288] = hi
        pooled[288:576] = lo
        loads["pool"].wait()
        for n in range(3):
            strips[:, 256 * n : 256 * (n + 1)] = dot(tab["pool"][...], pooled[:, 256 * n : 256 * (n + 1)])
        hi, lo = split(strips[...])
        loads["pair"].wait()
        for n in range(3):
            cols = slice(256 * n, 256 * (n + 1))
            cells = dot(lanes_cat(hi[0:160, cols], lo[0:160, cols]), tab["pair"][...])
            for j in range(2):
                for i in range(2):
                    r = (j * 2 + i) * 40
                    half[j + 1, i + 1, :, 128 * n : 128 * (n + 1)] = cells[r : r + 40]
        loads["quad"].wait()
        cells = dot(lanes_cat(hi[160:208], lo[160:208]), tab["quad"][...])
        quart[1, 1, :, 0:256] = cells[0:40]

        pl.semaphore_wait(barrier, ngy - 1 + group - 1)

        def remote(k, src, dst, to):
            return pltpu.make_async_remote_copy(
                src_ref=src,
                dst_ref=dst,
                send_sem=halo_send.at[k],
                recv_sem=halo_recv.at[k],
                device_id=to,
                device_id_type=MESH,
            )

        first = pl.multiple_of(128 * (1 - gz), 128)
        own, far = pl.ds(0, 384), pl.ds(384, 256)
        up_x, down_x = (gx + 1, gy, gz), (gx - 1, gy, gz)
        up_y, down_y = (gx, gy + 1, gz), (gx, gy - 1, gz)
        across = (gx, gy, 1 - gz)
        mid = pl.ds(1, 2)
        z_half = remote(0, half.at[mid, mid, :, pl.ds(first, 256)], half.at[mid, mid, :, far], across)
        z_quart = remote(1, quart.at[1, 1, :, pl.ds(0, 256)], quart.at[1, 1, :, pl.ds(256, 256)], across)
        x_up = [
            remote(2, half.at[mid, 2, :, own], half.at[mid, 0, :, own], up_x),
            remote(3, half.at[mid, 2, :, far], half.at[mid, 0, :, far], up_x),
            remote(4, quart.at[1, 1], quart.at[1, 0], up_x),
        ]
        x_down = [
            remote(5, half.at[mid, 1, :, own], half.at[mid, 3, :, own], down_x),
            remote(6, half.at[mid, 1, :, far], half.at[mid, 3, :, far], down_x),
            remote(7, quart.at[1, 1], quart.at[1, 2], down_x),
        ]
        y_up = [
            remote(8, half.at[2, mid, :, own], half.at[0, mid, :, own], up_y),
            remote(9, half.at[2, mid, :, far], half.at[0, mid, :, far], up_y),
            remote(10, half.at[2, 0], half.at[0, 0], up_y),
            remote(11, half.at[2, 3], half.at[0, 3], up_y),
            remote(12, quart.at[1], quart.at[0], up_y),
        ]
        y_down = [
            remote(13, half.at[1, mid, :, own], half.at[3, mid, :, own], down_y),
            remote(14, half.at[1, mid, :, far], half.at[3, mid, :, far], down_y),
            remote(15, half.at[1, 0], half.at[3, 0], down_y),
            remote(16, half.at[1, 3], half.at[3, 3], down_y),
            remote(17, quart.at[1], quart.at[2], down_y),
        ]

        def each(copies, which, to_up, to_down, act):
            @pl.when(to_up)
            def _():
                for k in which:
                    act(copies[0][k])

            @pl.when(to_down)
            def _():
                for k in which:
                    act(copies[1][k])

        has_ux, has_dx, has_uy, has_dy = gx < ngx - 1, gx > 0, gy < ngy - 1, gy > 0
        xs, ys = (x_up, x_down), (y_up, y_down)

        z_half.start()
        z_quart.start()
        each(xs, (0,), has_ux, has_dx, start)
        each(ys, (0,), has_uy, has_dy, start)

        skip_weights()
        spread_weights()
        hi, lo = split(feat[...])
        fs[0:576] = hi
        fs[576:1152] = lo

        v = dot(stacked(fs), skw[...])
        v = v[:, 0:128] + v[:, 128:256] + biast[0:1]
        for n in range(6):
            pre[:, 128 * n : 128 * (n + 1)] = v[576 * n : 576 * (n + 1)]
        loads["xy0"].wait()
        xy_transform(tab["xy0"], fs, 576, 3, 256)

        z_half.wait_recv()
        z_quart.wait_recv()
        each(xs, (1, 2), has_ux, has_dx, start)
        each(ys, (1,), has_uy, has_dy, start)

        loads["z0"].wait()
        z_transform(th[...], tl[...], tab["z0"], 768, kh, kl, 0)
        modes_forward(0)

        each(xs, (0, 1, 2), has_dx, has_ux, recv)
        each(ys, (2, 3, 4), has_uy, has_dy, start)

        loads["z0t"].wait()
        a = lanes_cat(qh[0], ql[0], qh[0])
        for n in range(3):
            cols = slice(256 * n, 256 * (n + 1))
            tz = rows_cat(tab["z0t"][0:512, cols], tab["z0t"][0:512, cols], tab["z0t"][512:1024, cols])
            hi, lo = split(dot(a, tz))
            bs[0:256, cols] = hi
            bs[256:512, cols] = lo
        loads["inv"].wait()
        for n in range(3):
            cols = slice(256 * n, 256 * (n + 1))
            pre[:, cols] = pre[:, cols] + dot(tab["inv"][...], rows_cat(bs[0:512, cols], bs[0:256, cols]))

        each(ys, (0, 1, 2, 3, 4), has_dy, has_uy, recv)
        for j in range(4):
            hi, lo = split(half[j].reshape(160, 640))
            hs[160 * j : 160 * (j + 1)] = hi
            hs[640 + 160 * j : 640 + 160 * (j + 1)] = lo
        cells = rows_cat(quart[...].reshape(360, 512), jnp.zeros((8, 512), F32))
        hi, lo = split(cells)
        qs[0:368] = hi
        qs[368:736] = lo
        z_half.wait_send()
        z_quart.wait_send()
        each(xs, (0, 1, 2), has_ux, has_dx, sent)
        each(ys, (0, 1, 2, 3, 4), has_uy, has_dy, sent)

    def coarse_part():
        cot, result, fs, half, hs, qs, kh, kl = (R.get(n) for n in ("cot", "result", "fs", "half", "hs", "qs", "kh", "kl"))
        pr, rh, rl, qh, ql, th, tl, t12 = (R.get(n) for n in ("pr", "rh", "rl", "qh", "ql", "th", "tl", "t12"))
        pre, gs, gqh, gql, ghh, ghl, wide, down = (R.get(n) for n in ("pre", "gs", "gqh", "gql", "ghh", "ghl", "wide", "down"))
        g12h, g12l, um, m2r, m0t, m1t, outt, gskip = (R.get(n) for n in ("g12h", "g12l", "um", "m2r", "m0t", "m1t", "outt", "gskip"))
        gbias, pay, result_hbm = (R.get(n) for n in ("gbias", "pay", "result_hbm"))
        got = {}
        for k, name in enumerate(FED):
            src, dst = R[name + "_hbm"], R[name.rstrip("0")]
            got[name] = local(2 + k, src.at[0], dst.at[0]) if name.endswith("0") else local(2 + k, src, dst)
        load_c = local(0, R["cot_hbm"], cot)
        for name in ("hs", "qs"):
            got[name].start()
        for name in used:
            loads[name].start()
            if name == "xy2":
                load_c.start()
                for name in FED:
                    if name not in ("hs", "qs"):
                        got[name].start()
        spread_weights()
        got["hs"].wait()
        got["qs"].wait()
        loads["xy1"].wait()
        xy_transform(tab["xy1"], hs, 640, 2, 256)
        data = rows_cat(hs[:, 512:640], hs[0:640, 512:640])
        hi, lo = split(dot(tab["xy1"][...], data))
        th[:, 512:640] = hi
        tl[:, 512:640] = lo
        loads["z1"].wait()
        z_transform(th[:, 0:640], tl[:, 0:640], tab["z1"], 640, kh, kl, 1)
        loads["xy2"].wait()
        xy_transform(tab["xy2"], qs, 368, 2, 256)
        loads["z2"].wait()
        z_transform(th[:, 0:512], tl[:, 0:512], tab["z2"], 512, kh, kl, 2)
        lax.fori_loop(1, 3, lambda l, c: (modes_forward(l), c)[1], 0)

        loads["z1c"].wait()
        loads["z2c"].wait()
        for l, name in ((1, "z1c"), (2, "z2c")):
            tz = tab[name]
            v = dot(lanes_cat(qh[l], ql[l], qh[l]), rows_cat(tz[0:512], tz[0:512], tz[512:1024]))
            hi, lo = split(v)
            t12[256 * (l - 1) : 256 * l] = hi
            t12[512 + 256 * (l - 1) : 512 + 256 * l] = lo
        loads["xy12"].wait()
        loads["unpair"].wait()
        s = dot(tab["xy12"][...], rows_cat(t12[...], t12[0:512]))
        for n in range(3):
            hi, lo = split(s[:, 128 * n : 128 * (n + 1)])
            v = dot(lanes_cat(hi, lo), tab["unpair"][...])
            for k in range(2):
                for step in range(2):
                    wide[2 * n + k, pl.ds(step, 144, stride=2), :] = v[:, 128 * k : 128 * (k + 1)]

        load_c.wait()
        got["pre"].wait()
        scale = 1.0 / math.sqrt(ngx * ngy * ngz * NP**3)
        c0 = math.sqrt(2.0 / math.pi)

        def activate(m, carry):
            rows = pl.ds(pl.multiple_of(m * 48, 48), 48)
            v = lanes_cat(*[wide[n, pl.ds(pl.multiple_of(m * 24, 24), 24), :] for n in range(6)])
            x = pre[rows, :] + rows_cat(v, v)
            x2 = x * x
            t = jnp.tanh(c0 * (x * (1.0 + 0.044715 * x2)))
            half_t = 0.5 * (1.0 + t)
            result[rows, :] = x * half_t
            slope = half_t + 0.5 * x * (1.0 - t * t) * (c0 * (1.0 + (3 * 0.044715) * x2))
            g = cot[rows, :] * scale * slope
            hi, lo = split(g)
            gs[rows, :] = hi
            gs[pl.ds(pl.multiple_of(576 + m * 48, 48), 48), :] = lo
            g2 = g[0:24] + g[24:48]
            for n in range(6):
                down[n, pl.ds(pl.multiple_of(m * 24, 24), 24), :] = g2[:, 128 * n : 128 * (n + 1)]
            return carry + jnp.sum(g.reshape(6, 8, 768), axis=0)

        colsum = lax.fori_loop(0, 12, activate, jnp.zeros((8, 768), F32))
        store = local(1, result, result_hbm)
        store.start()
        gbias[...] = fold_lanes(colsum)

        for name in ("xy0", "z0", "pair"):
            loads[name].wait()
        xy_transform(tab["xy0"], gs, 576, 3, 256)
        z_transform(th[...], tl[...], tab["z0"], 768, gqh, gql, 0)
        for n in range(3):
            v = [down[2 * n + k, pl.ds(0, 144, stride=2), :] + down[2 * n + k, pl.ds(1, 144, stride=2), :] for k in range(2)]
            hi, lo = split(lanes_cat(*v))
            hi, lo = split(dot(lanes_cat(hi, lo), tab["pair"][...]))
            ghh[:, 128 * n : 128 * (n + 1)] = hi
            ghl[:, 128 * n : 128 * (n + 1)] = lo
        loads["xy12t"].wait()
        hi, lo = split(dot(tab["xy12t"][...], rows_cat(ghh[...], ghl[...], ghh[...])))
        g12h[...] = hi
        g12l[...] = lo
        loads["z2ct"].wait()
        z_transform(g12h[0:256], g12l[0:256], tab["z1"], 384, gqh, gql, 1, (0, 640))
        z_transform(g12h[256:512], g12l[256:512], tab["z2ct"], 384, gqh, gql, 2)

        for name in ("fs", "kh0", "kl0", "pr0", "rh0", "rl0"):
            got[name].wait()
        total = dot(stacked(fs), stacked(gs), TN)
        total = total[0:128] + total[128:256]
        total = jnp.where(diag_io, total[:, 0:128] + total[:, 128:256], 0.0)
        s = total[0:32] + total[32:64] + total[64:96] + total[96:128]
        s = s + pltpu.roll(s, 64, 1)
        gskip[...] = s + pltpu.roll(s, 32, 1)

        def gram(ah, al, bh, bl):
            a, b = [], []
            for ca, cb in quads:
                x, y = ah[:, ca], al[:, ca]
                v, w = bh[:, cb], bl[:, cb]
                a += [x, y, x]
                b += [v, v, w]
            g = jnp.where(diag_ir, dot(rows_cat(*a), rows_cat(*b), TN), 0.0)
            return fold_lanes(g[0:32] + g[32:64] + g[64:96] + g[96:128])

        low = iota((32, 128), 1) < 64

        def modes_backward(l, carry):
            u = um[l]
            u = lanes_cat(u, u)
            e = jnp.zeros((256, 128), F32)
            g2 = []
            g_out = gram(gqh.at[l], gql.at[l], rh.at[l], rl.at[l])
            data = [(gqh[l, :, c], gql[l, :, c]) for c, _ in quads]
            g = dot(rows_cat(*[lanes_cat(a, b, a) for a, b in data]), outt[l])
            for k, (_, cols) in enumerate(quads):
                gr = g[256 * k : 256 * (k + 1)]
                d = gr * pr[l, :, cols]
                m2 = m2r[l, 0:1, cols]
                dm = d * m2
                e = e + dm[:, 0:128] + dm[:, 128:256]
                g2.append(jnp.sum((d * u).reshape(32, 8, 256), axis=0))
                hi, lo = split(gr * (u * m2))
                rh[l, :, cols] = hi
                rl[l, :, cols] = lo
            g_in = gram(kh.at[l], kl.at[l], rh.at[l], rl.at[l])
            e = (e + pltpu.roll(e, 64, 1)).reshape(16, 16, 128)
            g0 = jnp.sum(e * m1t[l][None, :, :], axis=1)
            g1 = jnp.sum(e * m0t[l][:, None, :], axis=0)
            g2 = jnp.sum(lanes_cat(*g2), axis=0, keepdims=True)
            g2 = jnp.where(iota((16, 1024), 0) == iota((16, 1024), 1) // 64, g2, 0.0)
            g2 = fold_lanes(g2)
            row = pl.multiple_of(l * 64, 64)
            pay[pl.ds(row, 32), :] = jnp.where(low, g_in, g_out)
            pay[pl.ds(row + 32, 16), :] = jnp.where(low[0:16], g0, g1)
            pay[pl.ds(row + 48, 16), :] = jnp.where(low[0:16], g2, 0.0)
            return carry

        lax.fori_loop(0, 3, modes_backward, 0)
        s = gskip[...]
        s = jnp.where(iota((16, 128), 1) < 96, s[0:16], s[16:32])
        pay[48:64] = jnp.where(low[0:16], pay[48:64], s)
        b = gbias[...] + pltpu.roll(gbias[...], 32, 1)
        b = jnp.broadcast_to(jnp.sum(b, axis=0, keepdims=True), (16, 128))
        pay[112:128] = jnp.where(low[0:16], pay[112:128], b)

        store.wait()

    def sum_part():
        pay, ra, rb, acc, red, red_ref = (R.get(n) for n in ("pay", "ra", "rb", "acc", "red", "red_ref"))
        greet()
        pl.semaphore_wait(barrier, ngy - 1 + group - 1)
        size = PAY // ngy

        def pushes(count, make, act):
            def body(k, carry):
                act(make(k))
                return carry

            lax.fori_loop(1, count, body, 0)

        def scatter(k):
            t = lax.rem(gy + k, ngy)
            return pltpu.make_async_remote_copy(
                src_ref=pay.at[pl.ds(pl.multiple_of(t * size, 8), size)],
                dst_ref=ra.at[k],
                send_sem=red_send.at[k],
                recv_sem=red_recv.at[k],
                device_id=(gx, t, gz),
                device_id_type=MESH,
            )

        def exchange(k):
            q = lax.rem(me + k, group)
            return pltpu.make_async_remote_copy(
                src_ref=acc,
                dst_ref=rb.at[me],
                send_sem=red_send.at[ngy + k],
                recv_sem=red_recv.at[ngy + k],
                device_id=(q // ngz, gy, lax.rem(q, ngz)),
                device_id_type=MESH,
            )

        mine = pl.ds(pl.multiple_of(gy * size, 8), size)

        def gather(k):
            t = lax.rem(gy + k, ngy)
            return pltpu.make_async_remote_copy(
                src_ref=red.at[mine],
                dst_ref=red.at[mine],
                send_sem=red_send.at[ngy + group + k],
                recv_sem=red_recv.at[ngy + group + k],
                device_id=(gx, t, gz),
                device_id_type=MESH,
            )

        pushes(ngy, scatter, start)
        pushes(ngy, scatter, recv)
        total = pay[mine]
        for k in range(1, ngy):
            total = total + ra[k]
        acc[...] = total
        rb[me] = total
        pushes(group, exchange, start)
        pushes(group, exchange, recv)
        total = rb[0]
        for k in range(1, group):
            total = total + rb[k]
        red[mine] = total
        pushes(ngy, gather, start)
        pushes(ngy, gather, recv)
        red_ref[...] = red[...]

        pushes(ngy, scatter, sent)
        pushes(group, exchange, sent)
        pushes(ngy, gather, sent)

    {"A": fine_part, "B": coarse_part, "C": sum_part}[parts]()


def unpack_kernel(red, skip, bias, modes, fin, fout):
    skip[0:16] = red[48:64, 64:96]
    skip[16:32] = red[48:64, 96:128]
    bias[...] = red[112:113, 64:96]
    for l in range(3):
        row = 64 * l
        fin[l] = red[row : row + 32, 0:64]
        fout[l] = red[row : row + 32, 64:128]
        modes[l, 0] = red[row + 32 : row + 48, 0:64]
        modes[l, 1] = red[row + 32 : row + 48, 64:128]
        modes[l, 2] = red[row + 48 : row + 64, 0:64]


def solution(mesh):
    sizes = tuple(mesh.shape[name] for name in ("gx", "gy", "gz"))
    ngx, ngy, ngz = sizes
    group = ngx * ngz
    size = PAY // ngy
    any_spec = pl.BlockSpec(memory_space=pl.ANY)
    vmem_spec = pl.BlockSpec(memory_space=pltpu.VMEM)
    shapes = dict(SHAPES)
    shapes.update(ra=((ngy, size, 128), F32), rb=((group, size, 128), F32), acc=((size, 128), F32))

    def call(part, args, flops):
        names = KERNELS[part]

        def out_shape(n):
            shape, kind = shapes[n]
            if part == "A" and len(shape) == 3:
                shape = (1,) + shape[1:]
            return jax.ShapeDtypeStruct(shape, kind)

        remote = {} if part == "B" else {"collective_id": "AC".index(part), "has_side_effects": True}
        return pl.pallas_call(
            lambda *refs: layer_kernel(sizes, part, *refs),
            name="part_" + part.lower(),
            out_shape=tuple(out_shape(n) for n in names["outs"]),
            in_specs=[any_spec if n.endswith("hbm") else vmem_spec for n in names["ins"]] + [any_spec] * len(names["tables"]),
            out_specs=tuple(any_spec if n.endswith("hbm") else vmem_spec for n in names["outs"]),
            scratch_shapes=[pltpu.VMEM(table_shape(n), BF) for n in names["tables"]]
            + [pltpu.VMEM(*shapes[n]) for n in names["scratch"]]
            + [
                pltpu.SemaphoreType.DMA((max(1, len(names["tables"])),)),
                pltpu.SemaphoreType.DMA((2 + len(FED),)),
                pltpu.SemaphoreType.DMA((18,)),
                pltpu.SemaphoreType.DMA((18,)),
                pltpu.SemaphoreType.DMA((2 * ngy + group,)),
                pltpu.SemaphoreType.DMA((2 * ngy + group,)),
            ],
            compiler_params=pltpu.CompilerParams(vmem_limit_bytes=58 * 1024 * 1024, **remote),
            cost_estimate=pl.CostEstimate(flops=flops, bytes_accessed=10 * 10**6, transcendentals=442368),
        )(*args, *[jnp.asarray(TABLES[n]) for n in names["tables"]])

    def per_device(features, cotangent, skip_weight, bias_vector, mode_factors, in_factors, out_factors):
        weights = (skip_weight, bias_vector.reshape(1, CH), mode_factors, in_factors, jnp.swapaxes(out_factors, 1, 2))
        fed = call("A", (features.reshape(576, 768), *weights), 5 * 10**9)
        result, pay = call("B", (cotangent.reshape(576, 768), *weights, *fed), 10**10)
        (red,) = call("C", (pay,), 10**6)
        outs = pl.pallas_call(
            unpack_kernel,
            name="unpack",
            out_shape=(
                jax.ShapeDtypeStruct((CH, CH), F32),
                jax.ShapeDtypeStruct((1, CH), F32),
                jax.ShapeDtypeStruct((3, 3, MD, RK), F32),
                jax.ShapeDtypeStruct((3, CH, RK), F32),
                jax.ShapeDtypeStruct((3, CH, RK), F32),
            ),
            in_specs=[vmem_spec],
            out_specs=(vmem_spec,) * 5,
        )(red)
        return (result.reshape(NP, NP, NP * CH), outs[0], outs[1].reshape(CH), outs[2], outs[3], jnp.swapaxes(outs[4], 1, 2))

    placed = (P("gx", "gy", "gz"), P("gx", "gy", "gz"), P(), P(), P(), P(), P())
    return jax.shard_map(
        per_device,
        mesh=mesh,
        in_specs=placed,
        out_specs=(P("gx", "gy", "gz"), P(), P(), P(), P(), P()),
        check_vma=False,
    )
```

```python
import math

import jax
import jax.numpy as jnp
import ml_dtypes
import numpy as np
from jax import lax
from jax.experimental import pallas as pl
from jax.experimental.pallas import tpu as pltpu
from jax.sharding import PartitionSpec as P

MESH = pl.DeviceIdType.MESH
BF = jnp.bfloat16
F32 = jnp.float32
CH, RK, MD, NP = 32, 64, 16, 24
NN = (((1,), (0,)), ((), ()))
NT = (((1,), (1,)), ((), ()))
TN = (((0,), (0,)), ((), ()))
PAY = 192


def basis(length):
    rows = np.arange(MD)
    freq = np.where(rows < MD // 2, rows, rows - MD // 2 + 1).astype(np.float64)
    phase = 2.0 * math.pi / length * freq[:, None] * np.arange(length)[None, :]
    wave = np.where((rows < MD // 2)[:, None], np.cos(phase), np.sin(phase))
    return wave * math.sqrt(2.0 / length)


def halves(x):
    x = np.asarray(x, np.float32)
    hi = x.astype(ml_dtypes.bfloat16)
    lo = (x - hi.astype(np.float32)).astype(ml_dtypes.bfloat16)
    return hi, lo


def left(x):
    hi, lo = halves(x)
    return np.concatenate([hi, hi, lo], axis=1)


def right(x):
    hi, lo = halves(x)
    return np.concatenate([hi, lo], axis=0)


def exact(x, times, axis):
    x = np.asarray(x, np.float32).astype(ml_dtypes.bfloat16)
    return np.concatenate([x] * times, axis=axis)


def channel_eye(b):
    return np.kron(b, np.eye(CH))


def make_tables():
    b24, b18 = basis(24), basis(18)
    pool = np.zeros((208, 12, 24))
    for j in range(2):
        for i in range(2):
            for r in range(36):
                x, y = i * 6 + r // 6, 2 * (j * 6 + r % 6)
                pool[(j * 2 + i) * 40 + r, x, y : y + 2] = 1 / 8
    for r in range(36):
        x, y = 2 * (r // 6), 4 * (r % 6)
        pool[160 + r, x : x + 2, y : y + 4] = 1 / 64
    pool = pool.reshape(208, 288)
    pair = channel_eye(np.kron(np.eye(4), np.ones((2, 1))))
    quad = np.zeros((24, 8))
    for z in range(24):
        quad[z, z // 4] = 1
    quad = channel_eye(quad)
    xy0 = np.kron(b24, b24)
    at4, at3 = (1, 2, 0, 3), (1, 0, 2)
    xy1 = np.zeros((256, 4, 4, 40))
    for j in range(4):
        for i in range(4):
            for r in range(36):
                xy1[:, j, i, r] = np.kron(b24[:, at4[i] * 6 + r // 6], b24[:, at4[j] * 6 + r % 6])
    xy2 = np.zeros((256, 368))
    for j in range(3):
        for i in range(3):
            for r in range(36):
                xy2[:, (j * 3 + i) * 40 + r] = np.kron(
                    b18[:, at3[i] * 6 + r // 6], b18[:, at3[j] * 6 + r % 6]
                )
    z0 = channel_eye(b24.T)
    z1s, z2s = [], []
    for gz in range(2):
        z1 = np.zeros((20, 16))
        z1[0:12] = b24[:, 6:18].T
        if gz == 0:
            z1[12:18] = b24[:, 18:24].T
        else:
            z1[12:16] = b24[:, 2:6].T
            z1[16:18] = b24[:, 0:2].T
        z1s.append(right(channel_eye(z1)))
        z2 = np.zeros((16, 16))
        z2[0:6] = b18[:, 6:12].T
        z2[8:14] = b18[:, 12:18].T if gz == 0 else b18[:, 0:6].T
        z2s.append(right(channel_eye(z2)))
    z1c = channel_eye(b24[:, 6:18])
    z2c = channel_eye(np.repeat(b18[:, 6:12], 2, axis=1))
    c1 = b24[:, 6:18]
    c2 = np.repeat(b18[:, 6:12], 2, axis=1)
    xy12 = np.concatenate([np.kron(c1, c1), np.kron(c2, c2)], axis=0)
    return {
        "pool": exact(pool, 2, 1),
        "pair": exact(pair, 2, 0),
        "quad": exact(quad, 2, 0),
        "unpair": exact(pair.T, 2, 0),
        "xy0": left(xy0),
        "z0": right(z0),
        "z0t": right(z0.T),
        "inv": left(xy0.T),
        "xy1": left(xy1.reshape(256, 640)),
        "z1": np.concatenate(z1s, axis=0),
        "xy2": left(xy2),
        "z2": np.concatenate(z2s, axis=0),
        "z1c": right(z1c),
        "z2c": right(z2c),
        "xy12": left(xy12.T),
        "xy12t": left(xy12),
        "z2ct": right(z2c.T),
    }


TABLES = make_tables()
NAMES = list(TABLES)


def table_shape(name):
    rows, cols = TABLES[name].shape
    return (rows // 2 if name in ("z1", "z2") else rows), cols


def dot(a, b, dims=NN):
    return lax.dot_general(a, b, dims, preferred_element_type=F32)


def split(x):
    hi = x.astype(BF)
    return hi, (x - hi.astype(F32)).astype(BF)


def rows_cat(*parts):
    return jnp.concatenate(parts, axis=0)


def lanes_cat(*parts):
    return jnp.concatenate(parts, axis=1)


def iota(shape, dim):
    return lax.broadcasted_iota(jnp.int32, shape, dim)


def fold_lanes(x):
    total = x[:, 0:128]
    for k in range(1, x.shape[1] // 128):
        total = total + x[:, 128 * k : 128 * (k + 1)]
    return total + pltpu.roll(total, 64, 1)


def layer_kernel(sizes, *refs):
    ngx, ngy, ngz = sizes
    refs = list(refs)
    take = lambda n: [refs.pop(0) for _ in range(n)]
    feat_hbm, cot_hbm, skip_ref, bias_ref, modes_ref, in_ref, out_ref = take(7)
    hbm = dict(zip(NAMES, take(len(NAMES))))
    result_hbm, red_ref = take(2)
    tab = dict(zip(NAMES, take(len(NAMES))))
    (feat, cot, result, fs, half, quart, hs, qs, kh, kl, pr, rh, rl, qh, ql, th, tl, bs, t12, pre, gs, gqh, gql, ghh, ghl,
     wide, down, g12h, g12l, um, m2r, m0t, m1t, inw, outw, outt, skw, biast, gskip, gbias, pay, ra, rb, acc, red, zsend, zrecv, qth, qtl) = take(49)
    table_sem, local_sem, halo_send, halo_recv, red_send, red_recv = take(6)

    gx, gy, gz = lax.axis_index("gx"), lax.axis_index("gy"), lax.axis_index("gz")
    me = gx * ngz + gz
    group = ngx * ngz

    load_f = pltpu.make_async_copy(feat_hbm, feat, local_sem.at[0])
    load_f.start()
    load_c = pltpu.make_async_copy(cot_hbm, cot, local_sem.at[1])
    loads = {}
    for k, name in enumerate(NAMES):
        rows = table_shape(name)[0]
        src = hbm[name].at[pl.ds(pl.multiple_of(gz * rows, 16), rows)] if name in ("z1", "z2") else hbm[name]
        loads[name] = pltpu.make_async_copy(src, tab[name], table_sem.at[k])
        if k < 3:
            loads[name].start()

    barrier = pltpu.get_barrier_semaphore()

    def greet_row(k, carry):
        pl.semaphore_signal(
            barrier, inc=1, device_id=(gx, lax.rem(gy + k, ngy), gz), device_id_type=MESH
        )
        return carry

    lax.fori_loop(1, ngy, greet_row, 0)

    def greet_plane(k, carry):
        q = lax.rem(me + k, group)
        pl.semaphore_signal(
            barrier, inc=1, device_id=(q // ngz, gy, lax.rem(q, ngz)), device_id_type=MESH
        )
        return carry

    lax.fori_loop(1, group, greet_plane, 0)

    def clear(j, i):
        half[j, i] = jnp.zeros((40, 640), F32)

    def clear_quarter(j, i):
        quart[j, i] = jnp.zeros((40, 512), F32)

    for edge, block in ((gx == 0, 2), (gx == ngx - 1, 3)):

        @pl.when(edge)
        def _():
            clear(0, block)
            clear(1, block)
            clear_quarter(0, block - 1)

    for edge, block in ((gy == 0, 2), (gy == ngy - 1, 3)):

        @pl.when(edge)
        def _():
            for i in range(4):
                clear(block, i)
            for i in range(3):
                clear_quarter(block - 1, i)

    load_f.wait()
    for name in NAMES[3:]:
        loads[name].start()
        if name == "xy2":
            load_c.start()
    cells = feat[...].reshape(12, 2, 24, 768)
    hi, lo = split((cells[:, 0] + cells[:, 1]).reshape(288, 768))
    gs[0:288] = hi
    gs[288:576] = lo
    loads["pool"].wait()
    for n in range(3):
        pre[0:208, 256 * n : 256 * (n + 1)] = dot(tab["pool"][...], gs[0:576, 256 * n : 256 * (n + 1)])
    hi, lo = split(pre[0:208])
    loads["pair"].wait()
    for n in range(3):
        cols = slice(256 * n, 256 * (n + 1))
        cells = dot(lanes_cat(hi[0:160, cols], lo[0:160, cols]), tab["pair"][...])
        for j in range(2):
            for i in range(2):
                r = (j * 2 + i) * 40
                half[j, i, :, 128 * n : 128 * (n + 1)] = cells[r : r + 40]
    loads["quad"].wait()
    cells = dot(lanes_cat(hi[160:208], lo[160:208]), tab["quad"][...])
    quart[0, 0, :, 0:256] = cells[0:40]
    for i in range(2):
        a, b = half[0, i, :, 128:256], half[1, i, :, 128:256]
        a = jnp.where(gz == 1, a, pltpu.roll(a, 64, 1))
        b = jnp.where(gz == 1, pltpu.roll(b, 64, 1), b)
        zsend[i] = jnp.where(iota((40, 128), 1) < 64, a, b)

    pl.semaphore_wait(barrier, ngy - 1 + group - 1)

    def remote(k, src, dst, to):
        return pltpu.make_async_remote_copy(
            src_ref=src,
            dst_ref=dst,
            send_sem=halo_send.at[k],
            recv_sem=halo_recv.at[k],
            device_id=to,
            device_id_type=MESH,
        )

    first = pl.multiple_of(256 * (1 - gz), 128)
    own, far, qown, qfar = pl.ds(0, 384), pl.ds(384, 256), pl.ds(0, 256), pl.ds(256, 256)
    mid, side = pl.ds(0, 2), pl.ds(2, 2)
    qside = pl.ds(1, 2)
    across = (gx, gy, 1 - gz)
    z_all = [
        remote(0, half.at[mid, mid, :, pl.ds(first, 128)], half.at[mid, mid, :, pl.ds(384, 128)], across),
        remote(1, zsend, zrecv, across),
        remote(2, quart.at[0, 0, :, qown], quart.at[0, 0, :, qfar], across),
    ]

    def x_copies(k, src, dst, to):
        return [
            remote(k, half.at[mid, src, :, own], half.at[mid, dst, :, own], to),
            remote(k + 1, quart.at[0, 0, :, qown], quart.at[0, dst - 1, :, qown], to),
            remote(k + 2, half.at[mid, src, :, far], half.at[mid, dst, :, far], to),
            remote(k + 3, quart.at[0, 0, :, qfar], quart.at[0, dst - 1, :, qfar], to),
        ]

    def y_copies(k, src, dst, to):
        return [
            remote(k, half.at[src, mid, :, own], half.at[dst, mid, :, own], to),
            remote(k + 1, quart.at[0, 0, :, qown], quart.at[dst - 1, 0, :, qown], to),
            remote(k + 2, half.at[src, side, :, own], half.at[dst, side, :, own], to),
            remote(k + 3, quart.at[0, qside, :, qown], quart.at[dst - 1, qside, :, qown], to),
            remote(k + 4, half.at[src, mid, :, far], half.at[dst, mid, :, far], to),
            remote(k + 5, quart.at[0, 0, :, qfar], quart.at[dst - 1, 0, :, qfar], to),
            remote(k + 6, half.at[src, side, :, far], half.at[dst, side, :, far], to),
            remote(k + 7, quart.at[0, qside, :, qfar], quart.at[dst - 1, qside, :, qfar], to),
        ]

    xs = x_copies(3, 1, 2, (gx + 1, gy, gz)), x_copies(7, 0, 3, (gx - 1, gy, gz))
    ys = y_copies(11, 1, 2, (gx, gy + 1, gz)), y_copies(19, 0, 3, (gx, gy - 1, gz))

    def each(copies, which, to_up, to_down, act):
        @pl.when(to_up)
        def _():
            for k in which:
                act(copies[0][k])

        @pl.when(to_down)
        def _():
            for k in which:
                act(copies[1][k])

    has_ux, has_dx, has_uy, has_dy = gx < ngx - 1, gx > 0, gy < ngy - 1, gy > 0
    start = lambda c: c.start()
    recv = lambda c: c.wait_recv()
    sent = lambda c: c.wait_send()

    for c in z_all:
        c.start()
    each(xs, (0, 1), has_ux, has_dx, start)
    each(ys, (0, 1), has_uy, has_dy, start)

    def dup64(x):
        eye = (iota((64, 128), 0) == iota((64, 128), 1) % 64).astype(BF)
        return dot(x, eye)

    def dup32(x):
        eye = (iota((32, 128), 0) == iota((32, 128), 1) % 32).astype(BF)
        return dot(x, eye)

    diag_ir = iota((128, 256), 0) // 32 == iota((128, 256), 1) // 64
    diag_ro = iota((256, 128), 0) // 64 == iota((256, 128), 1) // 32
    diag_io = iota((128, 128), 0) // 32 == iota((128, 128), 1) // 32
    eye64 = (iota((64, 64), 0) == iota((64, 64), 1)).astype(BF)

    b0, b1 = split(jnp.broadcast_to(bias_ref[...], (16, 32)))
    biast[...] = (dup32(b0) + dup32(b1))[0:8]
    w0, w1 = [jnp.where(diag_io, rows_cat(*[dup32(w)] * 4), 0.0).astype(BF) for w in split(skip_ref[...])]
    w0 = lanes_cat(w0, w1)
    skw[...] = rows_cat(w0, w0)

    def spread(l, carry):
        i0, i1 = split(in_ref[l])
        o0, o1 = split(out_ref[l])

        def wide(w):
            t = dup64(w)
            return jnp.where(diag_ir, rows_cat(*[lanes_cat(t, t)] * 4), 0.0).astype(BF)

        def tall(w):
            t = dup32(dot(eye64, w, NT).astype(BF))
            return jnp.where(diag_ro, rows_cat(*[t] * 4), 0.0).astype(BF)

        w0 = wide(i0)
        inw[l] = rows_cat(w0, w0, wide(i1))
        w0 = wide(o0)
        outt[l] = rows_cat(w0, w0, wide(o1))
        w0 = lanes_cat(tall(o0), tall(o1))
        outw[l] = rows_cat(w0, w0)
        dup = []
        for d in range(3):
            m = modes_ref[l, d]
            hi, lo = split(m)
            rest = (m - hi.astype(F32) - lo.astype(F32)).astype(BF)
            dup.append(dup64(hi) + dup64(lo) + dup64(rest))
        m0t[l] = dup[0]
        m1t[l] = dup[1]
        um[l] = (dup[0][:, None, :] * dup[1][None, :, :]).reshape(256, 128)
        line = lanes_cat(*[dup[2]] * 8)
        line = jnp.where(iota((16, 1024), 0) == iota((16, 1024), 1) // 64, line, 0.0)
        m2r[l] = jnp.broadcast_to(jnp.sum(line, axis=0, keepdims=True), (8, 1024))
        return carry

    lax.fori_loop(0, 3, spread, 0)

    hi, lo = split(feat[...])
    fs[0:576] = hi
    fs[576:1152] = lo

    def stacked(ref):
        parts = [slice(128 * n, 128 * (n + 1)) for n in range(6)]
        return rows_cat(*[lanes_cat(ref[0:576, c], ref[576:1152, c]) for c in parts])

    def xy_transform(table, hi_lo, rows, chunks, wide):
        for n in range(chunks):
            cols = slice(wide * n, wide * (n + 1))
            data = rows_cat(hi_lo[0 : 2 * rows, cols], hi_lo[0:rows, cols])
            hi, lo = split(dot(table[...], data))
            th[:, cols] = hi
            tl[:, cols] = lo

    def z_transform(hi, lo, table, depth, into_h, into_l, l, parts=None):
        a = lanes_cat(hi, lo, hi)
        zh, zl = (0, depth) if parts is None else parts
        for n in range(2):
            cols = slice(256 * n, 256 * (n + 1))
            tz = rows_cat(table[zh : zh + depth, cols], table[zh : zh + depth, cols], table[zl : zl + depth, cols])
            vh, vl = split(dot(a, tz))
            into_h[l, :, cols] = vh
            into_l[l, :, cols] = vl

    quads = [(slice(128 * c, 128 * (c + 1)), slice(256 * c, 256 * (c + 1))) for c in range(4)]

    def modes_forward(l):
        data = [(kh[l, :, c], kl[l, :, c]) for c, _ in quads]
        p = dot(rows_cat(*[lanes_cat(a, b, a) for a, b in data]), inw[l])
        u = um[l]
        u = lanes_cat(u, u)
        data = []
        for k, (_, cols) in enumerate(quads):
            pk = p[256 * k : 256 * (k + 1)]
            pr[l, :, cols] = pk
            a, b = split(pk * u * m2r[l, 0:1, cols])
            rh[l, :, cols] = a
            rl[l, :, cols] = b
            data.append(lanes_cat(a, b))
        q = dot(rows_cat(*data), outw[l])
        q = q[:, 0:128] + q[:, 128:256]
        for k, (cols, _) in enumerate(quads):
            a, b = split(q[256 * k : 256 * (k + 1)])
            qh[l, :, cols] = a
            ql[l, :, cols] = b

    v = dot(stacked(fs), skw[...])
    v = v[:, 0:128] + v[:, 128:256] + biast[0:1]
    for n in range(6):
        pre[:, 128 * n : 128 * (n + 1)] = v[576 * n : 576 * (n + 1)]
    loads["xy0"].wait()
    xy_transform(tab["xy0"], fs, 576, 3, 256)

    each(xs, (0, 1), has_dx, has_ux, recv)
    each(ys, (2, 3), has_uy, has_dy, start)

    loads["z0"].wait()
    z_transform(th[...], tl[...], tab["z0"], 768, kh, kl, 0)

    for c in z_all:
        c.wait_recv()
    low = iota((40, 128), 1) < 64
    for i in range(2):
        a = zrecv[i]
        half[0, i, :, 512:640] = jnp.where(low, a, 0.0)
        half[1, i, :, 512:640] = jnp.where(low, pltpu.roll(a, 64, 1), 0.0)
    each(xs, (2, 3), has_ux, has_dx, start)
    each(ys, (4, 5), has_uy, has_dy, start)

    modes_forward(0)
    loads["z0t"].wait()
    a = lanes_cat(qh[0], ql[0], qh[0])
    for n in range(3):
        cols = slice(256 * n, 256 * (n + 1))
        tz = rows_cat(tab["z0t"][0:512, cols], tab["z0t"][0:512, cols], tab["z0t"][512:1024, cols])
        hi, lo = split(dot(a, tz))
        bs[0:256, cols] = hi
        bs[256:512, cols] = lo
    each(xs, (2, 3), has_dx, has_ux, recv)
    each(ys, (6, 7), has_uy, has_dy, start)
    loads["inv"].wait()
    for n in range(3):
        cols = slice(256 * n, 256 * (n + 1))
        pre[:, cols] = pre[:, cols] + dot(tab["inv"][...], rows_cat(bs[0:512, cols], bs[0:256, cols]))

    def halves_of(cols, qcols):
        for j in range(4):
            hi, lo = split(half[j, :, :, cols].reshape(160, -1))
            hs[160 * j : 160 * (j + 1), cols] = hi
            hs[640 + 160 * j : 640 + 160 * (j + 1), cols] = lo
        cells = quart[:, :, :, qcols].reshape(360, 256)
        hi, lo = split(rows_cat(cells, jnp.zeros((8, 256), F32)))
        qs[0:368, qcols] = hi
        qs[368:736, qcols] = lo

    def one_chunk(table, data, rows, cols, into_h, into_l):
        v = rows_cat(data[0 : 2 * rows, cols], data[0:rows, cols])
        hi, lo = split(dot(table[...], v))
        into_h[:, cols] = hi
        into_l[:, cols] = lo

    each(ys, (0, 1, 2, 3), has_dy, has_uy, recv)
    halves_of(slice(0, 384), slice(0, 256))
    loads["xy1"].wait()
    loads["xy2"].wait()
    one_chunk(tab["xy1"], hs, 640, slice(0, 256), th, tl)
    v = lanes_cat(hs[0:640, 256:384], hs[640:1280, 256:384])
    v = dot(tab["xy1"][:, 640:1920], rows_cat(v, v))
    hi, lo = split(v[:, 0:128] + v[:, 128:256])
    th[:, 256:384] = hi
    tl[:, 256:384] = lo
    one_chunk(tab["xy2"], qs, 368, slice(0, 256), qth, qtl)

    each(ys, (4, 5, 6, 7), has_dy, has_uy, recv)
    halves_of(slice(384, 640), slice(256, 512))
    one_chunk(tab["xy1"], hs, 640, slice(384, 640), th, tl)
    one_chunk(tab["xy2"], qs, 368, slice(256, 512), qth, qtl)
    loads["z1"].wait()
    z_transform(th[:, 0:640], tl[:, 0:640], tab["z1"], 640, kh, kl, 1)
    loads["z2"].wait()
    z_transform(qth[...], qtl[...], tab["z2"], 512, kh, kl, 2)
    lax.fori_loop(1, 3, lambda l, c: (modes_forward(l), c)[1], 0)

    loads["z1c"].wait()
    loads["z2c"].wait()
    for l, name in ((1, "z1c"), (2, "z2c")):
        tz = tab[name]
        v = dot(lanes_cat(qh[l], ql[l], qh[l]), rows_cat(tz[0:512], tz[0:512], tz[512:1024]))
        hi, lo = split(v)
        t12[256 * (l - 1) : 256 * l] = hi
        t12[512 + 256 * (l - 1) : 512 + 256 * l] = lo
    loads["xy12"].wait()
    loads["unpair"].wait()
    s = dot(tab["xy12"][...], rows_cat(t12[...], t12[0:512]))
    for n in range(3):
        hi, lo = split(s[:, 128 * n : 128 * (n + 1)])
        v = dot(lanes_cat(hi, lo), tab["unpair"][...])
        for k in range(2):
            for step in range(2):
                wide[2 * n + k, pl.ds(step, 144, stride=2), :] = v[:, 128 * k : 128 * (k + 1)]

    load_c.wait()
    scale = 1.0 / math.sqrt(ngx * ngy * ngz * NP**3)
    c0 = math.sqrt(2.0 / math.pi)
    store = pltpu.make_async_copy(result, result_hbm, local_sem.at[2])

    def activate(m, carry):
        rows = pl.ds(pl.multiple_of(m * 48, 48), 48)
        v = lanes_cat(*[wide[n, pl.ds(pl.multiple_of(m * 24, 24), 24), :] for n in range(6)])
        x = pre[rows, :] + rows_cat(v, v)
        x2 = x * x
        t = jnp.tanh(c0 * (x * (1.0 + 0.044715 * x2)))
        half_t = 0.5 * (1.0 + t)
        result[rows, :] = x * half_t
        slope = half_t + 0.5 * x * (1.0 - t * t) * (c0 * (1.0 + (3 * 0.044715) * x2))
        g = cot[rows, :] * scale * slope
        hi, lo = split(g)
        gs[rows, :] = hi
        gs[pl.ds(pl.multiple_of(576 + m * 48, 48), 48), :] = lo
        g2 = g[0:24] + g[24:48]
        for n in range(6):
            down[n, pl.ds(pl.multiple_of(m * 24, 24), 24), :] = g2[:, 128 * n : 128 * (n + 1)]
        return carry + jnp.sum(g.reshape(6, 8, 768), axis=0)

    colsum = lax.fori_loop(0, 12, activate, jnp.zeros((8, 768), F32))
    store.start()
    gbias[...] = fold_lanes(colsum)

    xy_transform(tab["xy0"], gs, 576, 3, 256)
    z_transform(th[...], tl[...], tab["z0"], 768, gqh, gql, 0)
    for n in range(3):
        v = [down[2 * n + k, pl.ds(0, 144, stride=2), :] + down[2 * n + k, pl.ds(1, 144, stride=2), :] for k in range(2)]
        hi, lo = split(lanes_cat(*v))
        hi, lo = split(dot(lanes_cat(hi, lo), tab["pair"][...]))
        ghh[:, 128 * n : 128 * (n + 1)] = hi
        ghl[:, 128 * n : 128 * (n + 1)] = lo
    loads["xy12t"].wait()
    hi, lo = split(dot(tab["xy12t"][...], rows_cat(ghh[...], ghl[...], ghh[...])))
    g12h[...] = hi
    g12l[...] = lo
    loads["z2ct"].wait()
    z_transform(g12h[0:256], g12l[0:256], tab["z1"], 384, gqh, gql, 1, (0, 640))
    z_transform(g12h[256:512], g12l[256:512], tab["z2ct"], 384, gqh, gql, 2)

    total = dot(stacked(fs), stacked(gs), TN)
    total = total[0:128] + total[128:256]
    total = jnp.where(diag_io, total[:, 0:128] + total[:, 128:256], 0.0)
    s = total[0:32] + total[32:64] + total[64:96] + total[96:128]
    s = s + pltpu.roll(s, 64, 1)
    gskip[...] = s + pltpu.roll(s, 32, 1)

    def gram(ah, al, bh, bl):
        a, b = [], []
        for ca, cb in quads:
            x, y = ah[:, ca], al[:, ca]
            v, w = bh[:, cb], bl[:, cb]
            a += [x, y, x]
            b += [v, v, w]
        g = jnp.where(diag_ir, dot(rows_cat(*a), rows_cat(*b), TN), 0.0)
        return fold_lanes(g[0:32] + g[32:64] + g[64:96] + g[96:128])

    low = iota((32, 128), 1) < 64

    def modes_backward(l, carry):
        u = um[l]
        u = lanes_cat(u, u)
        e = jnp.zeros((256, 128), F32)
        g2 = []
        g_out = gram(gqh.at[l], gql.at[l], rh.at[l], rl.at[l])
        data = [(gqh[l, :, c], gql[l, :, c]) for c, _ in quads]
        g = dot(rows_cat(*[lanes_cat(a, b, a) for a, b in data]), outt[l])
        for k, (_, cols) in enumerate(quads):
            gr = g[256 * k : 256 * (k + 1)]
            d = gr * pr[l, :, cols]
            m2 = m2r[l, 0:1, cols]
            dm = d * m2
            e = e + dm[:, 0:128] + dm[:, 128:256]
            g2.append(jnp.sum((d * u).reshape(32, 8, 256), axis=0))
            hi, lo = split(gr * (u * m2))
            rh[l, :, cols] = hi
            rl[l, :, cols] = lo
        g_in = gram(kh.at[l], kl.at[l], rh.at[l], rl.at[l])
        e = (e + pltpu.roll(e, 64, 1)).reshape(16, 16, 128)
        g0 = jnp.sum(e * m1t[l][None, :, :], axis=1)
        g1 = jnp.sum(e * m0t[l][:, None, :], axis=0)
        g2 = jnp.sum(lanes_cat(*g2), axis=0, keepdims=True)
        g2 = jnp.where(iota((16, 1024), 0) == iota((16, 1024), 1) // 64, g2, 0.0)
        g2 = fold_lanes(g2)
        row = pl.multiple_of(l * 64, 64)
        pay[pl.ds(row, 32), :] = jnp.where(low, g_in, g_out)
        pay[pl.ds(row + 32, 16), :] = jnp.where(low[0:16], g0, g1)
        pay[pl.ds(row + 48, 16), :] = jnp.where(low[0:16], g2, 0.0)
        return carry

    lax.fori_loop(0, 3, modes_backward, 0)
    s = gskip[...]
    s = jnp.where(iota((16, 128), 1) < 96, s[0:16], s[16:32])
    pay[48:64] = jnp.where(low[0:16], pay[48:64], s)
    b = gbias[...] + pltpu.roll(gbias[...], 32, 1)
    b = jnp.broadcast_to(jnp.sum(b, axis=0, keepdims=True), (16, 128))
    pay[112:128] = jnp.where(low[0:16], pay[112:128], b)

    size = PAY // ngy

    def pushes(count, make, act):
        def body(k, carry):
            act(make(k))
            return carry

        lax.fori_loop(1, count, body, 0)

    def scatter(k):
        t = lax.rem(gy + k, ngy)
        return pltpu.make_async_remote_copy(
            src_ref=pay.at[pl.ds(pl.multiple_of(t * size, 8), size)],
            dst_ref=ra.at[k],
            send_sem=red_send.at[k],
            recv_sem=red_recv.at[k],
            device_id=(gx, t, gz),
            device_id_type=MESH,
        )

    def exchange(k):
        q = lax.rem(me + k, group)
        return pltpu.make_async_remote_copy(
            src_ref=acc,
            dst_ref=rb.at[me],
            send_sem=red_send.at[ngy + k],
            recv_sem=red_recv.at[ngy + k],
            device_id=(q // ngz, gy, lax.rem(q, ngz)),
            device_id_type=MESH,
        )

    mine = pl.ds(pl.multiple_of(gy * size, 8), size)

    def gather(k):
        t = lax.rem(gy + k, ngy)
        return pltpu.make_async_remote_copy(
            src_ref=red.at[mine],
            dst_ref=red.at[mine],
            send_sem=red_send.at[ngy + group + k],
            recv_sem=red_recv.at[ngy + group + k],
            device_id=(gx, t, gz),
            device_id_type=MESH,
        )

    pushes(ngy, scatter, start)
    pushes(ngy, scatter, recv)
    total = pay[mine]
    for k in range(1, ngy):
        total = total + ra[k]
    acc[...] = total
    rb[me] = total
    pushes(group, exchange, start)
    pushes(group, exchange, recv)
    total = rb[0]
    for k in range(1, group):
        total = total + rb[k]
    red[mine] = total
    pushes(ngy, gather, start)
    pushes(ngy, gather, recv)
    red_ref[...] = red[...]

    pushes(ngy, scatter, sent)
    pushes(group, exchange, sent)
    pushes(ngy, gather, sent)
    for c in z_all:
        c.wait_send()
    each(xs, range(4), has_ux, has_dx, sent)
    each(ys, range(8), has_uy, has_dy, sent)
    store.wait()


def unpack_kernel(result_in, red, result_out, skip, bias, modes, fin, fout, held, sem):
    parts = [pl.ds(144 * k, 144) for k in range(4)]
    fetch = [pltpu.make_async_copy(result_in.at[p], held.at[p], sem.at[k]) for k, p in enumerate(parts)]
    store = [pltpu.make_async_copy(held.at[p], result_out.at[p], sem.at[4 + k]) for k, p in enumerate(parts)]
    for copy in fetch:
        copy.start()
    skip[0:16] = red[48:64, 64:96]
    skip[16:32] = red[48:64, 96:128]
    bias[...] = red[112:113, 64:96]
    for l in range(3):
        row = 64 * l
        fin[l] = red[row : row + 32, 0:64]
        fout[l] = red[row : row + 32, 64:128]
        modes[l, 0] = red[row + 32 : row + 48, 0:64]
        modes[l, 1] = red[row + 32 : row + 48, 64:128]
        modes[l, 2] = red[row + 48 : row + 64, 0:64]
    for a, b in zip(fetch, store):
        a.wait()
        b.start()
    for copy in store:
        copy.wait()


def solution(mesh):
    sizes = tuple(mesh.shape[name] for name in ("gx", "gy", "gz"))
    ngx, ngy, ngz = sizes
    group = ngx * ngz
    size = PAY // ngy
    any_spec = pl.BlockSpec(memory_space=pl.ANY)
    vmem_spec = pl.BlockSpec(memory_space=pltpu.VMEM)
    scratch = [pltpu.VMEM(table_shape(n), BF) for n in NAMES] + [
        pltpu.VMEM((576, 768), F32),
        pltpu.VMEM((576, 768), F32),
        pltpu.VMEM((576, 768), F32),
        pltpu.VMEM((1152, 768), BF),
        pltpu.VMEM((4, 4, 40, 640), F32),
        pltpu.VMEM((3, 3, 40, 512), F32),
        pltpu.VMEM((1280, 640), BF),
        pltpu.VMEM((736, 512), BF),
        pltpu.VMEM((3, 256, 512), BF),
        pltpu.VMEM((3, 256, 512), BF),
        pltpu.VMEM((3, 256, 1024), F32),
        pltpu.VMEM((3, 256, 1024), BF),
        pltpu.VMEM((3, 256, 1024), BF),
        pltpu.VMEM((3, 256, 512), BF),
        pltpu.VMEM((3, 256, 512), BF),
        pltpu.VMEM((256, 768), BF),
        pltpu.VMEM((256, 768), BF),
        pltpu.VMEM((512, 768), BF),
        pltpu.VMEM((1024, 384), BF),
        pltpu.VMEM((576, 768), F32),
        pltpu.VMEM((1152, 768), BF),
        pltpu.VMEM((3, 256, 512), BF),
        pltpu.VMEM((3, 256, 512), BF),
        pltpu.VMEM((144, 384), BF),
        pltpu.VMEM((144, 384), BF),
        pltpu.VMEM((6, 288, 128), F32),
        pltpu.VMEM((6, 288, 128), F32),
        pltpu.VMEM((512, 384), BF),
        pltpu.VMEM((512, 384), BF),
        pltpu.VMEM((3, 256, 128), F32),
        pltpu.VMEM((3, 8, 1024), F32),
        pltpu.VMEM((3, 16, 128), F32),
        pltpu.VMEM((3, 16, 128), F32),
        pltpu.VMEM((3, 384, 256), BF),
        pltpu.VMEM((3, 512, 256), BF),
        pltpu.VMEM((3, 384, 256), BF),
        pltpu.VMEM((256, 256), BF),
        pltpu.VMEM((8, 128), F32),
        pltpu.VMEM((32, 128), F32),
        pltpu.VMEM((8, 128), F32),
        pltpu.VMEM((PAY, 128), F32),
        pltpu.VMEM((ngy, size, 128), F32),
        pltpu.VMEM((group, size, 128), F32),
        pltpu.VMEM((size, 128), F32),
        pltpu.VMEM((PAY, 128), F32),
        pltpu.VMEM((2, 40, 128), F32),
        pltpu.VMEM((2, 40, 128), F32),
        pltpu.VMEM((256, 512), BF),
        pltpu.VMEM((256, 512), BF),
        pltpu.SemaphoreType.DMA((len(NAMES),)),
        pltpu.SemaphoreType.DMA((3,)),
        pltpu.SemaphoreType.DMA((27,)),
        pltpu.SemaphoreType.DMA((27,)),
        pltpu.SemaphoreType.DMA((2 * ngy + group,)),
        pltpu.SemaphoreType.DMA((2 * ngy + group,)),
    ]

    def per_device(features, cotangent, skip_weight, bias_vector, mode_factors, in_factors, out_factors):
        tables = [jnp.asarray(TABLES[n]) for n in NAMES]
        result, red = pl.pallas_call(
            lambda *refs: layer_kernel(sizes, *refs),
            name="layer",
            out_shape=(jax.ShapeDtypeStruct((576, 768), F32), jax.ShapeDtypeStruct((PAY, 128), F32)),
            in_specs=[any_spec] * 2 + [vmem_spec] * 5 + [any_spec] * len(NAMES),
            out_specs=(any_spec, vmem_spec),
            scratch_shapes=scratch,
            compiler_params=pltpu.CompilerParams(
                collective_id=0, has_side_effects=True, vmem_limit_bytes=60 * 1024 * 1024
            ),
            cost_estimate=pl.CostEstimate(flops=32 * 10**9, bytes_accessed=20 * 10**6, transcendentals=442368),
        )(
            features.reshape(576, 768),
            cotangent.reshape(576, 768),
            skip_weight,
            bias_vector.reshape(1, CH),
            mode_factors,
            in_factors,
            jnp.swapaxes(out_factors, 1, 2),
            *tables,
        )
        outs = pl.pallas_call(
            unpack_kernel,
            name="unpack",
            out_shape=(
                jax.ShapeDtypeStruct((576, 768), F32),
                jax.ShapeDtypeStruct((CH, CH), F32),
                jax.ShapeDtypeStruct((1, CH), F32),
                jax.ShapeDtypeStruct((3, 3, MD, RK), F32),
                jax.ShapeDtypeStruct((3, CH, RK), F32),
                jax.ShapeDtypeStruct((3, CH, RK), F32),
            ),
            in_specs=[any_spec, vmem_spec],
            out_specs=(any_spec,) + (vmem_spec,) * 5,
            scratch_shapes=[pltpu.VMEM((576, 768), F32), pltpu.SemaphoreType.DMA((8,))],
        )(result, red)
        return (outs[0].reshape(NP, NP, NP * CH), outs[1], outs[2].reshape(CH), outs[3], outs[4], jnp.swapaxes(outs[5], 1, 2))

    placed = (P("gx", "gy", "gz"), P("gx", "gy", "gz"), P(), P(), P(), P(), P())
    return jax.shard_map(
        per_device,
        mesh=mesh,
        in_specs=placed,
        out_specs=(P("gx", "gy", "gz"), P(), P(), P(), P(), P()),
        check_vma=False,
    )
```

```python
import math

import jax
import jax.numpy as jnp
import ml_dtypes
import numpy as np
from jax import lax
from jax.experimental import pallas as pl
from jax.experimental.pallas import tpu as pltpu
from jax.sharding import PartitionSpec as P

MESH = pl.DeviceIdType.MESH
BF = jnp.bfloat16
F32 = jnp.float32
CH, RK, MD, NP = 32, 64, 16, 24
NN = (((1,), (0,)), ((), ()))
NT = (((1,), (1,)), ((), ()))
TN = (((0,), (0,)), ((), ()))
PAY = 192


def basis(length):
    rows = np.arange(MD)
    freq = np.where(rows < MD // 2, rows, rows - MD // 2 + 1).astype(np.float64)
    phase = 2.0 * math.pi / length * freq[:, None] * np.arange(length)[None, :]
    wave = np.where((rows < MD // 2)[:, None], np.cos(phase), np.sin(phase))
    return wave * math.sqrt(2.0 / length)


def halves(x):
    x = np.asarray(x, np.float32)
    hi = x.astype(ml_dtypes.bfloat16)
    lo = (x - hi.astype(np.float32)).astype(ml_dtypes.bfloat16)
    return hi, lo


def left(x):
    hi, lo = halves(x)
    return np.concatenate([hi, hi, lo], axis=1)


def right(x):
    hi, lo = halves(x)
    return np.concatenate([hi, lo], axis=0)


def exact(x, times, axis):
    x = np.asarray(x, np.float32).astype(ml_dtypes.bfloat16)
    return np.concatenate([x] * times, axis=axis)


def channel_eye(b):
    return np.kron(b, np.eye(CH))


def make_tables():
    b24, b18 = basis(24), basis(18)
    pool = np.zeros((208, 12, 24))
    for j in range(2):
        for i in range(2):
            for r in range(36):
                x, y = i * 6 + r // 6, 2 * (j * 6 + r % 6)
                pool[(j * 2 + i) * 40 + r, x, y : y + 2] = 1 / 8
    for r in range(36):
        x, y = 2 * (r // 6), 4 * (r % 6)
        pool[160 + r, x : x + 2, y : y + 4] = 1 / 64
    pool = pool.reshape(208, 288)
    pair = channel_eye(np.kron(np.eye(4), np.ones((2, 1))))
    quad = np.zeros((24, 8))
    for z in range(24):
        quad[z, z // 4] = 1
    quad = channel_eye(quad)
    xy0 = np.kron(b24, b24)
    at4, at3 = (1, 2, 0, 3), (1, 0, 2)
    xy1 = np.zeros((256, 4, 4, 40))
    for j in range(4):
        for i in range(4):
            for r in range(36):
                xy1[:, j, i, r] = np.kron(b24[:, at4[i] * 6 + r // 6], b24[:, at4[j] * 6 + r % 6])
    xy2 = np.zeros((256, 368))
    for j in range(3):
        for i in range(3):
            for r in range(36):
                xy2[:, (j * 3 + i) * 40 + r] = np.kron(
                    b18[:, at3[i] * 6 + r // 6], b18[:, at3[j] * 6 + r % 6]
                )
    z0 = channel_eye(b24.T)
    z1s, z2s = [], []
    for gz in range(2):
        z1 = np.zeros((20, 16))
        z1[0:12] = b24[:, 6:18].T
        if gz == 0:
            z1[12:18] = b24[:, 18:24].T
        else:
            z1[12:16] = b24[:, 2:6].T
            z1[16:18] = b24[:, 0:2].T
        z1s.append(right(channel_eye(z1)))
        z2 = np.zeros((16, 16))
        z2[0:6] = b18[:, 6:12].T
        z2[8:14] = b18[:, 12:18].T if gz == 0 else b18[:, 0:6].T
        z2s.append(right(channel_eye(z2)))
    z1c = channel_eye(b24[:, 6:18])
    z2c = channel_eye(np.repeat(b18[:, 6:12], 2, axis=1))
    c1 = b24[:, 6:18]
    c2 = np.repeat(b18[:, 6:12], 2, axis=1)
    xy12 = np.concatenate([np.kron(c1, c1), np.kron(c2, c2)], axis=0)
    return {
        "pool": exact(pool, 2, 1),
        "pair": exact(pair, 2, 0),
        "quad": exact(quad, 2, 0),
        "unpair": exact(pair.T, 2, 0),
        "xy0": left(xy0),
        "z0": right(z0),
        "z0t": right(z0.T),
        "inv": left(xy0.T),
        "xy1": left(xy1.reshape(256, 640)),
        "z1": np.concatenate(z1s, axis=0),
        "xy2": left(xy2),
        "z2": np.concatenate(z2s, axis=0),
        "z1c": right(z1c),
        "z2c": right(z2c),
        "xy12": left(xy12.T),
        "xy12t": left(xy12),
        "z2ct": right(z2c.T),
    }


TABLES = make_tables()
NAMES = list(TABLES)


def table_shape(name):
    rows, cols = TABLES[name].shape
    return (rows // 2 if name in ("z1", "z2") else rows), cols


def dot(a, b, dims=NN):
    return lax.dot_general(a, b, dims, preferred_element_type=F32)


def split(x):
    hi = x.astype(BF)
    return hi, (x - hi.astype(F32)).astype(BF)


def rows_cat(*parts):
    return jnp.concatenate(parts, axis=0)


def lanes_cat(*parts):
    return jnp.concatenate(parts, axis=1)


def iota(shape, dim):
    return lax.broadcasted_iota(jnp.int32, shape, dim)


def fold_lanes(x):
    total = x[:, 0:128]
    for k in range(1, x.shape[1] // 128):
        total = total + x[:, 128 * k : 128 * (k + 1)]
    return total + pltpu.roll(total, 64, 1)


def layer_kernel(sizes, *refs):
    ngx, ngy, ngz = sizes
    refs = list(refs)
    take = lambda n: [refs.pop(0) for _ in range(n)]
    feat_hbm, cot_hbm = take(2)
    weights_hbm = take(5)
    hbm = dict(zip(NAMES, take(len(NAMES))))
    result_hbm, red_hbm = take(2)
    tab = dict(zip(NAMES, take(len(NAMES))))
    (feat, cot, result, fs, half, quart, hs, qs, kh, kl, pr, rh, rl, qh, ql, th, tl, bs, t12, pre, gs, gqh, gql, ghh, ghl,
     wide, down, g12h, g12l, um, m2r, m0t, m1t, inw, outw, outt, skw, biast, gskip, gbias, pay, ra, rb, acc, red, zsend, zrecv, qth, qtl, fst, kt,
     skip_ref, bias_ref, modes_ref, in_ref, out_ref) = take(56)
    table_sem, local_sem, halo_send, halo_recv, red_send, red_recv = take(6)

    gx, gy, gz = lax.axis_index("gx"), lax.axis_index("gy"), lax.axis_index("gz")
    me = gx * ngz + gz
    group = ngx * ngz

    load_f = pltpu.make_async_copy(feat_hbm, feat, local_sem.at[0])
    load_f.start()
    load_c = pltpu.make_async_copy(cot_hbm, cot, local_sem.at[1])
    loads = {}
    for k, name in enumerate(NAMES):
        rows = table_shape(name)[0]
        src = hbm[name].at[pl.ds(pl.multiple_of(gz * rows, 16), rows)] if name in ("z1", "z2") else hbm[name]
        loads[name] = pltpu.make_async_copy(src, tab[name], table_sem.at[k])
        if k < 3:
            loads[name].start()
    load_w = [
        pltpu.make_async_copy(src, dst, local_sem.at[3 + k])
        for k, (src, dst) in enumerate(zip(weights_hbm, (skip_ref, bias_ref, modes_ref, in_ref, out_ref)))
    ]
    for c in load_w:
        c.start()

    barrier = pltpu.get_barrier_semaphore()

    def greet_row(k, carry):
        pl.semaphore_signal(
            barrier, inc=1, device_id=(gx, lax.rem(gy + k, ngy), gz), device_id_type=MESH
        )
        return carry

    lax.fori_loop(1, ngy, greet_row, 0)

    def greet_plane(k, carry):
        q = lax.rem(me + k, group)
        pl.semaphore_signal(
            barrier, inc=1, device_id=(q // ngz, gy, lax.rem(q, ngz)), device_id_type=MESH
        )
        return carry

    lax.fori_loop(1, group, greet_plane, 0)

    def clear(j, i):
        half[j, i] = jnp.zeros((40, 640), F32)

    def clear_quarter(j, i):
        quart[j, i] = jnp.zeros((40, 512), F32)

    for edge, block in ((gx == 0, 2), (gx == ngx - 1, 3)):

        @pl.when(edge)
        def _():
            clear(0, block)
            clear(1, block)
            clear_quarter(0, block - 1)

    for edge, block in ((gy == 0, 2), (gy == ngy - 1, 3)):

        @pl.when(edge)
        def _():
            for i in range(4):
                clear(block, i)
            for i in range(3):
                clear_quarter(block - 1, i)

    load_f.wait()
    for name in NAMES[3:]:
        loads[name].start()
        if name == "xy2":
            load_c.start()
    cells = feat[...].reshape(12, 2, 24, 768)
    hi, lo = split((cells[:, 0] + cells[:, 1]).reshape(288, 768))
    gs[0:288] = hi
    gs[288:576] = lo
    loads["pool"].wait()
    for n in range(3):
        pre[0:208, 256 * n : 256 * (n + 1)] = dot(tab["pool"][...], gs[0:576, 256 * n : 256 * (n + 1)])
    hi, lo = split(pre[0:208])
    loads["pair"].wait()
    for n in range(3):
        cols = slice(256 * n, 256 * (n + 1))
        cells = dot(lanes_cat(hi[0:160, cols], lo[0:160, cols]), tab["pair"][...])
        for j in range(2):
            for i in range(2):
                r = (j * 2 + i) * 40
                half[j, i, :, 128 * n : 128 * (n + 1)] = cells[r : r + 40]
    loads["quad"].wait()
    cells = dot(lanes_cat(hi[160:208], lo[160:208]), tab["quad"][...])
    quart[0, 0, :, 0:256] = cells[0:40]
    for i in range(2):
        a, b = half[0, i, :, 128:256], half[1, i, :, 128:256]
        a = jnp.where(gz == 1, a, pltpu.roll(a, 64, 1))
        b = jnp.where(gz == 1, pltpu.roll(b, 64, 1), b)
        zsend[i] = jnp.where(iota((40, 128), 1) < 64, a, b)

    pl.semaphore_wait(barrier, ngy - 1 + group - 1)

    def remote(k, src, dst, to):
        return pltpu.make_async_remote_copy(
            src_ref=src,
            dst_ref=dst,
            send_sem=halo_send.at[k],
            recv_sem=halo_recv.at[k],
            device_id=to,
            device_id_type=MESH,
        )

    first = pl.multiple_of(256 * (1 - gz), 128)
    own, far, qown, qfar = pl.ds(0, 384), pl.ds(384, 256), pl.ds(0, 256), pl.ds(256, 256)
    mid, side = pl.ds(0, 2), pl.ds(2, 2)
    qside = pl.ds(1, 2)
    across = (gx, gy, 1 - gz)
    z_all = [
        remote(0, half.at[mid, mid, :, pl.ds(first, 128)], half.at[mid, mid, :, pl.ds(384, 128)], across),
        remote(1, zsend, zrecv, across),
        remote(2, quart.at[0, 0, :, qown], quart.at[0, 0, :, qfar], across),
    ]

    def x_copies(k, src, dst, to):
        return [
            remote(k, half.at[mid, src, :, own], half.at[mid, dst, :, own], to),
            remote(k + 1, quart.at[0, 0, :, qown], quart.at[0, dst - 1, :, qown], to),
            remote(k + 2, half.at[mid, src, :, far], half.at[mid, dst, :, far], to),
            remote(k + 3, quart.at[0, 0, :, qfar], quart.at[0, dst - 1, :, qfar], to),
        ]

    def y_copies(k, src, dst, to):
        return [
            remote(k, half.at[src, mid, :, own], half.at[dst, mid, :, own], to),
            remote(k + 1, quart.at[0, 0, :, qown], quart.at[dst - 1, 0, :, qown], to),
            remote(k + 2, half.at[src, side, :, own], half.at[dst, side, :, own], to),
            remote(k + 3, quart.at[0, qside, :, qown], quart.at[dst - 1, qside, :, qown], to),
            remote(k + 4, half.at[src, mid, :, far], half.at[dst, mid, :, far], to),
            remote(k + 5, quart.at[0, 0, :, qfar], quart.at[dst - 1, 0, :, qfar], to),
            remote(k + 6, half.at[src, side, :, far], half.at[dst, side, :, far], to),
            remote(k + 7, quart.at[0, qside, :, qfar], quart.at[dst - 1, qside, :, qfar], to),
        ]

    xs = x_copies(3, 1, 2, (gx + 1, gy, gz)), x_copies(7, 0, 3, (gx - 1, gy, gz))
    ys = y_copies(11, 1, 2, (gx, gy + 1, gz)), y_copies(19, 0, 3, (gx, gy - 1, gz))

    def each(copies, which, to_up, to_down, act):
        @pl.when(to_up)
        def _():
            for k in which:
                act(copies[0][k])

        @pl.when(to_down)
        def _():
            for k in which:
                act(copies[1][k])

    has_ux, has_dx, has_uy, has_dy = gx < ngx - 1, gx > 0, gy < ngy - 1, gy > 0
    start = lambda c: c.start()
    recv = lambda c: c.wait_recv()
    sent = lambda c: c.wait_send()

    for c in z_all:
        c.start()
    each(xs, (0, 1), has_ux, has_dx, start)
    each(ys, (0, 1), has_uy, has_dy, start)

    for c in load_w:
        c.wait()

    def dup64(x):
        eye = (iota((64, 128), 0) == iota((64, 128), 1) % 64).astype(BF)
        return dot(x, eye)

    def dup32(x):
        eye = (iota((32, 128), 0) == iota((32, 128), 1) % 32).astype(BF)
        return dot(x, eye)

    diag_ir = iota((128, 256), 0) // 32 == iota((128, 256), 1) // 64
    diag_ro = iota((256, 128), 0) // 64 == iota((256, 128), 1) // 32
    diag_io = iota((128, 128), 0) // 32 == iota((128, 128), 1) // 32
    eye64 = (iota((64, 64), 0) == iota((64, 64), 1)).astype(BF)

    b0, b1 = split(jnp.broadcast_to(bias_ref[...], (16, 32)))
    biast[...] = (dup32(b0) + dup32(b1))[0:8]
    w0, w1 = [jnp.where(diag_io, rows_cat(*[dup32(w)] * 4), 0.0).astype(BF) for w in split(skip_ref[...])]
    w0 = lanes_cat(w0, w1)
    skw[...] = rows_cat(w0, w0)

    def spread(l, carry):
        i0, i1 = split(in_ref[l])
        o0, o1 = split(out_ref[l])

        def wide(w):
            t = dup64(w)
            return jnp.where(diag_ir, rows_cat(*[lanes_cat(t, t)] * 4), 0.0).astype(BF)

        def tall(w):
            t = dup32(dot(eye64, w, NT).astype(BF))
            return jnp.where(diag_ro, rows_cat(*[t] * 4), 0.0).astype(BF)

        w0 = wide(i0)
        inw[l] = rows_cat(w0, w0, wide(i1))
        w0 = wide(o0)
        outt[l] = rows_cat(w0, w0, wide(o1))
        w0 = lanes_cat(tall(o0), tall(o1))
        outw[l] = rows_cat(w0, w0)
        dup = []
        for d in range(3):
            m = modes_ref[l, d]
            hi, lo = split(m)
            rest = (m - hi.astype(F32) - lo.astype(F32)).astype(BF)
            dup.append(dup64(hi) + dup64(lo) + dup64(rest))
        m0t[l] = dup[0]
        m1t[l] = dup[1]
        um[l] = (dup[0][:, None, :] * dup[1][None, :, :]).reshape(256, 128)
        line = lanes_cat(*[dup[2]] * 8)
        line = jnp.where(iota((16, 1024), 0) == iota((16, 1024), 1) // 64, line, 0.0)
        m2r[l] = jnp.broadcast_to(jnp.sum(line, axis=0, keepdims=True), (8, 1024))
        return carry

    lax.fori_loop(0, 3, spread, 0)

    hi, lo = split(feat[...])
    fs[0:576] = hi
    fs[576:1152] = lo

    def stacked(ref):
        parts = [slice(128 * n, 128 * (n + 1)) for n in range(6)]
        return rows_cat(*[lanes_cat(ref[0:576, c], ref[576:1152, c]) for c in parts])

    def xy_transform(table, hi_lo, rows, chunks, wide):
        for n in range(chunks):
            cols = slice(wide * n, wide * (n + 1))
            data = rows_cat(hi_lo[0 : 2 * rows, cols], hi_lo[0:rows, cols])
            hi, lo = split(dot(table[...], data))
            th[:, cols] = hi
            tl[:, cols] = lo

    def z_transform(hi, lo, table, depth, into_h, into_l, l, parts=None):
        a = lanes_cat(hi, lo, hi)
        zh, zl = (0, depth) if parts is None else parts
        for n in range(2):
            cols = slice(256 * n, 256 * (n + 1))
            tz = rows_cat(table[zh : zh + depth, cols], table[zh : zh + depth, cols], table[zl : zl + depth, cols])
            vh, vl = split(dot(a, tz))
            into_h[l, :, cols] = vh
            into_l[l, :, cols] = vl

    quads = [(slice(128 * c, 128 * (c + 1)), slice(256 * c, 256 * (c + 1))) for c in range(4)]

    def modes_forward(l):
        data = [(kh[l, :, c], kl[l, :, c]) for c, _ in quads]
        kt[l] = jnp.transpose(rows_cat(*[lanes_cat(a, b) for a, b in data]))
        p = dot(rows_cat(*[lanes_cat(a, b, a) for a, b in data]), inw[l])
        u = um[l]
        u = lanes_cat(u, u)
        data = []
        for k, (_, cols) in enumerate(quads):
            pk = p[256 * k : 256 * (k + 1)]
            pr[l, :, cols] = pk
            a, b = split(pk * u * m2r[l, 0:1, cols])
            rh[l, :, cols] = a
            rl[l, :, cols] = b
            data.append(lanes_cat(a, b))
        q = dot(rows_cat(*data), outw[l])
        q = q[:, 0:128] + q[:, 128:256]
        for k, (cols, _) in enumerate(quads):
            a, b = split(q[256 * k : 256 * (k + 1)])
            qh[l, :, cols] = a
            ql[l, :, cols] = b

    v = stacked(fs)
    fst[...] = jnp.transpose(v)
    v = dot(v, skw[...])
    v = v[:, 0:128] + v[:, 128:256] + biast[0:1]
    for n in range(6):
        pre[:, 128 * n : 128 * (n + 1)] = v[576 * n : 576 * (n + 1)]
    loads["xy0"].wait()
    xy_transform(tab["xy0"], fs, 576, 3, 256)

    each(xs, (0, 1), has_dx, has_ux, recv)
    each(ys, (2, 3), has_uy, has_dy, start)

    loads["z0"].wait()
    z_transform(th[...], tl[...], tab["z0"], 768, kh, kl, 0)

    for c in z_all:
        c.wait_recv()
    low = iota((40, 128), 1) < 64
    for i in range(2):
        a = zrecv[i]
        half[0, i, :, 512:640] = jnp.where(low, a, 0.0)
        half[1, i, :, 512:640] = jnp.where(low, pltpu.roll(a, 64, 1), 0.0)
    each(xs, (2, 3), has_ux, has_dx, start)
    each(ys, (4, 5), has_uy, has_dy, start)

    modes_forward(0)
    loads["z0t"].wait()
    a = lanes_cat(qh[0], ql[0], qh[0])
    for n in range(3):
        cols = slice(256 * n, 256 * (n + 1))
        tz = rows_cat(tab["z0t"][0:512, cols], tab["z0t"][0:512, cols], tab["z0t"][512:1024, cols])
        hi, lo = split(dot(a, tz))
        bs[0:256, cols] = hi
        bs[256:512, cols] = lo
    each(xs, (2, 3), has_dx, has_ux, recv)
    each(ys, (6, 7), has_uy, has_dy, start)
    loads["inv"].wait()
    for n in range(3):
        cols = slice(256 * n, 256 * (n + 1))
        pre[:, cols] = pre[:, cols] + dot(tab["inv"][...], rows_cat(bs[0:512, cols], bs[0:256, cols]))

    def halves_of(cols, qcols):
        for j in range(4):
            hi, lo = split(half[j, :, :, cols].reshape(160, -1))
            hs[160 * j : 160 * (j + 1), cols] = hi
            hs[640 + 160 * j : 640 + 160 * (j + 1), cols] = lo
        cells = quart[:, :, :, qcols].reshape(360, 256)
        hi, lo = split(rows_cat(cells, jnp.zeros((8, 256), F32)))
        qs[0:368, qcols] = hi
        qs[368:736, qcols] = lo

    def one_chunk(table, data, rows, cols, into_h, into_l):
        v = rows_cat(data[0 : 2 * rows, cols], data[0:rows, cols])
        hi, lo = split(dot(table[...], v))
        into_h[:, cols] = hi
        into_l[:, cols] = lo

    each(ys, (0, 1, 2, 3), has_dy, has_uy, recv)
    halves_of(slice(0, 384), slice(0, 256))
    loads["xy1"].wait()
    loads["xy2"].wait()
    one_chunk(tab["xy1"], hs, 640, slice(0, 256), th, tl)
    v = lanes_cat(hs[0:640, 256:384], hs[640:1280, 256:384])
    v = dot(tab["xy1"][:, 640:1920], rows_cat(v, v))
    hi, lo = split(v[:, 0:128] + v[:, 128:256])
    th[:, 256:384] = hi
    tl[:, 256:384] = lo
    one_chunk(tab["xy2"], qs, 368, slice(0, 256), qth, qtl)

    each(ys, (4, 5, 6, 7), has_dy, has_uy, recv)
    halves_of(slice(384, 640), slice(256, 512))
    one_chunk(tab["xy1"], hs, 640, slice(384, 640), th, tl)
    one_chunk(tab["xy2"], qs, 368, slice(256, 512), qth, qtl)
    loads["z1"].wait()
    z_transform(th[:, 0:640], tl[:, 0:640], tab["z1"], 640, kh, kl, 1)
    loads["z2"].wait()
    z_transform(qth[...], qtl[...], tab["z2"], 512, kh, kl, 2)
    lax.fori_loop(1, 3, lambda l, c: (modes_forward(l), c)[1], 0)

    loads["z1c"].wait()
    loads["z2c"].wait()
    for l, name in ((1, "z1c"), (2, "z2c")):
        tz = tab[name]
        v = dot(lanes_cat(qh[l], ql[l], qh[l]), rows_cat(tz[0:512], tz[0:512], tz[512:1024]))
        hi, lo = split(v)
        t12[256 * (l - 1) : 256 * l] = hi
        t12[512 + 256 * (l - 1) : 512 + 256 * l] = lo
    loads["xy12"].wait()
    loads["unpair"].wait()
    s = dot(tab["xy12"][...], rows_cat(t12[...], t12[0:512]))
    for n in range(3):
        hi, lo = split(s[:, 128 * n : 128 * (n + 1)])
        v = dot(lanes_cat(hi, lo), tab["unpair"][...])
        for k in range(2):
            for step in range(2):
                wide[2 * n + k, pl.ds(step, 144, stride=2), :] = v[:, 128 * k : 128 * (k + 1)]

    load_c.wait()
    scale = 1.0 / math.sqrt(ngx * ngy * ngz * NP**3)
    c0 = math.sqrt(2.0 / math.pi)
    store = pltpu.make_async_copy(result, result_hbm, local_sem.at[2])

    def activate(m, carry):
        rows = pl.ds(pl.multiple_of(m * 48, 48), 48)
        v = lanes_cat(*[wide[n, pl.ds(pl.multiple_of(m * 24, 24), 24), :] for n in range(6)])
        x = pre[rows, :] + rows_cat(v, v)
        x2 = x * x
        t = jnp.tanh(c0 * (x * (1.0 + 0.044715 * x2)))
        half_t = 0.5 * (1.0 + t)
        result[rows, :] = x * half_t
        slope = half_t + 0.5 * x * (1.0 - t * t) * (c0 * (1.0 + (3 * 0.044715) * x2))
        g = cot[rows, :] * scale * slope
        hi, lo = split(g)
        gs[rows, :] = hi
        gs[pl.ds(pl.multiple_of(576 + m * 48, 48), 48), :] = lo
        g2 = g[0:24] + g[24:48]
        for n in range(6):
            down[n, pl.ds(pl.multiple_of(m * 24, 24), 24), :] = g2[:, 128 * n : 128 * (n + 1)]
        return carry + jnp.sum(g.reshape(6, 8, 768), axis=0)

    colsum = lax.fori_loop(0, 12, activate, jnp.zeros((8, 768), F32))
    store.start()
    gbias[...] = fold_lanes(colsum)

    xy_transform(tab["xy0"], gs, 576, 3, 256)
    z_transform(th[...], tl[...], tab["z0"], 768, gqh, gql, 0)
    for n in range(3):
        v = [down[2 * n + k, pl.ds(0, 144, stride=2), :] + down[2 * n + k, pl.ds(1, 144, stride=2), :] for k in range(2)]
        hi, lo = split(lanes_cat(*v))
        hi, lo = split(dot(lanes_cat(hi, lo), tab["pair"][...]))
        ghh[:, 128 * n : 128 * (n + 1)] = hi
        ghl[:, 128 * n : 128 * (n + 1)] = lo
    loads["xy12t"].wait()
    hi, lo = split(dot(tab["xy12t"][...], rows_cat(ghh[...], ghl[...], ghh[...])))
    g12h[...] = hi
    g12l[...] = lo
    loads["z2ct"].wait()
    z_transform(g12h[0:256], g12l[0:256], tab["z1"], 384, gqh, gql, 1, (0, 640))
    z_transform(g12h[256:512], g12l[256:512], tab["z2ct"], 384, gqh, gql, 2)

    total = dot(fst[...], stacked(gs))
    total = total[0:128] + total[128:256]
    total = jnp.where(diag_io, total[:, 0:128] + total[:, 128:256], 0.0)
    s = total[0:32] + total[32:64] + total[64:96] + total[96:128]
    s = s + pltpu.roll(s, 64, 1)
    gskip[...] = s + pltpu.roll(s, 32, 1)

    def gram(at, bh, bl):
        g = dot(at, rows_cat(*[lanes_cat(bh[:, c], bl[:, c]) for _, c in quads]))
        g = g[0:128] + g[128:256]
        g = jnp.where(diag_ir, g[:, 0:256] + g[:, 256:512], 0.0)
        return fold_lanes(g[0:32] + g[32:64] + g[64:96] + g[96:128])

    low = iota((32, 128), 1) < 64

    def modes_backward(l, carry):
        u = um[l]
        u = lanes_cat(u, u)
        e = jnp.zeros((256, 128), F32)
        g2 = []
        data = [(gqh[l, :, c], gql[l, :, c]) for c, _ in quads]
        g_out = gram(jnp.transpose(rows_cat(*[lanes_cat(a, b) for a, b in data])), rh.at[l], rl.at[l])
        g = dot(rows_cat(*[lanes_cat(a, b, a) for a, b in data]), outt[l])
        for k, (_, cols) in enumerate(quads):
            gr = g[256 * k : 256 * (k + 1)]
            d = gr * pr[l, :, cols]
            m2 = m2r[l, 0:1, cols]
            dm = d * m2
            e = e + dm[:, 0:128] + dm[:, 128:256]
            g2.append(jnp.sum((d * u).reshape(32, 8, 256), axis=0))
            hi, lo = split(gr * (u * m2))
            rh[l, :, cols] = hi
            rl[l, :, cols] = lo
        g_in = gram(kt[l], rh.at[l], rl.at[l])
        e = (e + pltpu.roll(e, 64, 1)).reshape(16, 16, 128)
        g0 = jnp.sum(e * m1t[l][None, :, :], axis=1)
        g1 = jnp.sum(e * m0t[l][:, None, :], axis=0)
        g2 = jnp.sum(lanes_cat(*g2), axis=0, keepdims=True)
        g2 = jnp.where(iota((16, 1024), 0) == iota((16, 1024), 1) // 64, g2, 0.0)
        g2 = fold_lanes(g2)
        row = pl.multiple_of(l * 64, 64)
        pay[pl.ds(row, 32), :] = jnp.where(low, g_in, g_out)
        pay[pl.ds(row + 32, 16), :] = jnp.where(low[0:16], g0, g1)
        pay[pl.ds(row + 48, 16), :] = jnp.where(low[0:16], g2, 0.0)
        return carry

    lax.fori_loop(0, 3, modes_backward, 0)
    s = gskip[...]
    s = jnp.where(iota((16, 128), 1) < 96, s[0:16], s[16:32])
    pay[48:64] = jnp.where(low[0:16], pay[48:64], s)
    b = gbias[...] + pltpu.roll(gbias[...], 32, 1)
    b = jnp.broadcast_to(jnp.sum(b, axis=0, keepdims=True), (16, 128))
    pay[112:128] = jnp.where(low[0:16], pay[112:128], b)

    size = PAY // ngy

    def pushes(count, make, act):
        def body(k, carry):
            act(make(k))
            return carry

        lax.fori_loop(1, count, body, 0)

    def scatter(k):
        t = lax.rem(gy + k, ngy)
        return pltpu.make_async_remote_copy(
            src_ref=pay.at[pl.ds(pl.multiple_of(t * size, 8), size)],
            dst_ref=ra.at[k],
            send_sem=red_send.at[k],
            recv_sem=red_recv.at[k],
            device_id=(gx, t, gz),
            device_id_type=MESH,
        )

    def exchange(k):
        q = lax.rem(me + k, group)
        return pltpu.make_async_remote_copy(
            src_ref=acc,
            dst_ref=rb.at[me],
            send_sem=red_send.at[ngy + k],
            recv_sem=red_recv.at[ngy + k],
            device_id=(q // ngz, gy, lax.rem(q, ngz)),
            device_id_type=MESH,
        )

    mine = pl.ds(pl.multiple_of(gy * size, 8), size)

    def gather(k):
        t = lax.rem(gy + k, ngy)
        return pltpu.make_async_remote_copy(
            src_ref=red.at[mine],
            dst_ref=red.at[mine],
            send_sem=red_send.at[ngy + group + k],
            recv_sem=red_recv.at[ngy + group + k],
            device_id=(gx, t, gz),
            device_id_type=MESH,
        )

    pushes(ngy, scatter, start)
    pushes(ngy, scatter, recv)
    total = pay[mine]
    for k in range(1, ngy):
        total = total + ra[k]
    acc[...] = total
    rb[me] = total
    pushes(group, exchange, start)
    pushes(group, exchange, recv)
    total = rb[0]
    for k in range(1, group):
        total = total + rb[k]
    red[mine] = total
    pushes(ngy, gather, start)
    pushes(ngy, gather, recv)
    store_red = pltpu.make_async_copy(red, red_hbm, local_sem.at[8])
    store_red.start()

    pushes(ngy, scatter, sent)
    pushes(group, exchange, sent)
    pushes(ngy, gather, sent)
    for c in z_all:
        c.wait_send()
    each(xs, range(4), has_ux, has_dx, sent)
    each(ys, range(8), has_uy, has_dy, sent)
    store.wait()
    store_red.wait()


def unpack_kernel(result_in, red_in, result_out, *refs):
    outs, (red, held), bufs, sem = refs[0:5], refs[5:7], refs[7:12], refs[12]
    skip, bias, modes, fin, fout = bufs
    parts = [pl.ds(96 * k, 96) for k in range(6)]
    fetch_red = pltpu.make_async_copy(red_in, red, sem.at[17])
    fetch_red.start()
    fetch = [pltpu.make_async_copy(result_in.at[p], held.at[p], sem.at[k]) for k, p in enumerate(parts)]
    store = [pltpu.make_async_copy(held.at[p], result_out.at[p], sem.at[6 + k]) for k, p in enumerate(parts)]
    small = [pltpu.make_async_copy(b, o, sem.at[12 + k]) for k, (b, o) in enumerate(zip(bufs, outs))]
    for copy in fetch:
        copy.start()
    fetch_red.wait()
    skip[0:16] = red[48:64, 64:96]
    skip[16:32] = red[48:64, 96:128]
    bias[...] = red[112:113, 64:96]
    for l in range(3):
        row = 64 * l
        fin[l] = red[row : row + 32, 0:64]
        fout[l] = red[row : row + 32, 64:128]
        modes[l, 0] = red[row + 32 : row + 48, 0:64]
        modes[l, 1] = red[row + 32 : row + 48, 64:128]
        modes[l, 2] = red[row + 48 : row + 64, 0:64]
    for copy in small:
        copy.start()
    for a, b in zip(fetch, store):
        a.wait()
        b.start()
    for copy in store + small:
        copy.wait()


def solution(mesh):
    sizes = tuple(mesh.shape[name] for name in ("gx", "gy", "gz"))
    ngx, ngy, ngz = sizes
    group = ngx * ngz
    size = PAY // ngy
    any_spec = pl.BlockSpec(memory_space=pl.ANY)
    scratch = [pltpu.VMEM(table_shape(n), BF) for n in NAMES] + [
        pltpu.VMEM((576, 768), F32),
        pltpu.VMEM((576, 768), F32),
        pltpu.VMEM((576, 768), F32),
        pltpu.VMEM((1152, 768), BF),
        pltpu.VMEM((4, 4, 40, 640), F32),
        pltpu.VMEM((3, 3, 40, 512), F32),
        pltpu.VMEM((1280, 640), BF),
        pltpu.VMEM((736, 512), BF),
        pltpu.VMEM((3, 256, 512), BF),
        pltpu.VMEM((3, 256, 512), BF),
        pltpu.VMEM((3, 256, 1024), F32),
        pltpu.VMEM((3, 256, 1024), BF),
        pltpu.VMEM((3, 256, 1024), BF),
        pltpu.VMEM((3, 256, 512), BF),
        pltpu.VMEM((3, 256, 512), BF),
        pltpu.VMEM((256, 768), BF),
        pltpu.VMEM((256, 768), BF),
        pltpu.VMEM((512, 768), BF),
        pltpu.VMEM((1024, 384), BF),
        pltpu.VMEM((576, 768), F32),
        pltpu.VMEM((1152, 768), BF),
        pltpu.VMEM((3, 256, 512), BF),
        pltpu.VMEM((3, 256, 512), BF),
        pltpu.VMEM((144, 384), BF),
        pltpu.VMEM((144, 384), BF),
        pltpu.VMEM((6, 288, 128), F32),
        pltpu.VMEM((6, 288, 128), F32),
        pltpu.VMEM((512, 384), BF),
        pltpu.VMEM((512, 384), BF),
        pltpu.VMEM((3, 256, 128), F32),
        pltpu.VMEM((3, 8, 1024), F32),
        pltpu.VMEM((3, 16, 128), F32),
        pltpu.VMEM((3, 16, 128), F32),
        pltpu.VMEM((3, 384, 256), BF),
        pltpu.VMEM((3, 512, 256), BF),
        pltpu.VMEM((3, 384, 256), BF),
        pltpu.VMEM((256, 256), BF),
        pltpu.VMEM((8, 128), F32),
        pltpu.VMEM((32, 128), F32),
        pltpu.VMEM((8, 128), F32),
        pltpu.VMEM((PAY, 128), F32),
        pltpu.VMEM((ngy, size, 128), F32),
        pltpu.VMEM((group, size, 128), F32),
        pltpu.VMEM((size, 128), F32),
        pltpu.VMEM((PAY, 128), F32),
        pltpu.VMEM((2, 40, 128), F32),
        pltpu.VMEM((2, 40, 128), F32),
        pltpu.VMEM((256, 512), BF),
        pltpu.VMEM((256, 512), BF),
        pltpu.VMEM((256, 3456), BF),
        pltpu.VMEM((3, 256, 1024), BF),
        pltpu.VMEM((CH, CH), F32),
        pltpu.VMEM((1, CH), F32),
        pltpu.VMEM((3, 3, MD, RK), F32),
        pltpu.VMEM((3, CH, RK), F32),
        pltpu.VMEM((3, CH, RK), F32),
        pltpu.SemaphoreType.DMA((len(NAMES),)),
        pltpu.SemaphoreType.DMA((9,)),
        pltpu.SemaphoreType.DMA((27,)),
        pltpu.SemaphoreType.DMA((27,)),
        pltpu.SemaphoreType.DMA((2 * ngy + group,)),
        pltpu.SemaphoreType.DMA((2 * ngy + group,)),
    ]

    def per_device(features, cotangent, skip_weight, bias_vector, mode_factors, in_factors, out_factors):
        tables = [jnp.asarray(TABLES[n]) for n in NAMES]
        result, red = pl.pallas_call(
            lambda *refs: layer_kernel(sizes, *refs),
            name="layer",
            out_shape=(jax.ShapeDtypeStruct((576, 768), F32), jax.ShapeDtypeStruct((PAY, 128), F32)),
            in_specs=[any_spec] * (7 + len(NAMES)),
            out_specs=(any_spec, any_spec),
            scratch_shapes=scratch,
            compiler_params=pltpu.CompilerParams(
                collective_id=0, has_side_effects=True, vmem_limit_bytes=60 * 1024 * 1024
            ),
            cost_estimate=pl.CostEstimate(flops=32 * 10**9, bytes_accessed=20 * 10**6, transcendentals=442368),
        )(
            features.reshape(576, 768),
            cotangent.reshape(576, 768),
            skip_weight,
            bias_vector.reshape(1, CH),
            mode_factors,
            in_factors,
            jnp.swapaxes(out_factors, 1, 2),
            *tables,
        )
        outs = pl.pallas_call(
            unpack_kernel,
            name="unpack",
            out_shape=(
                jax.ShapeDtypeStruct((576, 768), F32),
                jax.ShapeDtypeStruct((CH, CH), F32),
                jax.ShapeDtypeStruct((1, CH), F32),
                jax.ShapeDtypeStruct((3, 3, MD, RK), F32),
                jax.ShapeDtypeStruct((3, CH, RK), F32),
                jax.ShapeDtypeStruct((3, CH, RK), F32),
            ),
            in_specs=[any_spec] * 2,
            out_specs=(any_spec,) * 6,
            scratch_shapes=[
                pltpu.VMEM((PAY, 128), F32),
                pltpu.VMEM((576, 768), F32),
                pltpu.VMEM((CH, CH), F32),
                pltpu.VMEM((1, CH), F32),
                pltpu.VMEM((3, 3, MD, RK), F32),
                pltpu.VMEM((3, CH, RK), F32),
                pltpu.VMEM((3, CH, RK), F32),
                pltpu.SemaphoreType.DMA((18,)),
            ],
        )(result, red)
        return (outs[0].reshape(NP, NP, NP * CH), outs[1], outs[2].reshape(CH), outs[3], outs[4], jnp.swapaxes(outs[5], 1, 2))

    placed = (P("gx", "gy", "gz"), P("gx", "gy", "gz"), P(), P(), P(), P(), P())
    return jax.shard_map(
        per_device,
        mesh=mesh,
        in_specs=placed,
        out_specs=(P("gx", "gy", "gz"), P(), P(), P(), P(), P()),
        check_vma=False,
    )
```

```python
import math

import jax
import jax.numpy as jnp
import ml_dtypes
import numpy as np
from jax import lax
from jax.experimental import pallas as pl
from jax.experimental.pallas import tpu as pltpu
from jax.sharding import PartitionSpec as P

MESH = pl.DeviceIdType.MESH
BF = jnp.bfloat16
F32 = jnp.float32
CH, RK, MD, NP = 32, 64, 16, 24
NN = (((1,), (0,)), ((), ()))
NT = (((1,), (1,)), ((), ()))
TN = (((0,), (0,)), ((), ()))
PAY = 192


def basis(length):
    rows = np.arange(MD)
    freq = np.where(rows < MD // 2, rows, rows - MD // 2 + 1).astype(np.float64)
    phase = 2.0 * math.pi / length * freq[:, None] * np.arange(length)[None, :]
    wave = np.where((rows < MD // 2)[:, None], np.cos(phase), np.sin(phase))
    return wave * math.sqrt(2.0 / length)


def halves(x):
    x = np.asarray(x, np.float32)
    hi = x.astype(ml_dtypes.bfloat16)
    lo = (x - hi.astype(np.float32)).astype(ml_dtypes.bfloat16)
    return hi, lo


def left(x):
    hi, lo = halves(x)
    return np.concatenate([hi, hi, lo], axis=1)


def right(x):
    hi, lo = halves(x)
    return np.concatenate([hi, lo], axis=0)


def exact(x, times, axis):
    x = np.asarray(x, np.float32).astype(ml_dtypes.bfloat16)
    return np.concatenate([x] * times, axis=axis)


def channel_eye(b):
    return np.kron(b, np.eye(CH))


def make_tables():
    b24, b18 = basis(24), basis(18)
    pool = np.zeros((208, 12, 24))
    for j in range(2):
        for i in range(2):
            for r in range(36):
                x, y = i * 6 + r // 6, 2 * (j * 6 + r % 6)
                pool[(j * 2 + i) * 40 + r, x, y : y + 2] = 1 / 8
    for r in range(36):
        x, y = 2 * (r // 6), 4 * (r % 6)
        pool[160 + r, x : x + 2, y : y + 4] = 1 / 64
    pool = pool.reshape(208, 288)
    pair = channel_eye(np.kron(np.eye(4), np.ones((2, 1))))
    quad = np.zeros((24, 8))
    for z in range(24):
        quad[z, z // 4] = 1
    quad = channel_eye(quad)
    xy0 = np.kron(b24, b24)
    at4, at3 = (1, 2, 0, 3), (1, 0, 2)
    xy1 = np.zeros((256, 4, 4, 40))
    for j in range(4):
        for i in range(4):
            for r in range(36):
                xy1[:, j, i, r] = np.kron(b24[:, at4[i] * 6 + r // 6], b24[:, at4[j] * 6 + r % 6])
    xy2 = np.zeros((256, 368))
    for j in range(3):
        for i in range(3):
            for r in range(36):
                xy2[:, (j * 3 + i) * 40 + r] = np.kron(
                    b18[:, at3[i] * 6 + r // 6], b18[:, at3[j] * 6 + r % 6]
                )
    z0 = channel_eye(b24.T)
    z1s, z2s = [], []
    for gz in range(2):
        z1 = np.zeros((20, 16))
        z1[0:12] = b24[:, 6:18].T
        if gz == 0:
            z1[12:18] = b24[:, 18:24].T
        else:
            z1[12:16] = b24[:, 2:6].T
            z1[16:18] = b24[:, 0:2].T
        z1s.append(right(channel_eye(z1)))
        z2 = np.zeros((16, 16))
        z2[0:6] = b18[:, 6:12].T
        z2[8:14] = b18[:, 12:18].T if gz == 0 else b18[:, 0:6].T
        z2s.append(right(channel_eye(z2)))
    z1c = channel_eye(b24[:, 6:18])
    z2c = channel_eye(np.repeat(b18[:, 6:12], 2, axis=1))
    c1 = b24[:, 6:18]
    c2 = np.repeat(b18[:, 6:12], 2, axis=1)
    xy12 = np.concatenate([np.kron(c1, c1), np.kron(c2, c2)], axis=0)
    return {
        "pool": exact(pool, 2, 1),
        "pair": exact(pair, 2, 0),
        "quad": exact(quad, 2, 0),
        "unpair": exact(pair.T, 2, 0),
        "xy0": left(xy0),
        "z0": right(z0),
        "z0t": right(z0.T),
        "inv": left(xy0.T),
        "xy1": left(xy1.reshape(256, 640)),
        "z1": np.concatenate(z1s, axis=0),
        "xy2": left(xy2),
        "z2": np.concatenate(z2s, axis=0),
        "z1c": right(z1c),
        "z2c": right(z2c),
        "xy12": left(xy12.T),
        "xy12t": left(xy12),
        "z2ct": right(z2c.T),
    }


TABLES = make_tables()
NAMES = list(TABLES)


def table_shape(name):
    rows, cols = TABLES[name].shape
    return (rows // 2 if name in ("z1", "z2") else rows), cols


def dot(a, b, dims=NN):
    return lax.dot_general(a, b, dims, preferred_element_type=F32)


def split(x):
    hi = x.astype(BF)
    return hi, (x - hi.astype(F32)).astype(BF)


def rows_cat(*parts):
    return jnp.concatenate(parts, axis=0)


def lanes_cat(*parts):
    return jnp.concatenate(parts, axis=1)


def iota(shape, dim):
    return lax.broadcasted_iota(jnp.int32, shape, dim)


def fold_lanes(x):
    total = x[:, 0:128]
    for k in range(1, x.shape[1] // 128):
        total = total + x[:, 128 * k : 128 * (k + 1)]
    return total + pltpu.roll(total, 64, 1)


def layer_kernel(sizes, *refs):
    ngx, ngy, ngz = sizes
    refs = list(refs)
    take = lambda n: [refs.pop(0) for _ in range(n)]
    feat_hbm, cot_hbm = take(2)
    weights_hbm = take(5)
    hbm = dict(zip(NAMES, take(len(NAMES))))
    result_hbm, red_hbm = take(2)
    tab = dict(zip(NAMES, take(len(NAMES))))
    (feat, cot, result, fs, half, quart, hs, qs, kh, kl, pr, rh, rl, qh, ql, th, tl, bs, t12, pre, gs, gqh, gql, ghh, ghl,
     wide, down, g12h, g12l, um, m2r, m0t, m1t, inw, outw, outt, skw, biast, gskip, gbias, pay, ra, rb, acc, red, zsend, zrecv, qth, qtl, fst, kt, kown,
     skip_ref, bias_ref, modes_ref, in_ref, out_ref) = take(57)
    table_sem, local_sem, halo_send, halo_recv, red_send, red_recv = take(6)

    gx, gy, gz = lax.axis_index("gx"), lax.axis_index("gy"), lax.axis_index("gz")
    me = gx * ngz + gz
    group = ngx * ngz

    load_f = pltpu.make_async_copy(feat_hbm, feat, local_sem.at[0])
    load_f.start()
    load_c = pltpu.make_async_copy(cot_hbm, cot, local_sem.at[1])
    loads = {}
    for k, name in enumerate(NAMES):
        rows = table_shape(name)[0]
        src = hbm[name].at[pl.ds(pl.multiple_of(gz * rows, 16), rows)] if name in ("z1", "z2") else hbm[name]
        loads[name] = pltpu.make_async_copy(src, tab[name], table_sem.at[k])
        if k < 3:
            loads[name].start()
    load_w = [
        pltpu.make_async_copy(src, dst, local_sem.at[3 + k])
        for k, (src, dst) in enumerate(zip(weights_hbm, (skip_ref, bias_ref, modes_ref, in_ref, out_ref)))
    ]
    for c in load_w:
        c.start()

    barrier = pltpu.get_barrier_semaphore()

    def greet_row(k, carry):
        pl.semaphore_signal(
            barrier, inc=1, device_id=(gx, lax.rem(gy + k, ngy), gz), device_id_type=MESH
        )
        return carry

    lax.fori_loop(1, ngy, greet_row, 0)

    def greet_plane(k, carry):
        q = lax.rem(me + k, group)
        pl.semaphore_signal(
            barrier, inc=1, device_id=(q // ngz, gy, lax.rem(q, ngz)), device_id_type=MESH
        )
        return carry

    lax.fori_loop(1, group, greet_plane, 0)

    def clear(j, i):
        half[j, i] = jnp.zeros((40, 640), F32)

    def clear_quarter(j, i):
        quart[j, i] = jnp.zeros((40, 512), F32)

    for edge, block in ((gx == 0, 2), (gx == ngx - 1, 3)):

        @pl.when(edge)
        def _():
            clear(0, block)
            clear(1, block)
            clear_quarter(0, block - 1)

    for edge, block in ((gy == 0, 2), (gy == ngy - 1, 3)):

        @pl.when(edge)
        def _():
            for i in range(4):
                clear(block, i)
            for i in range(3):
                clear_quarter(block - 1, i)

    load_f.wait()
    for name in NAMES[3:]:
        loads[name].start()
        if name == "xy2":
            load_c.start()
    cells = feat[...].reshape(12, 2, 24, 768)
    hi, lo = split((cells[:, 0] + cells[:, 1]).reshape(288, 768))
    gs[0:288] = hi
    gs[288:576] = lo
    loads["pool"].wait()
    for n in range(3):
        pre[0:208, 256 * n : 256 * (n + 1)] = dot(tab["pool"][...], gs[0:576, 256 * n : 256 * (n + 1)])
    hi, lo = split(pre[0:208])
    loads["pair"].wait()
    for n in range(3):
        cols = slice(256 * n, 256 * (n + 1))
        cells = dot(lanes_cat(hi[0:160, cols], lo[0:160, cols]), tab["pair"][...])
        for j in range(2):
            for i in range(2):
                r = (j * 2 + i) * 40
                half[j, i, :, 128 * n : 128 * (n + 1)] = cells[r : r + 40]
    loads["quad"].wait()
    cells = dot(lanes_cat(hi[160:208], lo[160:208]), tab["quad"][...])
    quart[0, 0, :, 0:256] = cells[0:40]
    for i in range(2):
        a, b = half[0, i, :, 128:256], half[1, i, :, 128:256]
        a = jnp.where(gz == 1, a, pltpu.roll(a, 64, 1))
        b = jnp.where(gz == 1, pltpu.roll(b, 64, 1), b)
        zsend[i] = jnp.where(iota((40, 128), 1) < 64, a, b)

    pl.semaphore_wait(barrier, ngy - 1 + group - 1)

    def remote(k, src, dst, to):
        return pltpu.make_async_remote_copy(
            src_ref=src,
            dst_ref=dst,
            send_sem=halo_send.at[k],
            recv_sem=halo_recv.at[k],
            device_id=to,
            device_id_type=MESH,
        )

    first = pl.multiple_of(256 * (1 - gz), 128)
    own, far, qown, qfar = pl.ds(0, 384), pl.ds(384, 256), pl.ds(0, 256), pl.ds(256, 256)
    mid, side = pl.ds(0, 2), pl.ds(2, 2)
    qside = pl.ds(1, 2)
    across = (gx, gy, 1 - gz)
    z_all = [
        remote(0, half.at[mid, mid, :, pl.ds(first, 128)], half.at[mid, mid, :, pl.ds(384, 128)], across),
        remote(1, zsend, zrecv, across),
        remote(2, quart.at[0, 0, :, qown], quart.at[0, 0, :, qfar], across),
    ]

    def x_copies(k, src, dst, to):
        return [
            remote(k, half.at[mid, src, :, own], half.at[mid, dst, :, own], to),
            remote(k + 1, quart.at[0, 0, :, qown], quart.at[0, dst - 1, :, qown], to),
            remote(k + 2, half.at[mid, src, :, far], half.at[mid, dst, :, far], to),
            remote(k + 3, quart.at[0, 0, :, qfar], quart.at[0, dst - 1, :, qfar], to),
        ]

    def y_copies(k, src, dst, to):
        return [
            remote(k, half.at[src, mid, :, own], half.at[dst, mid, :, own], to),
            remote(k + 1, quart.at[0, 0, :, qown], quart.at[dst - 1, 0, :, qown], to),
            remote(k + 2, half.at[src, side, :, own], half.at[dst, side, :, own], to),
            remote(k + 3, quart.at[0, qside, :, qown], quart.at[dst - 1, qside, :, qown], to),
            remote(k + 4, half.at[src, mid, :, far], half.at[dst, mid, :, far], to),
            remote(k + 5, quart.at[0, 0, :, qfar], quart.at[dst - 1, 0, :, qfar], to),
            remote(k + 6, half.at[src, side, :, far], half.at[dst, side, :, far], to),
            remote(k + 7, quart.at[0, qside, :, qfar], quart.at[dst - 1, qside, :, qfar], to),
        ]

    xs = x_copies(3, 1, 2, (gx + 1, gy, gz)), x_copies(7, 0, 3, (gx - 1, gy, gz))
    ys = y_copies(11, 1, 2, (gx, gy + 1, gz)), y_copies(19, 0, 3, (gx, gy - 1, gz))

    def each(copies, which, to_up, to_down, act):
        @pl.when(to_up)
        def _():
            for k in which:
                act(copies[0][k])

        @pl.when(to_down)
        def _():
            for k in which:
                act(copies[1][k])

    has_ux, has_dx, has_uy, has_dy = gx < ngx - 1, gx > 0, gy < ngy - 1, gy > 0
    start = lambda c: c.start()
    recv = lambda c: c.wait_recv()
    sent = lambda c: c.wait_send()

    for c in z_all:
        c.start()
    each(xs, (0, 1), has_ux, has_dx, start)
    each(ys, (0, 1), has_uy, has_dy, start)

    for c in load_w:
        c.wait()

    def dup64(x):
        eye = (iota((64, 128), 0) == iota((64, 128), 1) % 64).astype(BF)
        return dot(x, eye)

    def dup32(x):
        eye = (iota((32, 128), 0) == iota((32, 128), 1) % 32).astype(BF)
        return dot(x, eye)

    diag_ir = iota((128, 256), 0) // 32 == iota((128, 256), 1) // 64
    diag_ro = iota((256, 128), 0) // 64 == iota((256, 128), 1) // 32
    diag_io = iota((128, 128), 0) // 32 == iota((128, 128), 1) // 32
    eye64 = (iota((64, 64), 0) == iota((64, 64), 1)).astype(BF)

    b0, b1 = split(jnp.broadcast_to(bias_ref[...], (16, 32)))
    biast[...] = (dup32(b0) + dup32(b1))[0:8]
    w0, w1 = [jnp.where(diag_io, rows_cat(*[dup32(w)] * 4), 0.0).astype(BF) for w in split(skip_ref[...])]
    w0 = lanes_cat(w0, w1)
    skw[...] = rows_cat(w0, w0)

    def spread(l, carry):
        i0, i1 = split(in_ref[l])
        o0, o1 = split(out_ref[l])

        def wide(w):
            t = dup64(w)
            return jnp.where(diag_ir, rows_cat(*[lanes_cat(t, t)] * 4), 0.0).astype(BF)

        def tall(w):
            t = dup32(dot(eye64, w, NT).astype(BF))
            return jnp.where(diag_ro, rows_cat(*[t] * 4), 0.0).astype(BF)

        w0 = wide(i0)
        inw[l] = rows_cat(w0, w0, wide(i1))
        w0 = wide(o0)
        outt[l] = rows_cat(w0, w0, wide(o1))
        w0 = lanes_cat(tall(o0), tall(o1))
        outw[l] = rows_cat(w0, w0)
        dup = []
        for d in range(3):
            m = modes_ref[l, d]
            hi, lo = split(m)
            rest = (m - hi.astype(F32) - lo.astype(F32)).astype(BF)
            dup.append(dup64(hi) + dup64(lo) + dup64(rest))
        m0t[l] = dup[0]
        m1t[l] = dup[1]
        um[l] = (dup[0][:, None, :] * dup[1][None, :, :]).reshape(256, 128)
        line = lanes_cat(*[dup[2]] * 8)
        line = jnp.where(iota((16, 1024), 0) == iota((16, 1024), 1) // 64, line, 0.0)
        m2r[l] = jnp.broadcast_to(jnp.sum(line, axis=0, keepdims=True), (8, 1024))
        return carry

    lax.fori_loop(0, 3, spread, 0)

    hi, lo = split(feat[...])
    fs[0:576] = hi
    fs[576:1152] = lo

    def stacked(ref):
        parts = [slice(128 * n, 128 * (n + 1)) for n in range(6)]
        return rows_cat(*[lanes_cat(ref[0:576, c], ref[576:1152, c]) for c in parts])

    def xy_transform(table, hi_lo, rows, chunks, wide):
        for n in range(chunks):
            cols = slice(wide * n, wide * (n + 1))
            data = rows_cat(hi_lo[0 : 2 * rows, cols], hi_lo[0:rows, cols])
            hi, lo = split(dot(table[...], data))
            th[:, cols] = hi
            tl[:, cols] = lo

    def z_transform(hi, lo, table, depth, into_h, into_l, l, parts=None):
        a = lanes_cat(hi, lo, hi)
        zh, zl = (0, depth) if parts is None else parts
        for n in range(2):
            cols = slice(256 * n, 256 * (n + 1))
            tz = rows_cat(table[zh : zh + depth, cols], table[zh : zh + depth, cols], table[zl : zl + depth, cols])
            vh, vl = split(dot(a, tz))
            into_h[l, :, cols] = vh
            into_l[l, :, cols] = vl

    quads = [(slice(128 * c, 128 * (c + 1)), slice(256 * c, 256 * (c + 1))) for c in range(4)]

    def modes_forward(l):
        data = [(kh[l, :, c], kl[l, :, c]) for c, _ in quads]
        kt[l] = jnp.transpose(rows_cat(*[lanes_cat(a, b) for a, b in data]))
        p = dot(rows_cat(*[lanes_cat(a, b, a) for a, b in data]), inw[l])
        u = um[l]
        u = lanes_cat(u, u)
        data = []
        for k, (_, cols) in enumerate(quads):
            pk = p[256 * k : 256 * (k + 1)]
            pr[l, :, cols] = pk
            a, b = split(pk * u * m2r[l, 0:1, cols])
            rh[l, :, cols] = a
            rl[l, :, cols] = b
            data.append(lanes_cat(a, b))
        q = dot(rows_cat(*data), outw[l])
        q = q[:, 0:128] + q[:, 128:256]
        for k, (cols, _) in enumerate(quads):
            a, b = split(q[256 * k : 256 * (k + 1)])
            qh[l, :, cols] = a
            ql[l, :, cols] = b

    v = stacked(fs)
    fst[...] = jnp.transpose(v)
    v = dot(v, skw[...])
    v = v[:, 0:128] + v[:, 128:256] + biast[0:1]
    for n in range(6):
        pre[:, 128 * n : 128 * (n + 1)] = v[576 * n : 576 * (n + 1)]
    loads["xy0"].wait()
    xy_transform(tab["xy0"], fs, 576, 3, 256)

    each(xs, (0, 1), has_dx, has_ux, recv)
    each(ys, (2, 3), has_uy, has_dy, start)

    loads["z0"].wait()
    z_transform(th[...], tl[...], tab["z0"], 768, kh, kl, 0)

    for c in z_all:
        c.wait_recv()
    low = iota((40, 128), 1) < 64
    for i in range(2):
        a = zrecv[i]
        half[0, i, :, 512:640] = jnp.where(low, a, 0.0)
        half[1, i, :, 512:640] = jnp.where(low, pltpu.roll(a, 64, 1), 0.0)
    each(xs, (2, 3), has_ux, has_dx, start)
    each(ys, (4, 5), has_uy, has_dy, start)

    modes_forward(0)
    loads["z0t"].wait()
    a = lanes_cat(qh[0], ql[0], qh[0])
    for n in range(3):
        cols = slice(256 * n, 256 * (n + 1))
        tz = rows_cat(tab["z0t"][0:512, cols], tab["z0t"][0:512, cols], tab["z0t"][512:1024, cols])
        hi, lo = split(dot(a, tz))
        bs[0:256, cols] = hi
        bs[256:512, cols] = lo
    each(xs, (2, 3), has_dx, has_ux, recv)
    each(ys, (6, 7), has_uy, has_dy, start)
    loads["inv"].wait()
    for n in range(3):
        cols = slice(256 * n, 256 * (n + 1))
        pre[:, cols] = pre[:, cols] + dot(tab["inv"][...], rows_cat(bs[0:512, cols], bs[0:256, cols]))

    def halves_of(cols, qcols):
        for j in range(4):
            hi, lo = split(half[j, :, :, cols].reshape(160, -1))
            hs[160 * j : 160 * (j + 1), cols] = hi
            hs[640 + 160 * j : 640 + 160 * (j + 1), cols] = lo
        cells = quart[:, :, :, qcols].reshape(360, 256)
        hi, lo = split(rows_cat(cells, jnp.zeros((8, 256), F32)))
        qs[0:368, qcols] = hi
        qs[368:736, qcols] = lo

    def one_chunk(table, data, rows, cols, into_h, into_l):
        v = rows_cat(data[0 : 2 * rows, cols], data[0:rows, cols])
        hi, lo = split(dot(table[...], v))
        into_h[:, cols] = hi
        into_l[:, cols] = lo

    each(ys, (0, 1, 2, 3), has_dy, has_uy, recv)
    halves_of(slice(0, 384), slice(0, 256))
    loads["xy1"].wait()
    loads["xy2"].wait()
    one_chunk(tab["xy1"], hs, 640, slice(0, 256), th, tl)
    v = lanes_cat(hs[0:640, 256:384], hs[640:1280, 256:384])
    v = dot(tab["xy1"][:, 640:1920], rows_cat(v, v))
    hi, lo = split(v[:, 0:128] + v[:, 128:256])
    th[:, 256:384] = hi
    tl[:, 256:384] = lo
    one_chunk(tab["xy2"], qs, 368, slice(0, 256), qth, qtl)

    def z_product(hi, lo, table, first, rows, depth):
        tz = table[first : first + depth]
        return dot(lanes_cat(hi, lo, hi), rows_cat(tz, tz, table[rows + first : rows + first + depth]))

    loads["z1"].wait()
    loads["z2"].wait()
    kown[0] = z_product(th[:, 0:384], tl[:, 0:384], tab["z1"], 0, 640, 384)
    kown[1] = z_product(qth[:, 0:256], qtl[:, 0:256], tab["z2"], 0, 512, 256)

    each(ys, (4, 5, 6, 7), has_dy, has_uy, recv)
    halves_of(slice(384, 640), slice(256, 512))
    one_chunk(tab["xy1"], hs, 640, slice(384, 640), th, tl)
    one_chunk(tab["xy2"], qs, 368, slice(256, 512), qth, qtl)
    hi, lo = split(kown[0] + z_product(th[:, 384:640], tl[:, 384:640], tab["z1"], 384, 640, 256))
    kh[1] = hi
    kl[1] = lo
    hi, lo = split(kown[1] + z_product(qth[:, 256:512], qtl[:, 256:512], tab["z2"], 256, 512, 256))
    kh[2] = hi
    kl[2] = lo
    for l in (1, 2):
        modes_forward(l)

    loads["z1c"].wait()
    loads["z2c"].wait()
    for l, name in ((1, "z1c"), (2, "z2c")):
        tz = tab[name]
        v = dot(lanes_cat(qh[l], ql[l], qh[l]), rows_cat(tz[0:512], tz[0:512], tz[512:1024]))
        hi, lo = split(v)
        t12[256 * (l - 1) : 256 * l] = hi
        t12[512 + 256 * (l - 1) : 512 + 256 * l] = lo
    loads["xy12"].wait()
    loads["unpair"].wait()
    s = dot(tab["xy12"][...], rows_cat(t12[...], t12[0:512]))
    for n in range(3):
        hi, lo = split(s[:, 128 * n : 128 * (n + 1)])
        v = dot(lanes_cat(hi, lo), tab["unpair"][...])
        for k in range(2):
            for step in range(2):
                wide[2 * n + k, pl.ds(step, 144, stride=2), :] = v[:, 128 * k : 128 * (k + 1)]

    load_c.wait()
    scale = 1.0 / math.sqrt(ngx * ngy * ngz * NP**3)
    c0 = math.sqrt(2.0 / math.pi)
    store = pltpu.make_async_copy(result, result_hbm, local_sem.at[2])

    def activate(m, carry):
        rows = pl.ds(pl.multiple_of(m * 48, 48), 48)
        v = lanes_cat(*[wide[n, pl.ds(pl.multiple_of(m * 24, 24), 24), :] for n in range(6)])
        x = pre[rows, :] + rows_cat(v, v)
        x2 = x * x
        t = jnp.tanh(c0 * (x * (1.0 + 0.044715 * x2)))
        half_t = 0.5 * (1.0 + t)
        result[rows, :] = x * half_t
        slope = half_t + 0.5 * x * (1.0 - t * t) * (c0 * (1.0 + (3 * 0.044715) * x2))
        g = cot[rows, :] * scale * slope
        hi, lo = split(g)
        gs[rows, :] = hi
        gs[pl.ds(pl.multiple_of(576 + m * 48, 48), 48), :] = lo
        g2 = g[0:24] + g[24:48]
        for n in range(6):
            down[n, pl.ds(pl.multiple_of(m * 24, 24), 24), :] = g2[:, 128 * n : 128 * (n + 1)]
        return carry + jnp.sum(g.reshape(6, 8, 768), axis=0)

    colsum = lax.fori_loop(0, 12, activate, jnp.zeros((8, 768), F32))
    store.start()
    gbias[...] = fold_lanes(colsum)

    xy_transform(tab["xy0"], gs, 576, 3, 256)
    z_transform(th[...], tl[...], tab["z0"], 768, gqh, gql, 0)
    for n in range(3):
        v = [down[2 * n + k, pl.ds(0, 144, stride=2), :] + down[2 * n + k, pl.ds(1, 144, stride=2), :] for k in range(2)]
        hi, lo = split(lanes_cat(*v))
        hi, lo = split(dot(lanes_cat(hi, lo), tab["pair"][...]))
        ghh[:, 128 * n : 128 * (n + 1)] = hi
        ghl[:, 128 * n : 128 * (n + 1)] = lo
    loads["xy12t"].wait()
    hi, lo = split(dot(tab["xy12t"][...], rows_cat(ghh[...], ghl[...], ghh[...])))
    g12h[...] = hi
    g12l[...] = lo
    loads["z2ct"].wait()
    z_transform(g12h[0:256], g12l[0:256], tab["z1"], 384, gqh, gql, 1, (0, 640))
    z_transform(g12h[256:512], g12l[256:512], tab["z2ct"], 384, gqh, gql, 2)

    total = dot(fst[...], stacked(gs))
    total = total[0:128] + total[128:256]
    total = jnp.where(diag_io, total[:, 0:128] + total[:, 128:256], 0.0)
    s = total[0:32] + total[32:64] + total[64:96] + total[96:128]
    s = s + pltpu.roll(s, 64, 1)
    gskip[...] = s + pltpu.roll(s, 32, 1)

    def gram(at, bh, bl):
        g = dot(at, rows_cat(*[lanes_cat(bh[:, c], bl[:, c]) for _, c in quads]))
        g = g[0:128] + g[128:256]
        g = jnp.where(diag_ir, g[:, 0:256] + g[:, 256:512], 0.0)
        return fold_lanes(g[0:32] + g[32:64] + g[64:96] + g[96:128])

    low = iota((32, 128), 1) < 64

    def modes_backward(l, carry):
        u = um[l]
        u = lanes_cat(u, u)
        e = jnp.zeros((256, 128), F32)
        g2 = []
        data = [(gqh[l, :, c], gql[l, :, c]) for c, _ in quads]
        g_out = gram(jnp.transpose(rows_cat(*[lanes_cat(a, b) for a, b in data])), rh.at[l], rl.at[l])
        g = dot(rows_cat(*[lanes_cat(a, b, a) for a, b in data]), outt[l])
        for k, (_, cols) in enumerate(quads):
            gr = g[256 * k : 256 * (k + 1)]
            d = gr * pr[l, :, cols]
            m2 = m2r[l, 0:1, cols]
            dm = d * m2
            e = e + dm[:, 0:128] + dm[:, 128:256]
            g2.append(jnp.sum((d * u).reshape(32, 8, 256), axis=0))
            hi, lo = split(gr * (u * m2))
            rh[l, :, cols] = hi
            rl[l, :, cols] = lo
        g_in = gram(kt[l], rh.at[l], rl.at[l])
        e = (e + pltpu.roll(e, 64, 1)).reshape(16, 16, 128)
        g0 = jnp.sum(e * m1t[l][None, :, :], axis=1)
        g1 = jnp.sum(e * m0t[l][:, None, :], axis=0)
        g2 = jnp.sum(lanes_cat(*g2), axis=0, keepdims=True)
        g2 = jnp.where(iota((16, 1024), 0) == iota((16, 1024), 1) // 64, g2, 0.0)
        g2 = fold_lanes(g2)
        row = 64 * l
        pay[pl.ds(row, 32), :] = jnp.where(low, g_in, g_out)
        pay[pl.ds(row + 32, 16), :] = jnp.where(low[0:16], g0, g1)
        pay[pl.ds(row + 48, 16), :] = jnp.where(low[0:16], g2, 0.0)
        return carry

    for l in range(3):
        modes_backward(l, 0)
    s = gskip[...]
    s = jnp.where(iota((16, 128), 1) < 96, s[0:16], s[16:32])
    pay[48:64] = jnp.where(low[0:16], pay[48:64], s)
    b = gbias[...] + pltpu.roll(gbias[...], 32, 1)
    b = jnp.broadcast_to(jnp.sum(b, axis=0, keepdims=True), (16, 128))
    pay[112:128] = jnp.where(low[0:16], pay[112:128], b)

    size = PAY // ngy

    def pushes(count, make, act):
        def body(k, carry):
            act(make(k))
            return carry

        lax.fori_loop(1, count, body, 0)

    def scatter(k):
        t = lax.rem(gy + k, ngy)
        return pltpu.make_async_remote_copy(
            src_ref=pay.at[pl.ds(pl.multiple_of(t * size, 8), size)],
            dst_ref=ra.at[k],
            send_sem=red_send.at[k],
            recv_sem=red_recv.at[k],
            device_id=(gx, t, gz),
            device_id_type=MESH,
        )

    def exchange(k):
        q = lax.rem(me + k, group)
        return pltpu.make_async_remote_copy(
            src_ref=acc,
            dst_ref=rb.at[me],
            send_sem=red_send.at[ngy + k],
            recv_sem=red_recv.at[ngy + k],
            device_id=(q // ngz, gy, lax.rem(q, ngz)),
            device_id_type=MESH,
        )

    mine = pl.ds(pl.multiple_of(gy * size, 8), size)

    def gather(k):
        t = lax.rem(gy + k, ngy)
        return pltpu.make_async_remote_copy(
            src_ref=red.at[mine],
            dst_ref=red.at[mine],
            send_sem=red_send.at[ngy + group + k],
            recv_sem=red_recv.at[ngy + group + k],
            device_id=(gx, t, gz),
            device_id_type=MESH,
        )

    for k in range(1, ngy):
        scatter(k).start()
    pushes(ngy, scatter, recv)
    total = pay[mine]
    for k in range(1, ngy):
        total = total + ra[k]
    acc[...] = total
    rb[me] = total
    for k in range(1, group):
        exchange(k).start()
    pushes(group, exchange, recv)
    total = rb[0]
    for k in range(1, group):
        total = total + rb[k]
    red[mine] = total
    for k in range(1, ngy):
        gather(k).start()
    pushes(ngy, gather, recv)
    store_red = pltpu.make_async_copy(red, red_hbm, local_sem.at[8])
    store_red.start()

    pushes(ngy, scatter, sent)
    pushes(group, exchange, sent)
    pushes(ngy, gather, sent)
    for c in z_all:
        c.wait_send()
    each(xs, range(4), has_ux, has_dx, sent)
    each(ys, range(8), has_uy, has_dy, sent)
    store.wait()
    store_red.wait()


def unpack_kernel(result_in, red_in, result_out, *refs):
    outs, (red, held), bufs, sem = refs[0:5], refs[5:7], refs[7:12], refs[12]
    skip, bias, modes, fin, fout = bufs
    parts = [pl.ds(96 * k, 96) for k in range(6)]
    fetch_red = pltpu.make_async_copy(red_in, red, sem.at[17])
    fetch_red.start()
    fetch = [pltpu.make_async_copy(result_in.at[p], held.at[p], sem.at[k]) for k, p in enumerate(parts)]
    store = [pltpu.make_async_copy(held.at[p], result_out.at[p], sem.at[6 + k]) for k, p in enumerate(parts)]
    small = [pltpu.make_async_copy(b, o, sem.at[12 + k]) for k, (b, o) in enumerate(zip(bufs, outs))]
    for copy in fetch:
        copy.start()
    fetch_red.wait()
    skip[0:16] = red[48:64, 64:96]
    skip[16:32] = red[48:64, 96:128]
    bias[...] = red[112:113, 64:96]
    for l in range(3):
        row = 64 * l
        fin[l] = red[row : row + 32, 0:64]
        fout[l] = red[row : row + 32, 64:128]
        modes[l, 0] = red[row + 32 : row + 48, 0:64]
        modes[l, 1] = red[row + 32 : row + 48, 64:128]
        modes[l, 2] = red[row + 48 : row + 64, 0:64]
    for copy in small:
        copy.start()
    for a, b in zip(fetch, store):
        a.wait()
        b.start()
    for copy in store + small:
        copy.wait()


def solution(mesh):
    sizes = tuple(mesh.shape[name] for name in ("gx", "gy", "gz"))
    ngx, ngy, ngz = sizes
    group = ngx * ngz
    size = PAY // ngy
    any_spec = pl.BlockSpec(memory_space=pl.ANY)
    scratch = [pltpu.VMEM(table_shape(n), BF) for n in NAMES] + [
        pltpu.VMEM((576, 768), F32),
        pltpu.VMEM((576, 768), F32),
        pltpu.VMEM((576, 768), F32),
        pltpu.VMEM((1152, 768), BF),
        pltpu.VMEM((4, 4, 40, 640), F32),
        pltpu.VMEM((3, 3, 40, 512), F32),
        pltpu.VMEM((1280, 640), BF),
        pltpu.VMEM((736, 512), BF),
        pltpu.VMEM((3, 256, 512), BF),
        pltpu.VMEM((3, 256, 512), BF),
        pltpu.VMEM((3, 256, 1024), F32),
        pltpu.VMEM((3, 256, 1024), BF),
        pltpu.VMEM((3, 256, 1024), BF),
        pltpu.VMEM((3, 256, 512), BF),
        pltpu.VMEM((3, 256, 512), BF),
        pltpu.VMEM((256, 768), BF),
        pltpu.VMEM((256, 768), BF),
        pltpu.VMEM((512, 768), BF),
        pltpu.VMEM((1024, 384), BF),
        pltpu.VMEM((576, 768), F32),
        pltpu.VMEM((1152, 768), BF),
        pltpu.VMEM((3, 256, 512), BF),
        pltpu.VMEM((3, 256, 512), BF),
        pltpu.VMEM((144, 384), BF),
        pltpu.VMEM((144, 384), BF),
        pltpu.VMEM((6, 288, 128), F32),
        pltpu.VMEM((6, 288, 128), F32),
        pltpu.VMEM((512, 384), BF),
        pltpu.VMEM((512, 384), BF),
        pltpu.VMEM((3, 256, 128), F32),
        pltpu.VMEM((3, 8, 1024), F32),
        pltpu.VMEM((3, 16, 128), F32),
        pltpu.VMEM((3, 16, 128), F32),
        pltpu.VMEM((3, 384, 256), BF),
        pltpu.VMEM((3, 512, 256), BF),
        pltpu.VMEM((3, 384, 256), BF),
        pltpu.VMEM((256, 256), BF),
        pltpu.VMEM((8, 128), F32),
        pltpu.VMEM((32, 128), F32),
        pltpu.VMEM((8, 128), F32),
        pltpu.VMEM((PAY, 128), F32),
        pltpu.VMEM((ngy, size, 128), F32),
        pltpu.VMEM((group, size, 128), F32),
        pltpu.VMEM((size, 128), F32),
        pltpu.VMEM((PAY, 128), F32),
        pltpu.VMEM((2, 40, 128), F32),
        pltpu.VMEM((2, 40, 128), F32),
        pltpu.VMEM((256, 512), BF),
        pltpu.VMEM((256, 512), BF),
        pltpu.VMEM((256, 3456), BF),
        pltpu.VMEM((3, 256, 1024), BF),
        pltpu.VMEM((2, 256, 512), F32),
        pltpu.VMEM((CH, CH), F32),
        pltpu.VMEM((1, CH), F32),
        pltpu.VMEM((3, 3, MD, RK), F32),
        pltpu.VMEM((3, CH, RK), F32),
        pltpu.VMEM((3, CH, RK), F32),
        pltpu.SemaphoreType.DMA((len(NAMES),)),
        pltpu.SemaphoreType.DMA((9,)),
        pltpu.SemaphoreType.DMA((27,)),
        pltpu.SemaphoreType.DMA((27,)),
        pltpu.SemaphoreType.DMA((2 * ngy + group,)),
        pltpu.SemaphoreType.DMA((2 * ngy + group,)),
    ]

    def per_device(features, cotangent, skip_weight, bias_vector, mode_factors, in_factors, out_factors):
        tables = [jnp.asarray(TABLES[n]) for n in NAMES]
        result, red = pl.pallas_call(
            lambda *refs: layer_kernel(sizes, *refs),
            name="layer",
            out_shape=(jax.ShapeDtypeStruct((576, 768), F32), jax.ShapeDtypeStruct((PAY, 128), F32)),
            in_specs=[any_spec] * (7 + len(NAMES)),
            out_specs=(any_spec, any_spec),
            scratch_shapes=scratch,
            compiler_params=pltpu.CompilerParams(
                collective_id=0, has_side_effects=True, vmem_limit_bytes=60 * 1024 * 1024
            ),
            cost_estimate=pl.CostEstimate(flops=32 * 10**9, bytes_accessed=20 * 10**6, transcendentals=442368),
        )(
            features.reshape(576, 768),
            cotangent.reshape(576, 768),
            skip_weight,
            bias_vector.reshape(1, CH),
            mode_factors,
            in_factors,
            jnp.swapaxes(out_factors, 1, 2),
            *tables,
        )
        outs = pl.pallas_call(
            unpack_kernel,
            name="unpack",
            out_shape=(
                jax.ShapeDtypeStruct((576, 768), F32),
                jax.ShapeDtypeStruct((CH, CH), F32),
                jax.ShapeDtypeStruct((1, CH), F32),
                jax.ShapeDtypeStruct((3, 3, MD, RK), F32),
                jax.ShapeDtypeStruct((3, CH, RK), F32),
                jax.ShapeDtypeStruct((3, CH, RK), F32),
            ),
            in_specs=[any_spec] * 2,
            out_specs=(any_spec,) * 6,
            scratch_shapes=[
                pltpu.VMEM((PAY, 128), F32),
                pltpu.VMEM((576, 768), F32),
                pltpu.VMEM((CH, CH), F32),
                pltpu.VMEM((1, CH), F32),
                pltpu.VMEM((3, 3, MD, RK), F32),
                pltpu.VMEM((3, CH, RK), F32),
                pltpu.VMEM((3, CH, RK), F32),
                pltpu.SemaphoreType.DMA((18,)),
            ],
        )(result, red)
        return (outs[0].reshape(NP, NP, NP * CH), outs[1], outs[2].reshape(CH), outs[3], outs[4], jnp.swapaxes(outs[5], 1, 2))

    placed = (P("gx", "gy", "gz"), P("gx", "gy", "gz"), P(), P(), P(), P(), P())
    return jax.shard_map(
        per_device,
        mesh=mesh,
        in_specs=placed,
        out_specs=(P("gx", "gy", "gz"), P(), P(), P(), P(), P()),
        check_vma=False,
    )
```

```python
import math

import jax
import jax.numpy as jnp
import ml_dtypes
import numpy as np
from jax import lax
from jax.experimental import pallas as pl
from jax.experimental.pallas import tpu as pltpu
from jax.sharding import PartitionSpec as P

MESH = pl.DeviceIdType.MESH
BF = jnp.bfloat16
F32 = jnp.float32
CH, RK, MD, NP = 32, 64, 16, 24
NN = (((1,), (0,)), ((), ()))
NT = (((1,), (1,)), ((), ()))
TN = (((0,), (0,)), ((), ()))
PAY = 192


def basis(length):
    rows = np.arange(MD)
    freq = np.where(rows < MD // 2, rows, rows - MD // 2 + 1).astype(np.float64)
    phase = 2.0 * math.pi / length * freq[:, None] * np.arange(length)[None, :]
    wave = np.where((rows < MD // 2)[:, None], np.cos(phase), np.sin(phase))
    return wave * math.sqrt(2.0 / length)


def halves(x):
    x = np.asarray(x, np.float32)
    hi = x.astype(ml_dtypes.bfloat16)
    lo = (x - hi.astype(np.float32)).astype(ml_dtypes.bfloat16)
    return hi, lo


def left(x):
    hi, lo = halves(x)
    return np.concatenate([hi, hi, lo], axis=1)


def right(x):
    hi, lo = halves(x)
    return np.concatenate([hi, lo], axis=0)


def exact(x, times, axis):
    x = np.asarray(x, np.float32).astype(ml_dtypes.bfloat16)
    return np.concatenate([x] * times, axis=axis)


def channel_eye(b):
    return np.kron(b, np.eye(CH))


def make_tables():
    b24, b18 = basis(24), basis(18)
    pool = np.zeros((208, 12, 24))
    for j in range(2):
        for i in range(2):
            for r in range(36):
                x, y = i * 6 + r // 6, 2 * (j * 6 + r % 6)
                pool[(j * 2 + i) * 40 + r, x, y : y + 2] = 1 / 8
    for r in range(36):
        x, y = 2 * (r // 6), 4 * (r % 6)
        pool[160 + r, x : x + 2, y : y + 4] = 1 / 64
    pool = pool.reshape(208, 288)
    pair = channel_eye(np.kron(np.eye(4), np.ones((2, 1))))
    quad = np.zeros((24, 8))
    for z in range(24):
        quad[z, z // 4] = 1
    quad = channel_eye(quad)
    xy0 = np.kron(b24, b24)
    at4, at3 = (1, 2, 0, 3), (1, 0, 2)
    xy1 = np.zeros((256, 4, 4, 40))
    for j in range(4):
        for i in range(4):
            for r in range(36):
                xy1[:, j, i, r] = np.kron(b24[:, at4[i] * 6 + r // 6], b24[:, at4[j] * 6 + r % 6])
    xy2 = np.zeros((256, 368))
    for j in range(3):
        for i in range(3):
            for r in range(36):
                xy2[:, (j * 3 + i) * 40 + r] = np.kron(
                    b18[:, at3[i] * 6 + r // 6], b18[:, at3[j] * 6 + r % 6]
                )
    z0 = channel_eye(b24.T)
    z1s, z2s = [], []
    for gz in range(2):
        z1 = np.zeros((20, 16))
        z1[0:12] = b24[:, 6:18].T
        if gz == 0:
            z1[12:18] = b24[:, 18:24].T
        else:
            z1[12:16] = b24[:, 2:6].T
            z1[16:18] = b24[:, 0:2].T
        z1s.append(right(channel_eye(z1)))
        z2 = np.zeros((16, 16))
        z2[0:6] = b18[:, 6:12].T
        z2[8:14] = b18[:, 12:18].T if gz == 0 else b18[:, 0:6].T
        z2s.append(right(channel_eye(z2)))
    z1c = channel_eye(b24[:, 6:18])
    z2c = channel_eye(np.repeat(b18[:, 6:12], 2, axis=1))
    c1 = b24[:, 6:18]
    c2 = np.repeat(b18[:, 6:12], 2, axis=1)
    xy12 = np.concatenate([np.kron(c1, c1), np.kron(c2, c2)], axis=0)
    return {
        "pool": exact(pool, 2, 1),
        "pair": exact(pair, 2, 0),
        "quad": exact(quad, 2, 0),
        "unpair": exact(pair.T, 2, 0),
        "xy0": left(xy0),
        "z0": right(z0),
        "z0t": right(z0.T),
        "inv": left(xy0.T),
        "xy1": left(xy1.reshape(256, 640)),
        "z1": np.concatenate(z1s, axis=0),
        "xy2": left(xy2),
        "z2": np.concatenate(z2s, axis=0),
        "z1c": right(z1c),
        "z2c": right(z2c),
        "xy12": left(xy12.T),
        "xy12t": left(xy12),
        "z2ct": right(z2c.T),
    }


TABLES = make_tables()
NAMES = list(TABLES)


def table_shape(name):
    rows, cols = TABLES[name].shape
    return (rows // 2 if name in ("z1", "z2") else rows), cols


def dot(a, b, dims=NN):
    return lax.dot_general(a, b, dims, preferred_element_type=F32)


def split(x):
    hi = x.astype(BF)
    return hi, (x - hi.astype(F32)).astype(BF)


def rows_cat(*parts):
    return jnp.concatenate(parts, axis=0)


def lanes_cat(*parts):
    return jnp.concatenate(parts, axis=1)


def iota(shape, dim):
    return lax.broadcasted_iota(jnp.int32, shape, dim)


def fold_lanes(x):
    total = x[:, 0:128]
    for k in range(1, x.shape[1] // 128):
        total = total + x[:, 128 * k : 128 * (k + 1)]
    return total + pltpu.roll(total, 64, 1)


def layer_kernel(sizes, *refs):
    ngx, ngy, ngz = sizes
    refs = list(refs)
    take = lambda n: [refs.pop(0) for _ in range(n)]
    feat_hbm, cot_hbm = take(2)
    weights_hbm = take(5)
    hbm = dict(zip(NAMES, take(len(NAMES))))
    result_hbm, red_hbm = take(2)
    tab = dict(zip(NAMES, take(len(NAMES))))
    (feat, cot, result, fs, half, quart, hs, qs, kh, kl, pr, rh, rl, qh, ql, th, tl, bs, t12, pre, gs, gqh, gql, ghh, ghl,
     wide, down, g12h, g12l, um, m2r, m0t, m1t, inw, outw, outt, skw, biast, gskip, gbias, pay, ra, rb, acc, red, zsend, zrecv, qth, qtl, fst, kt, kown,
     skip_ref, bias_ref, modes_ref, in_ref, out_ref) = take(57)
    table_sem, local_sem, halo_send, halo_recv, red_send, red_recv = take(6)

    gx, gy, gz = lax.axis_index("gx"), lax.axis_index("gy"), lax.axis_index("gz")
    me = gx * ngz + gz
    group = ngx * ngz

    load_f = pltpu.make_async_copy(feat_hbm, feat, local_sem.at[0])
    load_f.start()
    load_c = pltpu.make_async_copy(cot_hbm, cot, local_sem.at[1])
    loads = {}
    for k, name in enumerate(NAMES):
        rows = table_shape(name)[0]
        src = hbm[name].at[pl.ds(pl.multiple_of(gz * rows, 16), rows)] if name in ("z1", "z2") else hbm[name]
        loads[name] = pltpu.make_async_copy(src, tab[name], table_sem.at[k])
        if k < 3:
            loads[name].start()
    load_w = [
        pltpu.make_async_copy(src, dst, local_sem.at[3 + k])
        for k, (src, dst) in enumerate(zip(weights_hbm, (skip_ref, bias_ref, modes_ref, in_ref, out_ref)))
    ]
    for c in load_w:
        c.start()

    barrier = pltpu.get_barrier_semaphore()

    def greet_row(k, carry):
        pl.semaphore_signal(
            barrier, inc=1, device_id=(gx, lax.rem(gy + k, ngy), gz), device_id_type=MESH
        )
        return carry

    lax.fori_loop(1, ngy, greet_row, 0)

    def greet_plane(k, carry):
        q = lax.rem(me + k, group)
        pl.semaphore_signal(
            barrier, inc=1, device_id=(q // ngz, gy, lax.rem(q, ngz)), device_id_type=MESH
        )
        return carry

    lax.fori_loop(1, group, greet_plane, 0)

    def clear(j, i):
        half[j, i] = jnp.zeros((40, 640), F32)

    def clear_quarter(j, i):
        quart[j, i] = jnp.zeros((40, 512), F32)

    for edge, block in ((gx == 0, 2), (gx == ngx - 1, 3)):

        @pl.when(edge)
        def _():
            clear(0, block)
            clear(1, block)
            clear_quarter(0, block - 1)

    for edge, block in ((gy == 0, 2), (gy == ngy - 1, 3)):

        @pl.when(edge)
        def _():
            for i in range(4):
                clear(block, i)
            for i in range(3):
                clear_quarter(block - 1, i)

    load_f.wait()
    for name in NAMES[3:]:
        loads[name].start()
        if name == "xy2":
            load_c.start()
    cells = feat[...].reshape(12, 2, 24, 768)
    hi, lo = split((cells[:, 0] + cells[:, 1]).reshape(288, 768))
    gs[0:288] = hi
    gs[288:576] = lo
    loads["pool"].wait()
    for n in range(3):
        pre[0:208, 256 * n : 256 * (n + 1)] = dot(tab["pool"][...], gs[0:576, 256 * n : 256 * (n + 1)])
    hi, lo = split(pre[0:208])
    loads["pair"].wait()
    for n in range(3):
        cols = slice(256 * n, 256 * (n + 1))
        cells = dot(lanes_cat(hi[0:160, cols], lo[0:160, cols]), tab["pair"][...])
        for j in range(2):
            for i in range(2):
                r = (j * 2 + i) * 40
                half[j, i, :, 128 * n : 128 * (n + 1)] = cells[r : r + 40]
    loads["quad"].wait()
    cells = dot(lanes_cat(hi[160:208], lo[160:208]), tab["quad"][...])
    quart[0, 0, :, 0:256] = cells[0:40]
    for i in range(2):
        a, b = half[0, i, :, 128:256], half[1, i, :, 128:256]
        a = jnp.where(gz == 1, a, pltpu.roll(a, 64, 1))
        b = jnp.where(gz == 1, pltpu.roll(b, 64, 1), b)
        zsend[i] = jnp.where(iota((40, 128), 1) < 64, a, b)

    pl.semaphore_wait(barrier, ngy - 1 + group - 1)

    def remote(k, src, dst, to):
        return pltpu.make_async_remote_copy(
            src_ref=src,
            dst_ref=dst,
            send_sem=halo_send.at[k],
            recv_sem=halo_recv.at[k],
            device_id=to,
            device_id_type=MESH,
        )

    first = pl.multiple_of(256 * (1 - gz), 128)
    own, far, qown, qfar = pl.ds(0, 384), pl.ds(384, 256), pl.ds(0, 256), pl.ds(256, 256)
    mid, side = pl.ds(0, 2), pl.ds(2, 2)
    qside = pl.ds(1, 2)
    across = (gx, gy, 1 - gz)
    z_all = [
        remote(0, half.at[mid, mid, :, pl.ds(first, 128)], half.at[mid, mid, :, pl.ds(384, 128)], across),
        remote(1, zsend, zrecv, across),
        remote(2, quart.at[0, 0, :, qown], quart.at[0, 0, :, qfar], across),
    ]

    def x_copies(k, src, dst, to):
        return [
            remote(k, half.at[mid, src, :, own], half.at[mid, dst, :, own], to),
            remote(k + 1, quart.at[0, 0, :, qown], quart.at[0, dst - 1, :, qown], to),
            remote(k + 2, half.at[mid, src, :, far], half.at[mid, dst, :, far], to),
            remote(k + 3, quart.at[0, 0, :, qfar], quart.at[0, dst - 1, :, qfar], to),
        ]

    def y_copies(k, src, dst, to):
        return [
            remote(k, half.at[src, mid, :, own], half.at[dst, mid, :, own], to),
            remote(k + 1, quart.at[0, 0, :, qown], quart.at[dst - 1, 0, :, qown], to),
            remote(k + 2, half.at[src, side, :, own], half.at[dst, side, :, own], to),
            remote(k + 3, quart.at[0, qside, :, qown], quart.at[dst - 1, qside, :, qown], to),
            remote(k + 4, half.at[src, mid, :, far], half.at[dst, mid, :, far], to),
            remote(k + 5, quart.at[0, 0, :, qfar], quart.at[dst - 1, 0, :, qfar], to),
            remote(k + 6, half.at[src, side, :, far], half.at[dst, side, :, far], to),
            remote(k + 7, quart.at[0, qside, :, qfar], quart.at[dst - 1, qside, :, qfar], to),
        ]

    xs = x_copies(3, 1, 2, (gx + 1, gy, gz)), x_copies(7, 0, 3, (gx - 1, gy, gz))
    ys = y_copies(11, 1, 2, (gx, gy + 1, gz)), y_copies(19, 0, 3, (gx, gy - 1, gz))

    def each(copies, which, to_up, to_down, act):
        @pl.when(to_up)
        def _():
            for k in which:
                act(copies[0][k])

        @pl.when(to_down)
        def _():
            for k in which:
                act(copies[1][k])

    has_ux, has_dx, has_uy, has_dy = gx < ngx - 1, gx > 0, gy < ngy - 1, gy > 0
    start = lambda c: c.start()
    recv = lambda c: c.wait_recv()
    sent = lambda c: c.wait_send()

    for c in z_all:
        c.start()
    each(xs, (0, 1), has_ux, has_dx, start)
    each(ys, (0, 1), has_uy, has_dy, start)

    for c in load_w:
        c.wait()

    def dup64(x):
        eye = (iota((64, 128), 0) == iota((64, 128), 1) % 64).astype(BF)
        return dot(x, eye)

    def dup32(x):
        eye = (iota((32, 128), 0) == iota((32, 128), 1) % 32).astype(BF)
        return dot(x, eye)

    diag_ir = iota((128, 256), 0) // 32 == iota((128, 256), 1) // 64
    diag_ro = iota((256, 128), 0) // 64 == iota((256, 128), 1) // 32
    diag_io = iota((128, 128), 0) // 32 == iota((128, 128), 1) // 32
    eye64 = (iota((64, 64), 0) == iota((64, 64), 1)).astype(BF)

    b0, b1 = split(jnp.broadcast_to(bias_ref[...], (16, 32)))
    biast[...] = (dup32(b0) + dup32(b1))[0:8]
    w0, w1 = [jnp.where(diag_io, rows_cat(*[dup32(w)] * 4), 0.0).astype(BF) for w in split(skip_ref[...])]
    w0 = lanes_cat(w0, w1)
    skw[...] = rows_cat(w0, w0)

    def spread(l, carry):
        i0, i1 = split(in_ref[l])
        o0, o1 = split(out_ref[l])

        def wide(w):
            t = dup64(w)
            return jnp.where(diag_ir, rows_cat(*[lanes_cat(t, t)] * 4), 0.0).astype(BF)

        def tall(w):
            t = dup32(dot(eye64, w, NT).astype(BF))
            return jnp.where(diag_ro, rows_cat(*[t] * 4), 0.0).astype(BF)

        w0 = wide(i0)
        inw[l] = rows_cat(w0, w0, wide(i1))
        w0 = wide(o0)
        outt[l] = rows_cat(w0, w0, wide(o1))
        w0 = lanes_cat(tall(o0), tall(o1))
        outw[l] = rows_cat(w0, w0)
        dup = []
        for d in range(3):
            m = modes_ref[l, d]
            hi, lo = split(m)
            rest = (m - hi.astype(F32) - lo.astype(F32)).astype(BF)
            dup.append(dup64(hi) + dup64(lo) + dup64(rest))
        m0t[l] = dup[0]
        m1t[l] = dup[1]
        um[l] = (dup[0][:, None, :] * dup[1][None, :, :]).reshape(256, 128)
        line = lanes_cat(*[dup[2]] * 8)
        line = jnp.where(iota((16, 1024), 0) == iota((16, 1024), 1) // 64, line, 0.0)
        m2r[l] = jnp.broadcast_to(jnp.sum(line, axis=0, keepdims=True), (8, 1024))
        return carry

    for l in range(3):
        spread(l, 0)

    hi, lo = split(feat[...])
    fs[0:576] = hi
    fs[576:1152] = lo

    def stacked(ref):
        parts = [slice(128 * n, 128 * (n + 1)) for n in range(6)]
        return rows_cat(*[lanes_cat(ref[0:576, c], ref[576:1152, c]) for c in parts])

    def xy_transform(table, hi_lo, rows, chunks, wide):
        for n in range(chunks):
            cols = slice(wide * n, wide * (n + 1))
            data = rows_cat(hi_lo[0 : 2 * rows, cols], hi_lo[0:rows, cols])
            hi, lo = split(dot(table[...], data))
            th[:, cols] = hi
            tl[:, cols] = lo

    def z_transform(hi, lo, table, depth, into_h, into_l, l, parts=None):
        a = lanes_cat(hi, lo, hi)
        zh, zl = (0, depth) if parts is None else parts
        for n in range(2):
            cols = slice(256 * n, 256 * (n + 1))
            tz = rows_cat(table[zh : zh + depth, cols], table[zh : zh + depth, cols], table[zl : zl + depth, cols])
            vh, vl = split(dot(a, tz))
            into_h[l, :, cols] = vh
            into_l[l, :, cols] = vl

    quads = [(slice(128 * c, 128 * (c + 1)), slice(256 * c, 256 * (c + 1))) for c in range(4)]

    def modes_forward(l):
        data = [(kh[l, :, c], kl[l, :, c]) for c, _ in quads]
        kt[l] = jnp.transpose(rows_cat(*[lanes_cat(a, b) for a, b in data]))
        p = dot(rows_cat(*[lanes_cat(a, b, a) for a, b in data]), inw[l])
        u = um[l]
        u = lanes_cat(u, u)
        data = []
        for k, (_, cols) in enumerate(quads):
            pk = p[256 * k : 256 * (k + 1)]
            pr[l, :, cols] = pk
            a, b = split(pk * u * m2r[l, 0:1, cols])
            rh[l, :, cols] = a
            rl[l, :, cols] = b
            data.append(lanes_cat(a, b))
        q = dot(rows_cat(*data), outw[l])
        q = q[:, 0:128] + q[:, 128:256]
        for k, (cols, _) in enumerate(quads):
            a, b = split(q[256 * k : 256 * (k + 1)])
            qh[l, :, cols] = a
            ql[l, :, cols] = b

    v = stacked(fs)
    fst[...] = jnp.transpose(v)
    v = dot(v, skw[...])
    v = v[:, 0:128] + v[:, 128:256] + biast[0:1]
    for n in range(6):
        pre[:, 128 * n : 128 * (n + 1)] = v[576 * n : 576 * (n + 1)]
    loads["xy0"].wait()
    xy_transform(tab["xy0"], fs, 576, 3, 256)

    each(xs, (0, 1), has_dx, has_ux, recv)
    each(ys, (2, 3), has_uy, has_dy, start)

    loads["z0"].wait()
    z_transform(th[...], tl[...], tab["z0"], 768, kh, kl, 0)

    for c in z_all:
        c.wait_recv()
    low = iota((40, 128), 1) < 64
    for i in range(2):
        a = zrecv[i]
        half[0, i, :, 512:640] = jnp.where(low, a, 0.0)
        half[1, i, :, 512:640] = jnp.where(low, pltpu.roll(a, 64, 1), 0.0)
    each(xs, (2, 3), has_ux, has_dx, start)
    each(ys, (4, 5), has_uy, has_dy, start)

    modes_forward(0)
    loads["z0t"].wait()
    a = lanes_cat(qh[0], ql[0], qh[0])
    for n in range(3):
        cols = slice(256 * n, 256 * (n + 1))
        tz = rows_cat(tab["z0t"][0:512, cols], tab["z0t"][0:512, cols], tab["z0t"][512:1024, cols])
        hi, lo = split(dot(a, tz))
        bs[0:256, cols] = hi
        bs[256:512, cols] = lo
    each(xs, (2, 3), has_dx, has_ux, recv)
    each(ys, (6, 7), has_uy, has_dy, start)
    loads["inv"].wait()
    for n in range(3):
        cols = slice(256 * n, 256 * (n + 1))
        pre[:, cols] = pre[:, cols] + dot(tab["inv"][...], rows_cat(bs[0:512, cols], bs[0:256, cols]))

    def halves_of(cols, qcols):
        for j in range(4):
            hi, lo = split(half[j, :, :, cols].reshape(160, -1))
            hs[160 * j : 160 * (j + 1), cols] = hi
            hs[640 + 160 * j : 640 + 160 * (j + 1), cols] = lo
        cells = quart[:, :, :, qcols].reshape(360, 256)
        hi, lo = split(rows_cat(cells, jnp.zeros((8, 256), F32)))
        qs[0:368, qcols] = hi
        qs[368:736, qcols] = lo

    def one_chunk(table, data, rows, cols, into_h, into_l):
        v = rows_cat(data[0 : 2 * rows, cols], data[0:rows, cols])
        hi, lo = split(dot(table[...], v))
        into_h[:, cols] = hi
        into_l[:, cols] = lo

    each(ys, (0, 1, 2, 3), has_dy, has_uy, recv)
    halves_of(slice(0, 384), slice(0, 256))
    loads["xy1"].wait()
    loads["xy2"].wait()
    one_chunk(tab["xy1"], hs, 640, slice(0, 256), th, tl)
    v = lanes_cat(hs[0:640, 256:384], hs[640:1280, 256:384])
    v = dot(tab["xy1"][:, 640:1920], rows_cat(v, v))
    hi, lo = split(v[:, 0:128] + v[:, 128:256])
    th[:, 256:384] = hi
    tl[:, 256:384] = lo
    one_chunk(tab["xy2"], qs, 368, slice(0, 256), qth, qtl)

    def z_product(hi, lo, table, first, rows, depth):
        tz = table[first : first + depth]
        return dot(lanes_cat(hi, lo, hi), rows_cat(tz, tz, table[rows + first : rows + first + depth]))

    loads["z1"].wait()
    loads["z2"].wait()
    kown[0] = z_product(th[:, 0:384], tl[:, 0:384], tab["z1"], 0, 640, 384)
    kown[1] = z_product(qth[:, 0:256], qtl[:, 0:256], tab["z2"], 0, 512, 256)

    for name in ("z1c", "z2c", "xy12", "unpair", "xy12t", "z2ct"):
        loads[name].wait()
    load_c.wait()
    each(ys, (4, 5, 6, 7), has_dy, has_uy, recv)
    halves_of(slice(384, 640), slice(256, 512))
    one_chunk(tab["xy1"], hs, 640, slice(384, 640), th, tl)
    one_chunk(tab["xy2"], qs, 368, slice(256, 512), qth, qtl)
    hi, lo = split(kown[0] + z_product(th[:, 384:640], tl[:, 384:640], tab["z1"], 384, 640, 256))
    kh[1] = hi
    kl[1] = lo
    hi, lo = split(kown[1] + z_product(qth[:, 256:512], qtl[:, 256:512], tab["z2"], 256, 512, 256))
    kh[2] = hi
    kl[2] = lo
    for l in (1, 2):
        modes_forward(l)

    for l, name in ((1, "z1c"), (2, "z2c")):
        tz = tab[name]
        v = dot(lanes_cat(qh[l], ql[l], qh[l]), rows_cat(tz[0:512], tz[0:512], tz[512:1024]))
        hi, lo = split(v)
        t12[256 * (l - 1) : 256 * l] = hi
        t12[512 + 256 * (l - 1) : 512 + 256 * l] = lo
    s = dot(tab["xy12"][...], rows_cat(t12[...], t12[0:512]))

    scale = 1.0 / math.sqrt(ngx * ngy * ngz * NP**3)
    c0 = math.sqrt(2.0 / math.pi)
    sums = []
    for n in range(3):
        cols = slice(256 * n, 256 * (n + 1))
        hi, lo = split(s[:, 128 * n : 128 * (n + 1)])
        v = dot(lanes_cat(hi, lo), tab["unpair"][...])
        for k in range(2):
            for step in range(2):
                wide[2 * n + k, pl.ds(step, 144, stride=2), :] = v[:, 128 * k : 128 * (k + 1)]
        colsum = jnp.zeros((8, 256), F32)
        for m in range(12):
            rows, pair = slice(48 * m, 48 * (m + 1)), slice(24 * m, 24 * (m + 1))
            v = lanes_cat(wide[2 * n, pair], wide[2 * n + 1, pair])
            x = pre[rows, cols] + rows_cat(v, v)
            x2 = x * x
            t = jnp.tanh(x * (c0 + (c0 * 0.044715) * x2))
            half_t = 0.5 + 0.5 * t
            result[rows, cols] = x * half_t
            slope = half_t + x * (1.0 - t * t) * (0.5 * c0 + (1.5 * c0 * 0.044715) * x2)
            g = cot[rows, cols] * scale * slope
            hi, lo = split(g)
            gs[rows, cols] = hi
            gs[576 + 48 * m : 576 + 48 * (m + 1), cols] = lo
            g2 = g[0:24] + g[24:48]
            down[2 * n, pair] = g2[:, 0:128]
            down[2 * n + 1, pair] = g2[:, 128:256]
            colsum = colsum + jnp.sum(g.reshape(6, 8, 256), axis=0)
        sums.append(colsum)
        one_chunk(tab["xy0"], gs, 576, cols, th, tl)
        v = [down[2 * n + k, pl.ds(0, 144, stride=2), :] + down[2 * n + k, pl.ds(1, 144, stride=2), :] for k in range(2)]
        hi, lo = split(lanes_cat(*v))
        hi, lo = split(dot(lanes_cat(hi, lo), tab["pair"][...]))
        ghh[:, 128 * n : 128 * (n + 1)] = hi
        ghl[:, 128 * n : 128 * (n + 1)] = lo
    store = pltpu.make_async_copy(result, result_hbm, local_sem.at[2])
    store.start()
    gbias[...] = fold_lanes(lanes_cat(*sums))

    z_transform(th[...], tl[...], tab["z0"], 768, gqh, gql, 0)
    hi, lo = split(dot(tab["xy12t"][...], rows_cat(ghh[...], ghl[...], ghh[...])))
    g12h[...] = hi
    g12l[...] = lo
    z_transform(g12h[0:256], g12l[0:256], tab["z1"], 384, gqh, gql, 1, (0, 640))
    z_transform(g12h[256:512], g12l[256:512], tab["z2ct"], 384, gqh, gql, 2)

    total = dot(fst[...], stacked(gs))
    total = total[0:128] + total[128:256]
    total = jnp.where(diag_io, total[:, 0:128] + total[:, 128:256], 0.0)
    s = total[0:32] + total[32:64] + total[64:96] + total[96:128]
    s = s + pltpu.roll(s, 64, 1)
    gskip[...] = s + pltpu.roll(s, 32, 1)

    def gram(at, bh, bl):
        g = dot(at, rows_cat(*[lanes_cat(bh[:, c], bl[:, c]) for _, c in quads]))
        g = g[0:128] + g[128:256]
        g = jnp.where(diag_ir, g[:, 0:256] + g[:, 256:512], 0.0)
        return fold_lanes(g[0:32] + g[32:64] + g[64:96] + g[96:128])

    low = iota((32, 128), 1) < 64

    def modes_backward(l, carry):
        u = um[l]
        u = lanes_cat(u, u)
        e = jnp.zeros((256, 128), F32)
        g2 = []
        data = [(gqh[l, :, c], gql[l, :, c]) for c, _ in quads]
        g_out = gram(jnp.transpose(rows_cat(*[lanes_cat(a, b) for a, b in data])), rh.at[l], rl.at[l])
        g = dot(rows_cat(*[lanes_cat(a, b, a) for a, b in data]), outt[l])
        for k, (_, cols) in enumerate(quads):
            gr = g[256 * k : 256 * (k + 1)]
            d = gr * pr[l, :, cols]
            m2 = m2r[l, 0:1, cols]
            dm = d * m2
            e = e + dm[:, 0:128] + dm[:, 128:256]
            g2.append(jnp.sum((d * u).reshape(32, 8, 256), axis=0))
            hi, lo = split(gr * (u * m2))
            rh[l, :, cols] = hi
            rl[l, :, cols] = lo
        g_in = gram(kt[l], rh.at[l], rl.at[l])
        e = (e + pltpu.roll(e, 64, 1)).reshape(16, 16, 128)
        g0 = jnp.sum(e * m1t[l][None, :, :], axis=1)
        g1 = jnp.sum(e * m0t[l][:, None, :], axis=0)
        g2 = jnp.sum(lanes_cat(*g2), axis=0, keepdims=True)
        g2 = jnp.where(iota((16, 1024), 0) == iota((16, 1024), 1) // 64, g2, 0.0)
        g2 = fold_lanes(g2)
        row = 64 * l
        pay[pl.ds(row, 32), :] = jnp.where(low, g_in, g_out)
        pay[pl.ds(row + 32, 16), :] = jnp.where(low[0:16], g0, g1)
        pay[pl.ds(row + 48, 16), :] = jnp.where(low[0:16], g2, 0.0)
        return carry

    for l in range(3):
        modes_backward(l, 0)
    s = gskip[...]
    s = jnp.where(iota((16, 128), 1) < 96, s[0:16], s[16:32])
    pay[48:64] = jnp.where(low[0:16], pay[48:64], s)
    b = gbias[...] + pltpu.roll(gbias[...], 32, 1)
    b = jnp.broadcast_to(jnp.sum(b, axis=0, keepdims=True), (16, 128))
    pay[112:128] = jnp.where(low[0:16], pay[112:128], b)

    size = PAY // ngy

    def pushes(count, make, act):
        def body(k, carry):
            act(make(k))
            return carry

        lax.fori_loop(1, count, body, 0)

    def scatter(k):
        t = lax.rem(gy + k, ngy)
        return pltpu.make_async_remote_copy(
            src_ref=pay.at[pl.ds(pl.multiple_of(t * size, 8), size)],
            dst_ref=ra.at[k],
            send_sem=red_send.at[k],
            recv_sem=red_recv.at[k],
            device_id=(gx, t, gz),
            device_id_type=MESH,
        )

    def exchange(k):
        q = lax.rem(me + k, group)
        return pltpu.make_async_remote_copy(
            src_ref=acc,
            dst_ref=rb.at[me],
            send_sem=red_send.at[ngy + k],
            recv_sem=red_recv.at[ngy + k],
            device_id=(q // ngz, gy, lax.rem(q, ngz)),
            device_id_type=MESH,
        )

    mine = pl.ds(pl.multiple_of(gy * size, 8), size)

    def gather(k):
        t = lax.rem(gy + k, ngy)
        return pltpu.make_async_remote_copy(
            src_ref=red.at[mine],
            dst_ref=red.at[mine],
            send_sem=red_send.at[ngy + group + k],
            recv_sem=red_recv.at[ngy + group + k],
            device_id=(gx, t, gz),
            device_id_type=MESH,
        )

    for k in range(1, ngy):
        scatter(k).start()
    pushes(ngy, scatter, recv)
    total = pay[mine]
    for k in range(1, ngy):
        total = total + ra[k]
    acc[...] = total
    rb[me] = total
    for k in range(1, group):
        exchange(k).start()
    pushes(group, exchange, recv)
    total = rb[0]
    for k in range(1, group):
        total = total + rb[k]
    red[mine] = total
    for k in range(1, ngy):
        gather(k).start()
    pushes(ngy, gather, recv)
    store_red = pltpu.make_async_copy(red, red_hbm, local_sem.at[8])
    store_red.start()

    pushes(ngy, scatter, sent)
    pushes(group, exchange, sent)
    pushes(ngy, gather, sent)
    for c in z_all:
        c.wait_send()
    each(xs, range(4), has_ux, has_dx, sent)
    each(ys, range(8), has_uy, has_dy, sent)
    store.wait()
    store_red.wait()


def unpack_kernel(result_in, red_in, result_out, *refs):
    outs, (red, held), bufs, sem = refs[0:5], refs[5:7], refs[7:12], refs[12]
    skip, bias, modes, fin, fout = bufs
    parts = [pl.ds(96 * k, 96) for k in range(6)]
    fetch_red = pltpu.make_async_copy(red_in, red, sem.at[17])
    fetch_red.start()
    fetch = [pltpu.make_async_copy(result_in.at[p], held.at[p], sem.at[k]) for k, p in enumerate(parts)]
    store = [pltpu.make_async_copy(held.at[p], result_out.at[p], sem.at[6 + k]) for k, p in enumerate(parts)]
    small = [pltpu.make_async_copy(b, o, sem.at[12 + k]) for k, (b, o) in enumerate(zip(bufs, outs))]
    for copy in fetch:
        copy.start()
    fetch_red.wait()
    skip[0:16] = red[48:64, 64:96]
    skip[16:32] = red[48:64, 96:128]
    bias[...] = red[112:113, 64:96]
    for l in range(3):
        row = 64 * l
        fin[l] = red[row : row + 32, 0:64]
        fout[l] = red[row : row + 32, 64:128]
        modes[l, 0] = red[row + 32 : row + 48, 0:64]
        modes[l, 1] = red[row + 32 : row + 48, 64:128]
        modes[l, 2] = red[row + 48 : row + 64, 0:64]
    for copy in small:
        copy.start()
    for a, b in zip(fetch, store):
        a.wait()
        b.start()
    for copy in store + small:
        copy.wait()


def solution(mesh):
    sizes = tuple(mesh.shape[name] for name in ("gx", "gy", "gz"))
    ngx, ngy, ngz = sizes
    group = ngx * ngz
    size = PAY // ngy
    any_spec = pl.BlockSpec(memory_space=pl.ANY)
    scratch = [pltpu.VMEM(table_shape(n), BF) for n in NAMES] + [
        pltpu.VMEM((576, 768), F32),
        pltpu.VMEM((576, 768), F32),
        pltpu.VMEM((576, 768), F32),
        pltpu.VMEM((1152, 768), BF),
        pltpu.VMEM((4, 4, 40, 640), F32),
        pltpu.VMEM((3, 3, 40, 512), F32),
        pltpu.VMEM((1280, 640), BF),
        pltpu.VMEM((736, 512), BF),
        pltpu.VMEM((3, 256, 512), BF),
        pltpu.VMEM((3, 256, 512), BF),
        pltpu.VMEM((3, 256, 1024), F32),
        pltpu.VMEM((3, 256, 1024), BF),
        pltpu.VMEM((3, 256, 1024), BF),
        pltpu.VMEM((3, 256, 512), BF),
        pltpu.VMEM((3, 256, 512), BF),
        pltpu.VMEM((256, 768), BF),
        pltpu.VMEM((256, 768), BF),
        pltpu.VMEM((512, 768), BF),
        pltpu.VMEM((1024, 384), BF),
        pltpu.VMEM((576, 768), F32),
        pltpu.VMEM((1152, 768), BF),
        pltpu.VMEM((3, 256, 512), BF),
        pltpu.VMEM((3, 256, 512), BF),
        pltpu.VMEM((144, 384), BF),
        pltpu.VMEM((144, 384), BF),
        pltpu.VMEM((6, 288, 128), F32),
        pltpu.VMEM((6, 288, 128), F32),
        pltpu.VMEM((512, 384), BF),
        pltpu.VMEM((512, 384), BF),
        pltpu.VMEM((3, 256, 128), F32),
        pltpu.VMEM((3, 8, 1024), F32),
        pltpu.VMEM((3, 16, 128), F32),
        pltpu.VMEM((3, 16, 128), F32),
        pltpu.VMEM((3, 384, 256), BF),
        pltpu.VMEM((3, 512, 256), BF),
        pltpu.VMEM((3, 384, 256), BF),
        pltpu.VMEM((256, 256), BF),
        pltpu.VMEM((8, 128), F32),
        pltpu.VMEM((32, 128), F32),
        pltpu.VMEM((8, 128), F32),
        pltpu.VMEM((PAY, 128), F32),
        pltpu.VMEM((ngy, size, 128), F32),
        pltpu.VMEM((group, size, 128), F32),
        pltpu.VMEM((size, 128), F32),
        pltpu.VMEM((PAY, 128), F32),
        pltpu.VMEM((2, 40, 128), F32),
        pltpu.VMEM((2, 40, 128), F32),
        pltpu.VMEM((256, 512), BF),
        pltpu.VMEM((256, 512), BF),
        pltpu.VMEM((256, 3456), BF),
        pltpu.VMEM((3, 256, 1024), BF),
        pltpu.VMEM((2, 256, 512), F32),
        pltpu.VMEM((CH, CH), F32),
        pltpu.VMEM((1, CH), F32),
        pltpu.VMEM((3, 3, MD, RK), F32),
        pltpu.VMEM((3, CH, RK), F32),
        pltpu.VMEM((3, CH, RK), F32),
        pltpu.SemaphoreType.DMA((len(NAMES),)),
        pltpu.SemaphoreType.DMA((9,)),
        pltpu.SemaphoreType.DMA((27,)),
        pltpu.SemaphoreType.DMA((27,)),
        pltpu.SemaphoreType.DMA((2 * ngy + group,)),
        pltpu.SemaphoreType.DMA((2 * ngy + group,)),
    ]

    def per_device(features, cotangent, skip_weight, bias_vector, mode_factors, in_factors, out_factors):
        tables = [jnp.asarray(TABLES[n]) for n in NAMES]
        result, red = pl.pallas_call(
            lambda *refs: layer_kernel(sizes, *refs),
            name="layer",
            out_shape=(jax.ShapeDtypeStruct((576, 768), F32), jax.ShapeDtypeStruct((PAY, 128), F32)),
            in_specs=[any_spec] * (7 + len(NAMES)),
            out_specs=(any_spec, any_spec),
            scratch_shapes=scratch,
            compiler_params=pltpu.CompilerParams(
                collective_id=0, has_side_effects=True, vmem_limit_bytes=60 * 1024 * 1024
            ),
            cost_estimate=pl.CostEstimate(flops=32 * 10**9, bytes_accessed=20 * 10**6, transcendentals=442368),
        )(
            features.reshape(576, 768),
            cotangent.reshape(576, 768),
            skip_weight,
            bias_vector.reshape(1, CH),
            mode_factors,
            in_factors,
            jnp.swapaxes(out_factors, 1, 2),
            *tables,
        )
        outs = pl.pallas_call(
            unpack_kernel,
            name="unpack",
            out_shape=(
                jax.ShapeDtypeStruct((576, 768), F32),
                jax.ShapeDtypeStruct((CH, CH), F32),
                jax.ShapeDtypeStruct((1, CH), F32),
                jax.ShapeDtypeStruct((3, 3, MD, RK), F32),
                jax.ShapeDtypeStruct((3, CH, RK), F32),
                jax.ShapeDtypeStruct((3, CH, RK), F32),
            ),
            in_specs=[any_spec] * 2,
            out_specs=(any_spec,) * 6,
            scratch_shapes=[
                pltpu.VMEM((PAY, 128), F32),
                pltpu.VMEM((576, 768), F32),
                pltpu.VMEM((CH, CH), F32),
                pltpu.VMEM((1, CH), F32),
                pltpu.VMEM((3, 3, MD, RK), F32),
                pltpu.VMEM((3, CH, RK), F32),
                pltpu.VMEM((3, CH, RK), F32),
                pltpu.SemaphoreType.DMA((18,)),
            ],
        )(result, red)
        return (outs[0].reshape(NP, NP, NP * CH), outs[1], outs[2].reshape(CH), outs[3], outs[4], jnp.swapaxes(outs[5], 1, 2))

    placed = (P("gx", "gy", "gz"), P("gx", "gy", "gz"), P(), P(), P(), P(), P())
    return jax.shard_map(
        per_device,
        mesh=mesh,
        in_specs=placed,
        out_specs=(P("gx", "gy", "gz"), P(), P(), P(), P(), P()),
        check_vma=False,
    )
```

```python
import math

import jax
import jax.numpy as jnp
import ml_dtypes
import numpy as np
from jax import lax
from jax.experimental import pallas as pl
from jax.experimental.pallas import tpu as pltpu
from jax.sharding import PartitionSpec as P

MESH = pl.DeviceIdType.MESH
BF = jnp.bfloat16
F32 = jnp.float32
CH, RK, MD, NP = 32, 64, 16, 24
NN = (((1,), (0,)), ((), ()))
NT = (((1,), (1,)), ((), ()))
TN = (((0,), (0,)), ((), ()))
PAY = 192


def basis(length):
    rows = np.arange(MD)
    freq = np.where(rows < MD // 2, rows, rows - MD // 2 + 1).astype(np.float64)
    phase = 2.0 * math.pi / length * freq[:, None] * np.arange(length)[None, :]
    wave = np.where((rows < MD // 2)[:, None], np.cos(phase), np.sin(phase))
    return wave * math.sqrt(2.0 / length)


def halves(x):
    x = np.asarray(x, np.float32)
    hi = x.astype(ml_dtypes.bfloat16)
    lo = (x - hi.astype(np.float32)).astype(ml_dtypes.bfloat16)
    return hi, lo


def left(x):
    hi, lo = halves(x)
    return np.concatenate([hi, hi, lo], axis=1)


def right(x):
    hi, lo = halves(x)
    return np.concatenate([hi, lo], axis=0)


def exact(x, times, axis):
    x = np.asarray(x, np.float32).astype(ml_dtypes.bfloat16)
    return np.concatenate([x] * times, axis=axis)


def channel_eye(b):
    return np.kron(b, np.eye(CH))


def make_tables():
    b24, b18 = basis(24), basis(18)
    pool = np.zeros((208, 12, 24))
    for j in range(2):
        for i in range(2):
            for r in range(36):
                x, y = i * 6 + r // 6, 2 * (j * 6 + r % 6)
                pool[(j * 2 + i) * 40 + r, x, y : y + 2] = 1 / 8
    for r in range(36):
        x, y = 2 * (r // 6), 4 * (r % 6)
        pool[160 + r, x : x + 2, y : y + 4] = 1 / 64
    pool = pool.reshape(208, 288)
    pair = channel_eye(np.kron(np.eye(4), np.ones((2, 1))))
    quad = np.zeros((24, 8))
    for z in range(24):
        quad[z, z // 4] = 1
    quad = channel_eye(quad)
    xy0 = np.kron(b24, b24)
    at4, at3 = (1, 2, 0, 3), (1, 0, 2)
    xy1 = np.zeros((256, 4, 4, 40))
    for j in range(4):
        for i in range(4):
            for r in range(36):
                xy1[:, j, i, r] = np.kron(b24[:, at4[i] * 6 + r // 6], b24[:, at4[j] * 6 + r % 6])
    xy2 = np.zeros((256, 368))
    for j in range(3):
        for i in range(3):
            for r in range(36):
                xy2[:, (j * 3 + i) * 40 + r] = np.kron(
                    b18[:, at3[i] * 6 + r // 6], b18[:, at3[j] * 6 + r % 6]
                )
    z0 = channel_eye(b24.T)
    z1s, z2s = [], []
    for gz in range(2):
        z1 = np.zeros((20, 16))
        z1[0:12] = b24[:, 6:18].T
        if gz == 0:
            z1[12:18] = b24[:, 18:24].T
        else:
            z1[12:16] = b24[:, 2:6].T
            z1[16:18] = b24[:, 0:2].T
        z1s.append(right(channel_eye(z1)))
        z2 = np.zeros((16, 16))
        z2[0:6] = b18[:, 6:12].T
        z2[8:14] = b18[:, 12:18].T if gz == 0 else b18[:, 0:6].T
        z2s.append(right(channel_eye(z2)))
    z1c = channel_eye(b24[:, 6:18])
    z2c = channel_eye(np.repeat(b18[:, 6:12], 2, axis=1))
    c1 = b24[:, 6:18]
    c2 = np.repeat(b18[:, 6:12], 2, axis=1)
    xy12 = np.concatenate([np.kron(c1, c1), np.kron(c2, c2)], axis=0)
    return {
        "pool": exact(pool, 2, 1),
        "pair": exact(pair, 2, 0),
        "quad": exact(quad, 2, 0),
        "unpair": exact(pair.T, 2, 0),
        "xy0": left(xy0),
        "z0": right(z0),
        "z0t": right(z0.T),
        "inv": left(xy0.T),
        "xy1": left(xy1.reshape(256, 640)),
        "z1": np.concatenate(z1s, axis=0),
        "xy2": left(xy2),
        "z2": np.concatenate(z2s, axis=0),
        "z1c": right(z1c),
        "z2c": right(z2c),
        "xy12": left(xy12.T),
        "xy12t": left(xy12),
        "z2ct": right(z2c.T),
    }


TABLES = make_tables()
NAMES = list(TABLES)


def table_shape(name):
    rows, cols = TABLES[name].shape
    return (rows // 2 if name in ("z1", "z2") else rows), cols


def dot(a, b, dims=NN):
    return lax.dot_general(a, b, dims, preferred_element_type=F32)


def split(x):
    hi = x.astype(BF)
    return hi, (x - hi.astype(F32)).astype(BF)


def rows_cat(*parts):
    return jnp.concatenate(parts, axis=0)


def lanes_cat(*parts):
    return jnp.concatenate(parts, axis=1)


def iota(shape, dim):
    return lax.broadcasted_iota(jnp.int32, shape, dim)


def fold_lanes(x):
    total = x[:, 0:128]
    for k in range(1, x.shape[1] // 128):
        total = total + x[:, 128 * k : 128 * (k + 1)]
    return total + pltpu.roll(total, 64, 1)


def layer_kernel(sizes, *refs):
    ngx, ngy, ngz = sizes
    refs = list(refs)
    take = lambda n: [refs.pop(0) for _ in range(n)]
    feat_hbm, cot_hbm = take(2)
    weights_hbm = take(5)
    hbm = dict(zip(NAMES, take(len(NAMES))))
    result_hbm, red_hbm = take(2)
    tab = dict(zip(NAMES, take(len(NAMES))))
    (feat, cot, result, fs, half, quart, hs, qs, kh, kl, pr, rh, rl, qh, ql, th, tl, bs, t12, pre, gs, gqh, gql, ghh, ghl,
     wide, down, g12h, g12l, um, m2r, m0t, m1t, inw, outw, outt, skw, biast, gskip, gbias, pay, ra, rb, acc, red, zsend, zrecv, qth, qtl, fst, kt, kown, strips, sh, sl,
     skip_ref, bias_ref, modes_ref, in_ref, out_ref) = take(60)
    table_sem, local_sem, halo_send, halo_recv, red_send, red_recv = take(6)

    gx, gy, gz = lax.axis_index("gx"), lax.axis_index("gy"), lax.axis_index("gz")
    me = gx * ngz + gz
    group = ngx * ngz

    thirds = [slice(256 * n, 256 * (n + 1)) for n in range(3)]
    load_f = [
        pltpu.make_async_copy(feat_hbm.at[:, pl.ds(256 * n, 256)], feat.at[:, pl.ds(256 * n, 256)], local_sem.at[9 + n])
        for n in range(3)
    ]
    for c in load_f:
        c.start()
    load_c = pltpu.make_async_copy(cot_hbm, cot, local_sem.at[1])
    loads = {}
    for k, name in enumerate(NAMES):
        rows = table_shape(name)[0]
        src = hbm[name].at[pl.ds(pl.multiple_of(gz * rows, 16), rows)] if name in ("z1", "z2") else hbm[name]
        loads[name] = pltpu.make_async_copy(src, tab[name], table_sem.at[k])
        if k < 3:
            loads[name].start()
    load_w = [
        pltpu.make_async_copy(src, dst, local_sem.at[3 + k])
        for k, (src, dst) in enumerate(zip(weights_hbm, (skip_ref, bias_ref, modes_ref, in_ref, out_ref)))
    ]
    for c in load_w:
        c.start()

    barrier = pltpu.get_barrier_semaphore()

    def greet_row(k, carry):
        pl.semaphore_signal(
            barrier, inc=1, device_id=(gx, lax.rem(gy + k, ngy), gz), device_id_type=MESH
        )
        return carry

    lax.fori_loop(1, ngy, greet_row, 0)

    def greet_plane(k, carry):
        q = lax.rem(me + k, group)
        pl.semaphore_signal(
            barrier, inc=1, device_id=(q // ngz, gy, lax.rem(q, ngz)), device_id_type=MESH
        )
        return carry

    lax.fori_loop(1, group, greet_plane, 0)

    def clear(j, i):
        half[j, i] = jnp.zeros((40, 640), F32)

    def clear_quarter(j, i):
        quart[j, i] = jnp.zeros((40, 512), F32)

    for edge, block in ((gx == 0, 2), (gx == ngx - 1, 3)):

        @pl.when(edge)
        def _():
            clear(0, block)
            clear(1, block)
            clear_quarter(0, block - 1)

    for edge, block in ((gy == 0, 2), (gy == ngy - 1, 3)):

        @pl.when(edge)
        def _():
            for i in range(4):
                clear(block, i)
            for i in range(3):
                clear_quarter(block - 1, i)

    loads["pool"].wait()
    loads["pair"].wait()
    for n, cols in enumerate(thirds):
        load_f[n].wait()
        if n == 2:
            for name in NAMES[3:]:
                loads[name].start()
                if name == "xy2":
                    load_c.start()
        cells = feat[:, cols].reshape(12, 2, 24, 256)
        hi, lo = split((cells[:, 0] + cells[:, 1]).reshape(288, 256))
        hi, lo = split(dot(tab["pool"][...], rows_cat(hi, lo)))
        strips[0, :, cols] = hi[160:208]
        strips[1, :, cols] = lo[160:208]
        cells = dot(lanes_cat(hi[0:160], lo[0:160]), tab["pair"][...])
        for j in range(2):
            for i in range(2):
                r = (j * 2 + i) * 40
                half[j, i, :, 128 * n : 128 * (n + 1)] = cells[r : r + 40]
    for i in range(2):
        a, b = half[0, i, :, 128:256], half[1, i, :, 128:256]
        a = jnp.where(gz == 1, a, pltpu.roll(a, 64, 1))
        b = jnp.where(gz == 1, pltpu.roll(b, 64, 1), b)
        zsend[i] = jnp.where(iota((40, 128), 1) < 64, a, b)

    pl.semaphore_wait(barrier, ngy - 1 + group - 1)

    def remote(k, src, dst, to):
        return pltpu.make_async_remote_copy(
            src_ref=src,
            dst_ref=dst,
            send_sem=halo_send.at[k],
            recv_sem=halo_recv.at[k],
            device_id=to,
            device_id_type=MESH,
        )

    first = pl.multiple_of(256 * (1 - gz), 128)
    own, far, qown, qfar = pl.ds(0, 384), pl.ds(384, 256), pl.ds(0, 256), pl.ds(256, 256)
    mid, side = pl.ds(0, 2), pl.ds(2, 2)
    qside = pl.ds(1, 2)
    across = (gx, gy, 1 - gz)
    z_all = [
        remote(0, half.at[mid, mid, :, pl.ds(first, 128)], half.at[mid, mid, :, pl.ds(384, 128)], across),
        remote(1, zsend, zrecv, across),
        remote(2, quart.at[0, 0, :, qown], quart.at[0, 0, :, qfar], across),
    ]

    def x_copies(k, src, dst, to):
        return [
            remote(k, half.at[mid, src, :, own], half.at[mid, dst, :, own], to),
            remote(k + 1, quart.at[0, 0, :, qown], quart.at[0, dst - 1, :, qown], to),
            remote(k + 2, half.at[mid, src, :, far], half.at[mid, dst, :, far], to),
            remote(k + 3, quart.at[0, 0, :, qfar], quart.at[0, dst - 1, :, qfar], to),
        ]

    def y_copies(k, src, dst, to):
        return [
            remote(k, half.at[src, mid, :, own], half.at[dst, mid, :, own], to),
            remote(k + 1, quart.at[0, 0, :, qown], quart.at[dst - 1, 0, :, qown], to),
            remote(k + 2, half.at[src, side, :, own], half.at[dst, side, :, own], to),
            remote(k + 3, quart.at[0, qside, :, qown], quart.at[dst - 1, qside, :, qown], to),
            remote(k + 4, half.at[src, mid, :, far], half.at[dst, mid, :, far], to),
            remote(k + 5, quart.at[0, 0, :, qfar], quart.at[dst - 1, 0, :, qfar], to),
            remote(k + 6, half.at[src, side, :, far], half.at[dst, side, :, far], to),
            remote(k + 7, quart.at[0, qside, :, qfar], quart.at[dst - 1, qside, :, qfar], to),
        ]

    xs = x_copies(3, 1, 2, (gx + 1, gy, gz)), x_copies(7, 0, 3, (gx - 1, gy, gz))
    ys = y_copies(11, 1, 2, (gx, gy + 1, gz)), y_copies(19, 0, 3, (gx, gy - 1, gz))

    def each(copies, which, to_up, to_down, act):
        @pl.when(to_up)
        def _():
            for k in which:
                act(copies[0][k])

        @pl.when(to_down)
        def _():
            for k in which:
                act(copies[1][k])

    has_ux, has_dx, has_uy, has_dy = gx < ngx - 1, gx > 0, gy < ngy - 1, gy > 0
    start = lambda c: c.start()
    recv = lambda c: c.wait_recv()
    sent = lambda c: c.wait_send()

    z_all[0].start()
    z_all[1].start()
    loads["quad"].wait()
    cells = dot(lanes_cat(strips[0], strips[1]), tab["quad"][...])
    quart[0, 0, :, 0:256] = cells[0:40]
    z_all[2].start()
    each(xs, (0, 1), has_ux, has_dx, start)
    each(ys, (0, 1), has_uy, has_dy, start)

    for c in load_w:
        c.wait()

    def dup64(x):
        eye = (iota((64, 128), 0) == iota((64, 128), 1) % 64).astype(BF)
        return dot(x, eye)

    def dup32(x):
        eye = (iota((32, 128), 0) == iota((32, 128), 1) % 32).astype(BF)
        return dot(x, eye)

    diag_ir = iota((128, 256), 0) // 32 == iota((128, 256), 1) // 64
    diag_ro = iota((256, 128), 0) // 64 == iota((256, 128), 1) // 32
    diag_io = iota((128, 128), 0) // 32 == iota((128, 128), 1) // 32
    eye64 = (iota((64, 64), 0) == iota((64, 64), 1)).astype(BF)

    b0, b1 = split(jnp.broadcast_to(bias_ref[...], (16, 32)))
    biast[...] = (dup32(b0) + dup32(b1))[0:8]
    w0, w1 = [jnp.where(diag_io, rows_cat(*[dup32(w)] * 4), 0.0).astype(BF) for w in split(skip_ref[...])]
    w0 = lanes_cat(w0, w1)
    skw[...] = rows_cat(w0, w0)

    def spread(l, carry):
        i0, i1 = split(in_ref[l])
        o0, o1 = split(out_ref[l])

        def wide(w):
            t = dup64(w)
            return jnp.where(diag_ir, rows_cat(*[lanes_cat(t, t)] * 4), 0.0).astype(BF)

        def tall(w):
            t = dup32(dot(eye64, w, NT).astype(BF))
            return jnp.where(diag_ro, rows_cat(*[t] * 4), 0.0).astype(BF)

        w0 = wide(i0)
        inw[l] = rows_cat(w0, w0, wide(i1))
        w0 = wide(o0)
        outt[l] = rows_cat(w0, w0, wide(o1))
        w0 = lanes_cat(tall(o0), tall(o1))
        outw[l] = rows_cat(w0, w0)
        dup = []
        for d in range(3):
            m = modes_ref[l, d]
            hi, lo = split(m)
            rest = (m - hi.astype(F32) - lo.astype(F32)).astype(BF)
            dup.append(dup64(hi) + dup64(lo) + dup64(rest))
        m0t[l] = dup[0]
        m1t[l] = dup[1]
        um[l] = (dup[0][:, None, :] * dup[1][None, :, :]).reshape(256, 128)
        line = lanes_cat(*[dup[2]] * 8)
        line = jnp.where(iota((16, 1024), 0) == iota((16, 1024), 1) // 64, line, 0.0)
        m2r[l] = jnp.broadcast_to(jnp.sum(line, axis=0, keepdims=True), (8, 1024))
        return carry

    for l in range(3):
        spread(l, 0)

    hi, lo = split(feat[...])
    fs[0:576] = hi
    fs[576:1152] = lo

    def stacked(ref):
        parts = [slice(128 * n, 128 * (n + 1)) for n in range(6)]
        return rows_cat(*[lanes_cat(ref[0:576, c], ref[576:1152, c]) for c in parts])

    def xy_transform(table, hi_lo, rows, chunks, wide):
        for n in range(chunks):
            cols = slice(wide * n, wide * (n + 1))
            data = rows_cat(hi_lo[0 : 2 * rows, cols], hi_lo[0:rows, cols])
            hi, lo = split(dot(table[...], data))
            th[:, cols] = hi
            tl[:, cols] = lo

    def z_transform(hi, lo, table, depth, into_h, into_l, l, parts=None):
        a = lanes_cat(hi, lo, hi)
        zh, zl = (0, depth) if parts is None else parts
        for n in range(2):
            cols = slice(256 * n, 256 * (n + 1))
            tz = rows_cat(table[zh : zh + depth, cols], table[zh : zh + depth, cols], table[zl : zl + depth, cols])
            vh, vl = split(dot(a, tz))
            into_h[l, :, cols] = vh
            into_l[l, :, cols] = vl

    quads = [(slice(128 * c, 128 * (c + 1)), slice(256 * c, 256 * (c + 1))) for c in range(4)]

    def modes_forward(l):
        data = [(kh[l, :, c], kl[l, :, c]) for c, _ in quads]
        kt[l] = jnp.transpose(rows_cat(*[lanes_cat(a, b) for a, b in data]))
        p = dot(rows_cat(*[lanes_cat(a, b, a) for a, b in data]), inw[l])
        u = um[l]
        u = lanes_cat(u, u)
        data = []
        for k, (_, cols) in enumerate(quads):
            pk = p[256 * k : 256 * (k + 1)]
            pr[l, :, cols] = pk
            a, b = split(pk * u * m2r[l, 0:1, cols])
            rh[l, :, cols] = a
            rl[l, :, cols] = b
            data.append(lanes_cat(a, b))
        q = dot(rows_cat(*data), outw[l])
        q = q[:, 0:128] + q[:, 128:256]
        for k, (cols, _) in enumerate(quads):
            a, b = split(q[256 * k : 256 * (k + 1)])
            qh[l, :, cols] = a
            ql[l, :, cols] = b

    v = stacked(fs)
    fst[...] = jnp.transpose(v)
    v = dot(v, skw[...])
    v = v[:, 0:128] + v[:, 128:256] + biast[0:1]
    for n in range(6):
        pre[:, 128 * n : 128 * (n + 1)] = v[576 * n : 576 * (n + 1)]
    loads["xy0"].wait()
    xy_transform(tab["xy0"], fs, 576, 3, 256)

    each(xs, (0, 1), has_dx, has_ux, recv)
    each(ys, (2, 3), has_uy, has_dy, start)

    loads["z0"].wait()
    z_transform(th[...], tl[...], tab["z0"], 768, kh, kl, 0)

    for c in z_all:
        c.wait_recv()
    low = iota((40, 128), 1) < 64
    for i in range(2):
        a = zrecv[i]
        half[0, i, :, 512:640] = jnp.where(low, a, 0.0)
        half[1, i, :, 512:640] = jnp.where(low, pltpu.roll(a, 64, 1), 0.0)
    each(xs, (2, 3), has_ux, has_dx, start)
    each(ys, (4, 5), has_uy, has_dy, start)

    modes_forward(0)
    loads["z0t"].wait()
    a = lanes_cat(qh[0], ql[0], qh[0])
    for n in range(3):
        cols = slice(256 * n, 256 * (n + 1))
        tz = rows_cat(tab["z0t"][0:512, cols], tab["z0t"][0:512, cols], tab["z0t"][512:1024, cols])
        hi, lo = split(dot(a, tz))
        bs[0:256, cols] = hi
        bs[256:512, cols] = lo
    each(xs, (2, 3), has_dx, has_ux, recv)
    each(ys, (6, 7), has_uy, has_dy, start)
    loads["inv"].wait()
    for n in range(3):
        cols = slice(256 * n, 256 * (n + 1))
        pre[:, cols] = pre[:, cols] + dot(tab["inv"][...], rows_cat(bs[0:512, cols], bs[0:256, cols]))

    def halves_of(cols, qcols):
        for j in range(4):
            hi, lo = split(half[j, :, :, cols].reshape(160, -1))
            hs[160 * j : 160 * (j + 1), cols] = hi
            hs[640 + 160 * j : 640 + 160 * (j + 1), cols] = lo
        cells = quart[:, :, :, qcols].reshape(360, 256)
        hi, lo = split(rows_cat(cells, jnp.zeros((8, 256), F32)))
        qs[0:368, qcols] = hi
        qs[368:736, qcols] = lo

    def one_chunk(table, data, rows, cols, into_h, into_l):
        v = rows_cat(data[0 : 2 * rows, cols], data[0:rows, cols])
        hi, lo = split(dot(table[...], v))
        into_h[:, cols] = hi
        into_l[:, cols] = lo

    each(ys, (0, 1, 2, 3), has_dy, has_uy, recv)
    halves_of(slice(0, 384), slice(0, 256))
    loads["xy1"].wait()
    loads["xy2"].wait()
    one_chunk(tab["xy1"], hs, 640, slice(0, 256), th, tl)
    v = lanes_cat(hs[0:640, 256:384], hs[640:1280, 256:384])
    v = dot(tab["xy1"][:, 640:1920], rows_cat(v, v))
    hi, lo = split(v[:, 0:128] + v[:, 128:256])
    th[:, 256:384] = hi
    tl[:, 256:384] = lo
    one_chunk(tab["xy2"], qs, 368, slice(0, 256), qth, qtl)

    def z_product(hi, lo, table, first, rows, depth):
        tz = table[first : first + depth]
        return dot(lanes_cat(hi, lo, hi), rows_cat(tz, tz, table[rows + first : rows + first + depth]))

    loads["z1"].wait()
    loads["z2"].wait()
    kown[0] = z_product(th[:, 0:384], tl[:, 0:384], tab["z1"], 0, 640, 384)
    kown[1] = z_product(qth[:, 0:256], qtl[:, 0:256], tab["z2"], 0, 512, 256)

    for name in ("z1c", "z2c", "xy12", "unpair", "xy12t", "z2ct"):
        loads[name].wait()
    load_c.wait()
    each(ys, (4, 5, 6, 7), has_dy, has_uy, recv)
    halves_of(slice(384, 640), slice(256, 512))
    one_chunk(tab["xy1"], hs, 640, slice(384, 640), th, tl)
    one_chunk(tab["xy2"], qs, 368, slice(256, 512), qth, qtl)
    hi, lo = split(kown[0] + z_product(th[:, 384:640], tl[:, 384:640], tab["z1"], 384, 640, 256))
    kh[1] = hi
    kl[1] = lo
    hi, lo = split(kown[1] + z_product(qth[:, 256:512], qtl[:, 256:512], tab["z2"], 256, 512, 256))
    kh[2] = hi
    kl[2] = lo
    for l in (1, 2):
        modes_forward(l)

    for l, name in ((1, "z1c"), (2, "z2c")):
        tz = tab[name]
        v = dot(lanes_cat(qh[l], ql[l], qh[l]), rows_cat(tz[0:512], tz[0:512], tz[512:1024]))
        hi, lo = split(v)
        t12[256 * (l - 1) : 256 * l] = hi
        t12[512 + 256 * (l - 1) : 512 + 256 * l] = lo
    s = dot(tab["xy12"][...], rows_cat(t12[...], t12[0:512]))

    scale = 1.0 / math.sqrt(ngx * ngy * ngz * NP**3)
    c0 = math.sqrt(2.0 / math.pi)
    sums = []
    for n in range(3):
        cols = slice(256 * n, 256 * (n + 1))
        hi, lo = split(s[:, 128 * n : 128 * (n + 1)])
        v = dot(lanes_cat(hi, lo), tab["unpair"][...])
        for k in range(2):
            for step in range(2):
                wide[2 * n + k, pl.ds(step, 144, stride=2), :] = v[:, 128 * k : 128 * (k + 1)]
        colsum = jnp.zeros((8, 256), F32)
        for m in range(12):
            rows, pair = slice(48 * m, 48 * (m + 1)), slice(24 * m, 24 * (m + 1))
            v = lanes_cat(wide[2 * n, pair], wide[2 * n + 1, pair])
            x = pre[rows, cols] + rows_cat(v, v)
            x2 = x * x
            t = jnp.tanh(x * (c0 + (c0 * 0.044715) * x2))
            half_t = 0.5 + 0.5 * t
            result[rows, cols] = x * half_t
            slope = half_t + x * (1.0 - t * t) * (0.5 * c0 + (1.5 * c0 * 0.044715) * x2)
            g = cot[rows, cols] * scale * slope
            hi, lo = split(g)
            gs[rows, cols] = hi
            gs[576 + 48 * m : 576 + 48 * (m + 1), cols] = lo
            g2 = g[0:24] + g[24:48]
            down[2 * n, pair] = g2[:, 0:128]
            down[2 * n + 1, pair] = g2[:, 128:256]
            colsum = colsum + jnp.sum(g.reshape(6, 8, 256), axis=0)
        sums.append(colsum)
        one_chunk(tab["xy0"], gs, 576, cols, th, tl)
        v = [down[2 * n + k, pl.ds(0, 144, stride=2), :] + down[2 * n + k, pl.ds(1, 144, stride=2), :] for k in range(2)]
        hi, lo = split(lanes_cat(*v))
        hi, lo = split(dot(lanes_cat(hi, lo), tab["pair"][...]))
        ghh[:, 128 * n : 128 * (n + 1)] = hi
        ghl[:, 128 * n : 128 * (n + 1)] = lo
    store = pltpu.make_async_copy(result, result_hbm, local_sem.at[2])
    store.start()
    gbias[...] = fold_lanes(lanes_cat(*sums))

    z_transform(th[...], tl[...], tab["z0"], 768, gqh, gql, 0)
    hi, lo = split(dot(tab["xy12t"][...], rows_cat(ghh[...], ghl[...], ghh[...])))
    g12h[...] = hi
    g12l[...] = lo
    z_transform(g12h[0:256], g12l[0:256], tab["z1"], 384, gqh, gql, 1, (0, 640))
    z_transform(g12h[256:512], g12l[256:512], tab["z2ct"], 384, gqh, gql, 2)

    def skip_gradient():
        total = dot(fst[...], stacked(gs))
        total = total[0:128] + total[128:256]
        total = jnp.where(diag_io, total[:, 0:128] + total[:, 128:256], 0.0)
        s = total[0:32] + total[32:64] + total[64:96] + total[96:128]
        s = s + pltpu.roll(s, 64, 1)
        gskip[...] = s + pltpu.roll(s, 32, 1)

    def gram(at, bh, bl):
        g = dot(at, rows_cat(*[lanes_cat(bh[:, c], bl[:, c]) for _, c in quads]))
        g = g[0:128] + g[128:256]
        g = jnp.where(diag_ir, g[:, 0:256] + g[:, 256:512], 0.0)
        return fold_lanes(g[0:32] + g[32:64] + g[64:96] + g[96:128])

    low = iota((32, 128), 1) < 64

    def rank_cotangents(l):
        data = [(gqh[l, :, c], gql[l, :, c]) for c, _ in quads]
        return dot(rows_cat(*[lanes_cat(a, b, a) for a, b in data]), outt[l])

    def weigh(l, g):
        u = um[l]
        u = lanes_cat(u, u)
        e = jnp.zeros((256, 128), F32)
        g2 = []
        for k, (_, cols) in enumerate(quads):
            gr = g[256 * k : 256 * (k + 1)]
            d = gr * pr[l, :, cols]
            m2 = m2r[l, 0:1, cols]
            dm = d * m2
            e = e + dm[:, 0:128] + dm[:, 128:256]
            g2.append(jnp.sum((d * u).reshape(32, 8, 256), axis=0))
            hi, lo = split(gr * (u * m2))
            sh[l, :, cols] = hi
            sl[l, :, cols] = lo
        e = (e + pltpu.roll(e, 64, 1)).reshape(16, 16, 128)
        g0 = jnp.sum(e * m1t[l][None, :, :], axis=1)
        g1 = jnp.sum(e * m0t[l][:, None, :], axis=0)
        g2 = jnp.sum(lanes_cat(*g2), axis=0, keepdims=True)
        g2 = jnp.where(iota((16, 1024), 0) == iota((16, 1024), 1) // 64, g2, 0.0)
        row = 64 * l
        pay[row + 32 : row + 48] = jnp.where(low[0:16], g0, g1)
        pay[row + 48 : row + 64] = jnp.where(low[0:16], fold_lanes(g2), 0.0)

    def factors(l):
        data = [(gqh[l, :, c], gql[l, :, c]) for c, _ in quads]
        g_out = gram(jnp.transpose(rows_cat(*[lanes_cat(a, b) for a, b in data])), rh.at[l], rl.at[l])
        g_in = gram(kt[l], sh.at[l], sl.at[l])
        pay[64 * l : 64 * l + 32] = jnp.where(low, g_in, g_out)

    g0 = rank_cotangents(0)
    g1 = rank_cotangents(1)
    weigh(0, g0)
    factors(0)
    g2 = rank_cotangents(2)
    weigh(1, g1)
    factors(1)
    weigh(2, g2)
    skip_gradient()
    factors(2)
    s = gskip[...]
    s = jnp.where(iota((16, 128), 1) < 96, s[0:16], s[16:32])
    pay[48:64] = jnp.where(low[0:16], pay[48:64], s)
    b = gbias[...] + pltpu.roll(gbias[...], 32, 1)
    b = jnp.broadcast_to(jnp.sum(b, axis=0, keepdims=True), (16, 128))
    pay[112:128] = jnp.where(low[0:16], pay[112:128], b)

    size = PAY // ngy

    def pushes(count, make, act):
        def body(k, carry):
            act(make(k))
            return carry

        lax.fori_loop(1, count, body, 0)

    def scatter(k):
        t = lax.rem(gy + k, ngy)
        return pltpu.make_async_remote_copy(
            src_ref=pay.at[pl.ds(pl.multiple_of(t * size, 8), size)],
            dst_ref=ra.at[k],
            send_sem=red_send.at[k],
            recv_sem=red_recv.at[k],
            device_id=(gx, t, gz),
            device_id_type=MESH,
        )

    def exchange(k):
        q = lax.rem(me + k, group)
        return pltpu.make_async_remote_copy(
            src_ref=acc,
            dst_ref=rb.at[me],
            send_sem=red_send.at[ngy + k],
            recv_sem=red_recv.at[ngy + k],
            device_id=(q // ngz, gy, lax.rem(q, ngz)),
            device_id_type=MESH,
        )

    mine = pl.ds(pl.multiple_of(gy * size, 8), size)

    def gather(k):
        t = lax.rem(gy + k, ngy)
        return pltpu.make_async_remote_copy(
            src_ref=red.at[mine],
            dst_ref=red.at[mine],
            send_sem=red_send.at[ngy + group + k],
            recv_sem=red_recv.at[ngy + group + k],
            device_id=(gx, t, gz),
            device_id_type=MESH,
        )

    for k in range(1, ngy):
        scatter(k).start()
    pushes(ngy, scatter, recv)
    total = pay[mine]
    for k in range(1, ngy):
        total = total + ra[k]
    acc[...] = total
    rb[me] = total
    for k in range(1, group):
        exchange(k).start()
    pushes(group, exchange, recv)
    total = rb[0]
    for k in range(1, group):
        total = total + rb[k]
    red[mine] = total
    for k in range(1, ngy):
        gather(k).start()
    pushes(ngy, gather, recv)
    store_red = pltpu.make_async_copy(red, red_hbm, local_sem.at[8])
    store_red.start()

    pushes(ngy, scatter, sent)
    pushes(group, exchange, sent)
    pushes(ngy, gather, sent)
    for c in z_all:
        c.wait_send()
    each(xs, range(4), has_ux, has_dx, sent)
    each(ys, range(8), has_uy, has_dy, sent)
    store.wait()
    store_red.wait()


def unpack_kernel(result_in, red_in, result_out, *refs):
    outs, (red, held), bufs, sem = refs[0:5], refs[5:7], refs[7:12], refs[12]
    skip, bias, modes, fin, fout = bufs
    parts = [pl.ds(96 * k, 96) for k in range(6)]
    fetch_red = pltpu.make_async_copy(red_in, red, sem.at[17])
    fetch_red.start()
    fetch = [pltpu.make_async_copy(result_in.at[p], held.at[p], sem.at[k]) for k, p in enumerate(parts)]
    store = [pltpu.make_async_copy(held.at[p], result_out.at[p], sem.at[6 + k]) for k, p in enumerate(parts)]
    small = [pltpu.make_async_copy(b, o, sem.at[12 + k]) for k, (b, o) in enumerate(zip(bufs, outs))]
    for copy in fetch:
        copy.start()
    fetch_red.wait()
    skip[0:16] = red[48:64, 64:96]
    skip[16:32] = red[48:64, 96:128]
    bias[...] = red[112:113, 64:96]
    for l in range(3):
        row = 64 * l
        fin[l] = red[row : row + 32, 0:64]
        fout[l] = red[row : row + 32, 64:128]
        modes[l, 0] = red[row + 32 : row + 48, 0:64]
        modes[l, 1] = red[row + 32 : row + 48, 64:128]
        modes[l, 2] = red[row + 48 : row + 64, 0:64]
    for copy in small:
        copy.start()
    for a, b in zip(fetch, store):
        a.wait()
        b.start()
    for copy in store + small:
        copy.wait()


def solution(mesh):
    sizes = tuple(mesh.shape[name] for name in ("gx", "gy", "gz"))
    ngx, ngy, ngz = sizes
    group = ngx * ngz
    size = PAY // ngy
    any_spec = pl.BlockSpec(memory_space=pl.ANY)
    scratch = [pltpu.VMEM(table_shape(n), BF) for n in NAMES] + [
        pltpu.VMEM((576, 768), F32),
        pltpu.VMEM((576, 768), F32),
        pltpu.VMEM((576, 768), F32),
        pltpu.VMEM((1152, 768), BF),
        pltpu.VMEM((4, 4, 40, 640), F32),
        pltpu.VMEM((3, 3, 40, 512), F32),
        pltpu.VMEM((1280, 640), BF),
        pltpu.VMEM((736, 512), BF),
        pltpu.VMEM((3, 256, 512), BF),
        pltpu.VMEM((3, 256, 512), BF),
        pltpu.VMEM((3, 256, 1024), F32),
        pltpu.VMEM((3, 256, 1024), BF),
        pltpu.VMEM((3, 256, 1024), BF),
        pltpu.VMEM((3, 256, 512), BF),
        pltpu.VMEM((3, 256, 512), BF),
        pltpu.VMEM((256, 768), BF),
        pltpu.VMEM((256, 768), BF),
        pltpu.VMEM((512, 768), BF),
        pltpu.VMEM((1024, 384), BF),
        pltpu.VMEM((576, 768), F32),
        pltpu.VMEM((1152, 768), BF),
        pltpu.VMEM((3, 256, 512), BF),
        pltpu.VMEM((3, 256, 512), BF),
        pltpu.VMEM((144, 384), BF),
        pltpu.VMEM((144, 384), BF),
        pltpu.VMEM((6, 288, 128), F32),
        pltpu.VMEM((6, 288, 128), F32),
        pltpu.VMEM((512, 384), BF),
        pltpu.VMEM((512, 384), BF),
        pltpu.VMEM((3, 256, 128), F32),
        pltpu.VMEM((3, 8, 1024), F32),
        pltpu.VMEM((3, 16, 128), F32),
        pltpu.VMEM((3, 16, 128), F32),
        pltpu.VMEM((3, 384, 256), BF),
        pltpu.VMEM((3, 512, 256), BF),
        pltpu.VMEM((3, 384, 256), BF),
        pltpu.VMEM((256, 256), BF),
        pltpu.VMEM((8, 128), F32),
        pltpu.VMEM((32, 128), F32),
        pltpu.VMEM((8, 128), F32),
        pltpu.VMEM((PAY, 128), F32),
        pltpu.VMEM((ngy, size, 128), F32),
        pltpu.VMEM((group, size, 128), F32),
        pltpu.VMEM((size, 128), F32),
        pltpu.VMEM((PAY, 128), F32),
        pltpu.VMEM((2, 40, 128), F32),
        pltpu.VMEM((2, 40, 128), F32),
        pltpu.VMEM((256, 512), BF),
        pltpu.VMEM((256, 512), BF),
        pltpu.VMEM((256, 3456), BF),
        pltpu.VMEM((3, 256, 1024), BF),
        pltpu.VMEM((2, 256, 512), F32),
        pltpu.VMEM((2, 48, 768), BF),
        pltpu.VMEM((3, 256, 1024), BF),
        pltpu.VMEM((3, 256, 1024), BF),
        pltpu.VMEM((CH, CH), F32),
        pltpu.VMEM((1, CH), F32),
        pltpu.VMEM((3, 3, MD, RK), F32),
        pltpu.VMEM((3, CH, RK), F32),
        pltpu.VMEM((3, CH, RK), F32),
        pltpu.SemaphoreType.DMA((len(NAMES),)),
        pltpu.SemaphoreType.DMA((12,)),
        pltpu.SemaphoreType.DMA((27,)),
        pltpu.SemaphoreType.DMA((27,)),
        pltpu.SemaphoreType.DMA((2 * ngy + group,)),
        pltpu.SemaphoreType.DMA((2 * ngy + group,)),
    ]

    def per_device(features, cotangent, skip_weight, bias_vector, mode_factors, in_factors, out_factors):
        tables = [jnp.asarray(TABLES[n]) for n in NAMES]
        result, red = pl.pallas_call(
            lambda *refs: layer_kernel(sizes, *refs),
            name="layer",
            out_shape=(jax.ShapeDtypeStruct((576, 768), F32), jax.ShapeDtypeStruct((PAY, 128), F32)),
            in_specs=[any_spec] * (7 + len(NAMES)),
            out_specs=(any_spec, any_spec),
            scratch_shapes=scratch,
            compiler_params=pltpu.CompilerParams(
                collective_id=0, has_side_effects=True, vmem_limit_bytes=60 * 1024 * 1024
            ),
            cost_estimate=pl.CostEstimate(flops=32 * 10**9, bytes_accessed=20 * 10**6, transcendentals=442368),
        )(
            features.reshape(576, 768),
            cotangent.reshape(576, 768),
            skip_weight,
            bias_vector.reshape(1, CH),
            mode_factors,
            in_factors,
            jnp.swapaxes(out_factors, 1, 2),
            *tables,
        )
        outs = pl.pallas_call(
            unpack_kernel,
            name="unpack",
            out_shape=(
                jax.ShapeDtypeStruct((576, 768), F32),
                jax.ShapeDtypeStruct((CH, CH), F32),
                jax.ShapeDtypeStruct((1, CH), F32),
                jax.ShapeDtypeStruct((3, 3, MD, RK), F32),
                jax.ShapeDtypeStruct((3, CH, RK), F32),
                jax.ShapeDtypeStruct((3, CH, RK), F32),
            ),
            in_specs=[any_spec] * 2,
            out_specs=(any_spec,) * 6,
            scratch_shapes=[
                pltpu.VMEM((PAY, 128), F32),
                pltpu.VMEM((576, 768), F32),
                pltpu.VMEM((CH, CH), F32),
                pltpu.VMEM((1, CH), F32),
                pltpu.VMEM((3, 3, MD, RK), F32),
                pltpu.VMEM((3, CH, RK), F32),
                pltpu.VMEM((3, CH, RK), F32),
                pltpu.SemaphoreType.DMA((18,)),
            ],
        )(result, red)
        return (outs[0].reshape(NP, NP, NP * CH), outs[1], outs[2].reshape(CH), outs[3], outs[4], jnp.swapaxes(outs[5], 1, 2))

    placed = (P("gx", "gy", "gz"), P("gx", "gy", "gz"), P(), P(), P(), P(), P())
    return jax.shard_map(
        per_device,
        mesh=mesh,
        in_specs=placed,
        out_specs=(P("gx", "gy", "gz"), P(), P(), P(), P(), P()),
        check_vma=False,
    )
```

```python
import math

import jax
import jax.numpy as jnp
import ml_dtypes
import numpy as np
from jax import lax
from jax.experimental import pallas as pl
from jax.experimental.pallas import tpu as pltpu
from jax.sharding import PartitionSpec as P

MESH = pl.DeviceIdType.MESH
BF = jnp.bfloat16
F32 = jnp.float32
CH, RK, MD, NP = 32, 64, 16, 24
NN = (((1,), (0,)), ((), ()))
NT = (((1,), (1,)), ((), ()))
TN = (((0,), (0,)), ((), ()))
PAY = 192


def basis(length):
    rows = np.arange(MD)
    freq = np.where(rows < MD // 2, rows, rows - MD // 2 + 1).astype(np.float64)
    phase = 2.0 * math.pi / length * freq[:, None] * np.arange(length)[None, :]
    wave = np.where((rows < MD // 2)[:, None], np.cos(phase), np.sin(phase))
    return wave * math.sqrt(2.0 / length)


def halves(x):
    x = np.asarray(x, np.float32)
    hi = x.astype(ml_dtypes.bfloat16)
    lo = (x - hi.astype(np.float32)).astype(ml_dtypes.bfloat16)
    return hi, lo


def left(x):
    hi, lo = halves(x)
    return np.concatenate([hi, hi, lo], axis=1)


def right(x):
    hi, lo = halves(x)
    return np.concatenate([hi, lo], axis=0)


def exact(x, times, axis):
    x = np.asarray(x, np.float32).astype(ml_dtypes.bfloat16)
    return np.concatenate([x] * times, axis=axis)


def channel_eye(b):
    return np.kron(b, np.eye(CH))


def make_tables():
    b24, b18 = basis(24), basis(18)
    pool = np.zeros((208, 12, 24))
    for j in range(2):
        for i in range(2):
            for r in range(36):
                x, y = i * 6 + r // 6, 2 * (j * 6 + r % 6)
                pool[(j * 2 + i) * 40 + r, x, y : y + 2] = 1 / 8
    for r in range(36):
        x, y = 2 * (r // 6), 4 * (r % 6)
        pool[160 + r, x : x + 2, y : y + 4] = 1 / 64
    pool = pool.reshape(208, 288)
    pair = channel_eye(np.kron(np.eye(4), np.ones((2, 1))))
    quad = np.zeros((24, 8))
    for z in range(24):
        quad[z, z // 4] = 1
    quad = channel_eye(quad)
    xy0 = np.kron(b24, b24)
    at4, at3 = (1, 2, 0, 3), (1, 0, 2)
    xy1 = np.zeros((256, 4, 4, 40))
    for j in range(4):
        for i in range(4):
            for r in range(36):
                xy1[:, j, i, r] = np.kron(b24[:, at4[i] * 6 + r // 6], b24[:, at4[j] * 6 + r % 6])
    xy2 = np.zeros((256, 368))
    for j in range(3):
        for i in range(3):
            for r in range(36):
                xy2[:, (j * 3 + i) * 40 + r] = np.kron(
                    b18[:, at3[i] * 6 + r // 6], b18[:, at3[j] * 6 + r % 6]
                )
    z0 = channel_eye(b24.T)
    z1s, z2s = [], []
    for gz in range(2):
        z1 = np.zeros((20, 16))
        z1[0:12] = b24[:, 6:18].T
        if gz == 0:
            z1[12:18] = b24[:, 18:24].T
        else:
            z1[12:16] = b24[:, 2:6].T
            z1[16:18] = b24[:, 0:2].T
        z1s.append(right(channel_eye(z1)))
        z2 = np.zeros((16, 16))
        z2[0:6] = b18[:, 6:12].T
        z2[8:14] = b18[:, 12:18].T if gz == 0 else b18[:, 0:6].T
        z2s.append(right(channel_eye(z2)))
    z1c = channel_eye(b24[:, 6:18])
    z2c = channel_eye(np.repeat(b18[:, 6:12], 2, axis=1))
    c1 = b24[:, 6:18]
    c2 = np.repeat(b18[:, 6:12], 2, axis=1)
    xy12 = np.concatenate([np.kron(c1, c1), np.kron(c2, c2)], axis=0)
    return {
        "pool": exact(pool, 2, 1),
        "pair": exact(pair, 2, 0),
        "quad": exact(quad, 2, 0),
        "unpair": exact(pair.T, 2, 0),
        "xy0": left(xy0),
        "z0": right(z0),
        "z0t": right(z0.T),
        "inv": left(xy0.T),
        "xy1": left(xy1.reshape(256, 640)),
        "z1": np.concatenate(z1s, axis=0),
        "xy2": left(xy2),
        "z2": np.concatenate(z2s, axis=0),
        "z1c": right(z1c),
        "z2c": right(z2c),
        "xy12": left(xy12.T),
        "xy12t": left(xy12),
        "z2ct": right(z2c.T),
    }


TABLES = make_tables()
NAMES = list(TABLES)


def table_shape(name):
    rows, cols = TABLES[name].shape
    return (rows // 2 if name in ("z1", "z2") else rows), cols


def dot(a, b, dims=NN):
    return lax.dot_general(a, b, dims, preferred_element_type=F32)


def split(x):
    hi = x.astype(BF)
    return hi, (x - hi.astype(F32)).astype(BF)


def rows_cat(*parts):
    return jnp.concatenate(parts, axis=0)


def lanes_cat(*parts):
    return jnp.concatenate(parts, axis=1)


def iota(shape, dim):
    return lax.broadcasted_iota(jnp.int32, shape, dim)


def fold_lanes(x):
    total = x[:, 0:128]
    for k in range(1, x.shape[1] // 128):
        total = total + x[:, 128 * k : 128 * (k + 1)]
    return total + pltpu.roll(total, 64, 1)


def layer_kernel(sizes, *refs):
    ngx, ngy, ngz = sizes
    refs = list(refs)
    take = lambda n: [refs.pop(0) for _ in range(n)]
    feat_hbm, cot_hbm = take(2)
    weights_hbm = take(5)
    hbm = dict(zip(NAMES, take(len(NAMES))))
    result_hbm, red_hbm = take(2)
    tab = dict(zip(NAMES, take(len(NAMES))))
    (feat, cot, result, fs, half, quart, hs, qs, kh, kl, pr, rh, rl, qh, ql, th, tl, bs, t12, pre, gs, gqh, gql, ghh, ghl,
     wide, down, g12h, g12l, um, m2r, m0t, m1t, inw, outw, outt, skw, biast, gskip, gbias, pay, ra, rb, acc, red, zsend, zrecv, qth, qtl, fst, kt, kown, strips, sh, sl,
     skip_ref, bias_ref, modes_ref, in_ref, out_ref) = take(60)
    table_sem, local_sem, halo_send, halo_recv, red_send, red_recv = take(6)

    gx, gy, gz = lax.axis_index("gx"), lax.axis_index("gy"), lax.axis_index("gz")
    me = gx * ngz + gz
    group = ngx * ngz

    thirds = [slice(256 * n, 256 * (n + 1)) for n in range(3)]
    load_f = [
        pltpu.make_async_copy(feat_hbm.at[:, pl.ds(256 * n, 256)], feat.at[:, pl.ds(256 * n, 256)], local_sem.at[9 + n])
        for n in range(3)
    ]
    for c in load_f:
        c.start()
    load_c = pltpu.make_async_copy(cot_hbm, cot, local_sem.at[1])
    loads = {}
    for k, name in enumerate(NAMES):
        rows = table_shape(name)[0]
        src = hbm[name].at[pl.ds(pl.multiple_of(gz * rows, 16), rows)] if name in ("z1", "z2") else hbm[name]
        loads[name] = pltpu.make_async_copy(src, tab[name], table_sem.at[k])
        if k < 3:
            loads[name].start()
    load_w = [
        pltpu.make_async_copy(src, dst, local_sem.at[3 + k])
        for k, (src, dst) in enumerate(zip(weights_hbm, (skip_ref, bias_ref, modes_ref, in_ref, out_ref)))
    ]
    for c in load_w:
        c.start()

    barrier = pltpu.get_barrier_semaphore()

    def greet_row(k, carry):
        pl.semaphore_signal(
            barrier, inc=1, device_id=(gx, lax.rem(gy + k, ngy), gz), device_id_type=MESH
        )
        return carry

    lax.fori_loop(1, ngy, greet_row, 0)

    def greet_plane(k, carry):
        q = lax.rem(me + k, group)
        pl.semaphore_signal(
            barrier, inc=1, device_id=(q // ngz, gy, lax.rem(q, ngz)), device_id_type=MESH
        )
        return carry

    lax.fori_loop(1, group, greet_plane, 0)

    def clear(j, i):
        half[j, i] = jnp.zeros((40, 640), F32)

    def clear_quarter(j, i):
        quart[j, i] = jnp.zeros((40, 512), F32)

    for edge, block in ((gx == 0, 2), (gx == ngx - 1, 3)):

        @pl.when(edge)
        def _():
            clear(0, block)
            clear(1, block)
            clear_quarter(0, block - 1)

    for edge, block in ((gy == 0, 2), (gy == ngy - 1, 3)):

        @pl.when(edge)
        def _():
            for i in range(4):
                clear(block, i)
            for i in range(3):
                clear_quarter(block - 1, i)

    loads["pool"].wait()
    loads["pair"].wait()
    for n, cols in enumerate(thirds):
        load_f[n].wait()
        if n == 2:
            for name in NAMES[3:]:
                loads[name].start()
                if name == "xy2":
                    load_c.start()
        cells = feat[:, cols].reshape(12, 2, 24, 256)
        hi, lo = split((cells[:, 0] + cells[:, 1]).reshape(288, 256))
        hi, lo = split(dot(tab["pool"][...], rows_cat(hi, lo)))
        strips[0, :, cols] = hi[160:208]
        strips[1, :, cols] = lo[160:208]
        cells = dot(lanes_cat(hi[0:160], lo[0:160]), tab["pair"][...])
        for j in range(2):
            for i in range(2):
                r = (j * 2 + i) * 40
                half[j, i, :, 128 * n : 128 * (n + 1)] = cells[r : r + 40]
    for i in range(2):
        a, b = half[0, i, :, 128:256], half[1, i, :, 128:256]
        a = jnp.where(gz == 1, a, pltpu.roll(a, 64, 1))
        b = jnp.where(gz == 1, pltpu.roll(b, 64, 1), b)
        zsend[i] = jnp.where(iota((40, 128), 1) < 64, a, b)

    pl.semaphore_wait(barrier, ngy - 1 + group - 1)

    def remote(k, src, dst, to):
        return pltpu.make_async_remote_copy(
            src_ref=src,
            dst_ref=dst,
            send_sem=halo_send.at[k],
            recv_sem=halo_recv.at[k],
            device_id=to,
            device_id_type=MESH,
        )

    first = pl.multiple_of(256 * (1 - gz), 128)
    own, full, rest = pl.ds(0, 384), pl.ds(384, 128), pl.ds(512, 128)
    qown, qfar = pl.ds(0, 256), pl.ds(256, 256)
    mid, side = pl.ds(0, 2), pl.ds(2, 2)
    qside = pl.ds(1, 2)
    across = (gx, gy, 1 - gz)
    z_all = [
        remote(0, half.at[mid, mid, :, pl.ds(first, 128)], half.at[mid, mid, :, pl.ds(384, 128)], across),
        remote(1, zsend, zrecv, across),
        remote(2, quart.at[0, 0, :, qown], quart.at[0, 0, :, qfar], across),
    ]

    def x_copies(k, src, dst, to):
        return [
            remote(k, half.at[mid, src, :, own], half.at[mid, dst, :, own], to),
            remote(k + 1, quart.at[0, 0, :, qown], quart.at[0, dst - 1, :, qown], to),
            remote(k + 2, half.at[mid, src, :, full], half.at[mid, dst, :, full], to),
            remote(k + 3, half.at[mid, src, :, rest], half.at[mid, dst, :, rest], to),
            remote(k + 4, quart.at[0, 0, :, qfar], quart.at[0, dst - 1, :, qfar], to),
        ]

    def y_copies(k, src, dst, to):
        return [
            remote(k, half.at[src, mid, :, own], half.at[dst, mid, :, own], to),
            remote(k + 1, quart.at[0, 0, :, qown], quart.at[dst - 1, 0, :, qown], to),
            remote(k + 2, half.at[src, side, :, own], half.at[dst, side, :, own], to),
            remote(k + 3, quart.at[0, qside, :, qown], quart.at[dst - 1, qside, :, qown], to),
            remote(k + 4, half.at[src, mid, :, full], half.at[dst, mid, :, full], to),
            remote(k + 5, half.at[src, side, :, full], half.at[dst, side, :, full], to),
            remote(k + 6, half.at[src, mid, :, rest], half.at[dst, mid, :, rest], to),
            remote(k + 7, quart.at[0, 0, :, qfar], quart.at[dst - 1, 0, :, qfar], to),
            remote(k + 8, half.at[src, side, :, rest], half.at[dst, side, :, rest], to),
            remote(k + 9, quart.at[0, qside, :, qfar], quart.at[dst - 1, qside, :, qfar], to),
        ]

    xs = x_copies(3, 1, 2, (gx + 1, gy, gz)), x_copies(8, 0, 3, (gx - 1, gy, gz))
    ys = y_copies(13, 1, 2, (gx, gy + 1, gz)), y_copies(23, 0, 3, (gx, gy - 1, gz))

    def each(copies, which, to_up, to_down, act):
        @pl.when(to_up)
        def _():
            for k in which:
                act(copies[0][k])

        @pl.when(to_down)
        def _():
            for k in which:
                act(copies[1][k])

    has_ux, has_dx, has_uy, has_dy = gx < ngx - 1, gx > 0, gy < ngy - 1, gy > 0
    start = lambda c: c.start()
    recv = lambda c: c.wait_recv()
    sent = lambda c: c.wait_send()

    z_all[0].start()
    z_all[1].start()
    loads["quad"].wait()
    cells = dot(lanes_cat(strips[0], strips[1]), tab["quad"][...])
    quart[0, 0, :, 0:256] = cells[0:40]
    z_all[2].start()
    each(xs, (0, 1), has_ux, has_dx, start)
    each(ys, (0, 1), has_uy, has_dy, start)

    for c in load_w:
        c.wait()

    def dup64(x):
        eye = (iota((64, 128), 0) == iota((64, 128), 1) % 64).astype(BF)
        return dot(x, eye)

    def dup32(x):
        eye = (iota((32, 128), 0) == iota((32, 128), 1) % 32).astype(BF)
        return dot(x, eye)

    diag_ir = iota((128, 256), 0) // 32 == iota((128, 256), 1) // 64
    diag_ro = iota((256, 128), 0) // 64 == iota((256, 128), 1) // 32
    diag_io = iota((128, 128), 0) // 32 == iota((128, 128), 1) // 32
    eye64 = (iota((64, 64), 0) == iota((64, 64), 1)).astype(BF)

    b0, b1 = split(jnp.broadcast_to(bias_ref[...], (16, 32)))
    biast[...] = (dup32(b0) + dup32(b1))[0:8]
    w0, w1 = [jnp.where(diag_io, rows_cat(*[dup32(w)] * 4), 0.0).astype(BF) for w in split(skip_ref[...])]
    w0 = lanes_cat(w0, w1)
    skw[...] = rows_cat(w0, w0)

    def spread(l, carry):
        i0, i1 = split(in_ref[l])
        o0, o1 = split(out_ref[l])

        def wide(w):
            t = dup64(w)
            return jnp.where(diag_ir, rows_cat(*[lanes_cat(t, t)] * 4), 0.0).astype(BF)

        def tall(w):
            t = dup32(dot(eye64, w, NT).astype(BF))
            return jnp.where(diag_ro, rows_cat(*[t] * 4), 0.0).astype(BF)

        w0 = wide(i0)
        inw[l] = rows_cat(w0, w0, wide(i1))
        w0 = wide(o0)
        outt[l] = rows_cat(w0, w0, wide(o1))
        w0 = lanes_cat(tall(o0), tall(o1))
        outw[l] = rows_cat(w0, w0)
        dup = []
        for d in range(3):
            m = modes_ref[l, d]
            hi, lo = split(m)
            rest = (m - hi.astype(F32) - lo.astype(F32)).astype(BF)
            dup.append(dup64(hi) + dup64(lo) + dup64(rest))
        m0t[l] = dup[0]
        m1t[l] = dup[1]
        um[l] = (dup[0][:, None, :] * dup[1][None, :, :]).reshape(256, 128)
        line = lanes_cat(*[dup[2]] * 8)
        line = jnp.where(iota((16, 1024), 0) == iota((16, 1024), 1) // 64, line, 0.0)
        m2r[l] = jnp.broadcast_to(jnp.sum(line, axis=0, keepdims=True), (8, 1024))
        return carry

    for l in range(3):
        spread(l, 0)

    hi, lo = split(feat[...])
    fs[0:576] = hi
    fs[576:1152] = lo

    def stacked(ref):
        parts = [slice(128 * n, 128 * (n + 1)) for n in range(6)]
        return rows_cat(*[lanes_cat(ref[0:576, c], ref[576:1152, c]) for c in parts])

    def xy_transform(table, hi_lo, rows, chunks, wide):
        for n in range(chunks):
            cols = slice(wide * n, wide * (n + 1))
            data = rows_cat(hi_lo[0 : 2 * rows, cols], hi_lo[0:rows, cols])
            hi, lo = split(dot(table[...], data))
            th[:, cols] = hi
            tl[:, cols] = lo

    def z_transform(hi, lo, table, depth, into_h, into_l, l, parts=None):
        a = lanes_cat(hi, lo, hi)
        zh, zl = (0, depth) if parts is None else parts
        for n in range(2):
            cols = slice(256 * n, 256 * (n + 1))
            tz = rows_cat(table[zh : zh + depth, cols], table[zh : zh + depth, cols], table[zl : zl + depth, cols])
            vh, vl = split(dot(a, tz))
            into_h[l, :, cols] = vh
            into_l[l, :, cols] = vl

    quads = [(slice(128 * c, 128 * (c + 1)), slice(256 * c, 256 * (c + 1))) for c in range(4)]

    def modes_forward(l):
        data = [(kh[l, :, c], kl[l, :, c]) for c, _ in quads]
        kt[l] = jnp.transpose(rows_cat(*[lanes_cat(a, b) for a, b in data]))
        p = dot(rows_cat(*[lanes_cat(a, b, a) for a, b in data]), inw[l])
        u = um[l]
        u = lanes_cat(u, u)
        data = []
        for k, (_, cols) in enumerate(quads):
            pk = p[256 * k : 256 * (k + 1)]
            pr[l, :, cols] = pk
            a, b = split(pk * u * m2r[l, 0:1, cols])
            rh[l, :, cols] = a
            rl[l, :, cols] = b
            data.append(lanes_cat(a, b))
        q = dot(rows_cat(*data), outw[l])
        q = q[:, 0:128] + q[:, 128:256]
        for k, (cols, _) in enumerate(quads):
            a, b = split(q[256 * k : 256 * (k + 1)])
            qh[l, :, cols] = a
            ql[l, :, cols] = b

    v = stacked(fs)
    fst[...] = jnp.transpose(v)
    v = dot(v, skw[...])
    v = v[:, 0:128] + v[:, 128:256] + biast[0:1]
    for n in range(6):
        pre[:, 128 * n : 128 * (n + 1)] = v[576 * n : 576 * (n + 1)]
    loads["xy0"].wait()
    xy_transform(tab["xy0"], fs, 576, 3, 256)

    each(xs, (0, 1), has_dx, has_ux, recv)
    each(ys, (2, 3), has_uy, has_dy, start)
    z_all[0].wait_recv()
    each(xs, (2,), has_ux, has_dx, start)
    each(ys, (4,), has_uy, has_dy, start)

    loads["z0"].wait()
    z_transform(th[...], tl[...], tab["z0"], 768, kh, kl, 0)

    for c in z_all[1:]:
        c.wait_recv()
    low = iota((40, 128), 1) < 64
    for i in range(2):
        a = zrecv[i]
        half[0, i, :, 512:640] = jnp.where(low, a, 0.0)
        half[1, i, :, 512:640] = jnp.where(low, pltpu.roll(a, 64, 1), 0.0)
    each(xs, (3, 4), has_ux, has_dx, start)
    each(ys, (6, 7), has_uy, has_dy, start)

    modes_forward(0)

    each(xs, (2,), has_dx, has_ux, recv)
    each(ys, (5,), has_uy, has_dy, start)
    loads["z0t"].wait()
    a = lanes_cat(qh[0], ql[0], qh[0])
    for n in range(3):
        cols = slice(256 * n, 256 * (n + 1))
        tz = rows_cat(tab["z0t"][0:512, cols], tab["z0t"][0:512, cols], tab["z0t"][512:1024, cols])
        hi, lo = split(dot(a, tz))
        bs[0:256, cols] = hi
        bs[256:512, cols] = lo
    each(xs, (3, 4), has_dx, has_ux, recv)
    each(ys, (8, 9), has_uy, has_dy, start)
    loads["inv"].wait()
    for n in range(3):
        cols = slice(256 * n, 256 * (n + 1))
        pre[:, cols] = pre[:, cols] + dot(tab["inv"][...], rows_cat(bs[0:512, cols], bs[0:256, cols]))

    def halves_of(cols, qcols):
        for j in range(4):
            hi, lo = split(half[j, :, :, cols].reshape(160, -1))
            hs[160 * j : 160 * (j + 1), cols] = hi
            hs[640 + 160 * j : 640 + 160 * (j + 1), cols] = lo
        cells = quart[:, :, :, qcols].reshape(360, 256)
        hi, lo = split(rows_cat(cells, jnp.zeros((8, 256), F32)))
        qs[0:368, qcols] = hi
        qs[368:736, qcols] = lo

    def one_chunk(table, data, rows, cols, into_h, into_l):
        v = rows_cat(data[0 : 2 * rows, cols], data[0:rows, cols])
        hi, lo = split(dot(table[...], v))
        into_h[:, cols] = hi
        into_l[:, cols] = lo

    each(ys, (0, 1, 2, 3), has_dy, has_uy, recv)
    halves_of(slice(0, 384), slice(0, 256))
    loads["xy1"].wait()
    loads["xy2"].wait()
    one_chunk(tab["xy1"], hs, 640, slice(0, 256), th, tl)
    v = lanes_cat(hs[0:640, 256:384], hs[640:1280, 256:384])
    v = dot(tab["xy1"][:, 640:1920], rows_cat(v, v))
    hi, lo = split(v[:, 0:128] + v[:, 128:256])
    th[:, 256:384] = hi
    tl[:, 256:384] = lo
    one_chunk(tab["xy2"], qs, 368, slice(0, 256), qth, qtl)

    def z_product(hi, lo, table, first, rows, depth):
        tz = table[first : first + depth]
        return dot(lanes_cat(hi, lo, hi), rows_cat(tz, tz, table[rows + first : rows + first + depth]))

    loads["z1"].wait()
    loads["z2"].wait()
    kown[0] = z_product(th[:, 0:384], tl[:, 0:384], tab["z1"], 0, 640, 384)
    kown[1] = z_product(qth[:, 0:256], qtl[:, 0:256], tab["z2"], 0, 512, 256)

    for name in ("z1c", "z2c", "xy12", "unpair", "xy12t", "z2ct"):
        loads[name].wait()
    load_c.wait()
    each(ys, range(4, 10), has_dy, has_uy, recv)
    halves_of(slice(384, 640), slice(256, 512))
    one_chunk(tab["xy1"], hs, 640, slice(384, 640), th, tl)
    one_chunk(tab["xy2"], qs, 368, slice(256, 512), qth, qtl)
    hi, lo = split(kown[0] + z_product(th[:, 384:640], tl[:, 384:640], tab["z1"], 384, 640, 256))
    kh[1] = hi
    kl[1] = lo
    hi, lo = split(kown[1] + z_product(qth[:, 256:512], qtl[:, 256:512], tab["z2"], 256, 512, 256))
    kh[2] = hi
    kl[2] = lo
    for l in (1, 2):
        modes_forward(l)

    for l, name in ((1, "z1c"), (2, "z2c")):
        tz = tab[name]
        v = dot(lanes_cat(qh[l], ql[l], qh[l]), rows_cat(tz[0:512], tz[0:512], tz[512:1024]))
        hi, lo = split(v)
        t12[256 * (l - 1) : 256 * l] = hi
        t12[512 + 256 * (l - 1) : 512 + 256 * l] = lo
    s = dot(tab["xy12"][...], rows_cat(t12[...], t12[0:512]))

    scale = 1.0 / math.sqrt(ngx * ngy * ngz * NP**3)
    c0 = math.sqrt(2.0 / math.pi)
    sums = []
    for n in range(3):
        cols = slice(256 * n, 256 * (n + 1))
        hi, lo = split(s[:, 128 * n : 128 * (n + 1)])
        v = dot(lanes_cat(hi, lo), tab["unpair"][...])
        for k in range(2):
            for step in range(2):
                wide[2 * n + k, pl.ds(step, 144, stride=2), :] = v[:, 128 * k : 128 * (k + 1)]
        colsum = jnp.zeros((8, 256), F32)
        for m in range(12):
            rows, pair = slice(48 * m, 48 * (m + 1)), slice(24 * m, 24 * (m + 1))
            v = lanes_cat(wide[2 * n, pair], wide[2 * n + 1, pair])
            x = pre[rows, cols] + rows_cat(v, v)
            x2 = x * x
            t = jnp.tanh(x * (c0 + (c0 * 0.044715) * x2))
            half_t = 0.5 + 0.5 * t
            result[rows, cols] = x * half_t
            slope = half_t + x * (1.0 - t * t) * (0.5 * c0 + (1.5 * c0 * 0.044715) * x2)
            g = cot[rows, cols] * scale * slope
            hi, lo = split(g)
            gs[rows, cols] = hi
            gs[576 + 48 * m : 576 + 48 * (m + 1), cols] = lo
            g2 = g[0:24] + g[24:48]
            down[2 * n, pair] = g2[:, 0:128]
            down[2 * n + 1, pair] = g2[:, 128:256]
            colsum = colsum + jnp.sum(g.reshape(6, 8, 256), axis=0)
        sums.append(colsum)
        one_chunk(tab["xy0"], gs, 576, cols, th, tl)
        v = [down[2 * n + k, pl.ds(0, 144, stride=2), :] + down[2 * n + k, pl.ds(1, 144, stride=2), :] for k in range(2)]
        hi, lo = split(lanes_cat(*v))
        hi, lo = split(dot(lanes_cat(hi, lo), tab["pair"][...]))
        ghh[:, 128 * n : 128 * (n + 1)] = hi
        ghl[:, 128 * n : 128 * (n + 1)] = lo
    store = pltpu.make_async_copy(result, result_hbm, local_sem.at[2])
    store.start()
    gbias[...] = fold_lanes(lanes_cat(*sums))

    z_transform(th[...], tl[...], tab["z0"], 768, gqh, gql, 0)
    hi, lo = split(dot(tab["xy12t"][...], rows_cat(ghh[...], ghl[...], ghh[...])))
    g12h[...] = hi
    g12l[...] = lo
    z_transform(g12h[0:256], g12l[0:256], tab["z1"], 384, gqh, gql, 1, (0, 640))
    z_transform(g12h[256:512], g12l[256:512], tab["z2ct"], 384, gqh, gql, 2)

    def skip_gradient():
        total = dot(fst[...], stacked(gs))
        total = total[0:128] + total[128:256]
        total = jnp.where(diag_io, total[:, 0:128] + total[:, 128:256], 0.0)
        s = total[0:32] + total[32:64] + total[64:96] + total[96:128]
        s = s + pltpu.roll(s, 64, 1)
        gskip[...] = s + pltpu.roll(s, 32, 1)

    def gram(at, bh, bl):
        g = dot(at, rows_cat(*[lanes_cat(bh[:, c], bl[:, c]) for _, c in quads]))
        g = g[0:128] + g[128:256]
        g = jnp.where(diag_ir, g[:, 0:256] + g[:, 256:512], 0.0)
        return fold_lanes(g[0:32] + g[32:64] + g[64:96] + g[96:128])

    low = iota((32, 128), 1) < 64

    def rank_cotangents(l):
        data = [(gqh[l, :, c], gql[l, :, c]) for c, _ in quads]
        return dot(rows_cat(*[lanes_cat(a, b, a) for a, b in data]), outt[l])

    def weigh(l, g):
        u = um[l]
        u = lanes_cat(u, u)
        e = jnp.zeros((256, 128), F32)
        g2 = []
        for k, (_, cols) in enumerate(quads):
            gr = g[256 * k : 256 * (k + 1)]
            d = gr * pr[l, :, cols]
            m2 = m2r[l, 0:1, cols]
            dm = d * m2
            e = e + dm[:, 0:128] + dm[:, 128:256]
            g2.append(jnp.sum((d * u).reshape(32, 8, 256), axis=0))
            hi, lo = split(gr * (u * m2))
            sh[l, :, cols] = hi
            sl[l, :, cols] = lo
        e = (e + pltpu.roll(e, 64, 1)).reshape(16, 16, 128)
        g0 = jnp.sum(e * m1t[l][None, :, :], axis=1)
        g1 = jnp.sum(e * m0t[l][:, None, :], axis=0)
        g2 = jnp.sum(lanes_cat(*g2), axis=0, keepdims=True)
        g2 = jnp.where(iota((16, 1024), 0) == iota((16, 1024), 1) // 64, g2, 0.0)
        row = 64 * l
        pay[row + 32 : row + 48] = jnp.where(low[0:16], g0, g1)
        pay[row + 48 : row + 64] = jnp.where(low[0:16], fold_lanes(g2), 0.0)

    def factors(l):
        data = [(gqh[l, :, c], gql[l, :, c]) for c, _ in quads]
        g_out = gram(jnp.transpose(rows_cat(*[lanes_cat(a, b) for a, b in data])), rh.at[l], rl.at[l])
        g_in = gram(kt[l], sh.at[l], sl.at[l])
        pay[64 * l : 64 * l + 32] = jnp.where(low, g_in, g_out)

    g0 = rank_cotangents(0)
    g1 = rank_cotangents(1)
    weigh(0, g0)
    factors(0)
    g2 = rank_cotangents(2)
    weigh(1, g1)
    factors(1)
    weigh(2, g2)
    skip_gradient()
    factors(2)
    s = gskip[...]
    s = jnp.where(iota((16, 128), 1) < 96, s[0:16], s[16:32])
    pay[48:64] = jnp.where(low[0:16], pay[48:64], s)
    b = gbias[...] + pltpu.roll(gbias[...], 32, 1)
    b = jnp.broadcast_to(jnp.sum(b, axis=0, keepdims=True), (16, 128))
    pay[112:128] = jnp.where(low[0:16], pay[112:128], b)

    size = PAY // ngy

    def pushes(count, make, act):
        def body(k, carry):
            act(make(k))
            return carry

        lax.fori_loop(1, count, body, 0)

    def scatter(k):
        t = lax.rem(gy + k, ngy)
        return pltpu.make_async_remote_copy(
            src_ref=pay.at[pl.ds(pl.multiple_of(t * size, 8), size)],
            dst_ref=ra.at[k],
            send_sem=red_send.at[k],
            recv_sem=red_recv.at[k],
            device_id=(gx, t, gz),
            device_id_type=MESH,
        )

    def exchange(k):
        q = lax.rem(me + k, group)
        return pltpu.make_async_remote_copy(
            src_ref=acc,
            dst_ref=rb.at[me],
            send_sem=red_send.at[ngy + k],
            recv_sem=red_recv.at[ngy + k],
            device_id=(q // ngz, gy, lax.rem(q, ngz)),
            device_id_type=MESH,
        )

    mine = pl.ds(pl.multiple_of(gy * size, 8), size)

    def gather(k):
        t = lax.rem(gy + k, ngy)
        return pltpu.make_async_remote_copy(
            src_ref=red.at[mine],
            dst_ref=red.at[mine],
            send_sem=red_send.at[ngy + group + k],
            recv_sem=red_recv.at[ngy + group + k],
            device_id=(gx, t, gz),
            device_id_type=MESH,
        )

    for k in range(1, ngy):
        scatter(k).start()
    pushes(ngy, scatter, recv)
    total = pay[mine]
    for k in range(1, ngy):
        total = total + ra[k]
    acc[...] = total
    rb[me] = total
    for k in range(1, group):
        exchange(k).start()
    pushes(group, exchange, recv)
    total = rb[0]
    for k in range(1, group):
        total = total + rb[k]
    red[mine] = total
    for k in range(1, ngy):
        gather(k).start()
    pushes(ngy, gather, recv)
    store_red = pltpu.make_async_copy(red, red_hbm, local_sem.at[8])
    store_red.start()

    pushes(ngy, scatter, sent)
    pushes(group, exchange, sent)
    pushes(ngy, gather, sent)
    for c in z_all:
        c.wait_send()
    each(xs, range(5), has_ux, has_dx, sent)
    each(ys, range(10), has_uy, has_dy, sent)
    store.wait()
    store_red.wait()


def unpack_kernel(result_in, red_in, result_out, *refs):
    outs, (red, held), bufs, sem = refs[0:5], refs[5:7], refs[7:12], refs[12]
    skip, bias, modes, fin, fout = bufs
    parts = [pl.ds(96 * k, 96) for k in range(6)]
    fetch_red = pltpu.make_async_copy(red_in, red, sem.at[17])
    fetch_red.start()
    fetch = [pltpu.make_async_copy(result_in.at[p], held.at[p], sem.at[k]) for k, p in enumerate(parts)]
    store = [pltpu.make_async_copy(held.at[p], result_out.at[p], sem.at[6 + k]) for k, p in enumerate(parts)]
    small = [pltpu.make_async_copy(b, o, sem.at[12 + k]) for k, (b, o) in enumerate(zip(bufs, outs))]
    for copy in fetch:
        copy.start()
    fetch_red.wait()
    skip[0:16] = red[48:64, 64:96]
    skip[16:32] = red[48:64, 96:128]
    bias[...] = red[112:113, 64:96]
    for l in range(3):
        row = 64 * l
        fin[l] = red[row : row + 32, 0:64]
        fout[l] = red[row : row + 32, 64:128]
        modes[l, 0] = red[row + 32 : row + 48, 0:64]
        modes[l, 1] = red[row + 32 : row + 48, 64:128]
        modes[l, 2] = red[row + 48 : row + 64, 0:64]
    for copy in small:
        copy.start()
    for a, b in zip(fetch, store):
        a.wait()
        b.start()
    for copy in store + small:
        copy.wait()


def solution(mesh):
    sizes = tuple(mesh.shape[name] for name in ("gx", "gy", "gz"))
    ngx, ngy, ngz = sizes
    group = ngx * ngz
    size = PAY // ngy
    any_spec = pl.BlockSpec(memory_space=pl.ANY)
    scratch = [pltpu.VMEM(table_shape(n), BF) for n in NAMES] + [
        pltpu.VMEM((576, 768), F32),
        pltpu.VMEM((576, 768), F32),
        pltpu.VMEM((576, 768), F32),
        pltpu.VMEM((1152, 768), BF),
        pltpu.VMEM((4, 4, 40, 640), F32),
        pltpu.VMEM((3, 3, 40, 512), F32),
        pltpu.VMEM((1280, 640), BF),
        pltpu.VMEM((736, 512), BF),
        pltpu.VMEM((3, 256, 512), BF),
        pltpu.VMEM((3, 256, 512), BF),
        pltpu.VMEM((3, 256, 1024), F32),
        pltpu.VMEM((3, 256, 1024), BF),
        pltpu.VMEM((3, 256, 1024), BF),
        pltpu.VMEM((3, 256, 512), BF),
        pltpu.VMEM((3, 256, 512), BF),
        pltpu.VMEM((256, 768), BF),
        pltpu.VMEM((256, 768), BF),
        pltpu.VMEM((512, 768), BF),
        pltpu.VMEM((1024, 384), BF),
        pltpu.VMEM((576, 768), F32),
        pltpu.VMEM((1152, 768), BF),
        pltpu.VMEM((3, 256, 512), BF),
        pltpu.VMEM((3, 256, 512), BF),
        pltpu.VMEM((144, 384), BF),
        pltpu.VMEM((144, 384), BF),
        pltpu.VMEM((6, 288, 128), F32),
        pltpu.VMEM((6, 288, 128), F32),
        pltpu.VMEM((512, 384), BF),
        pltpu.VMEM((512, 384), BF),
        pltpu.VMEM((3, 256, 128), F32),
        pltpu.VMEM((3, 8, 1024), F32),
        pltpu.VMEM((3, 16, 128), F32),
        pltpu.VMEM((3, 16, 128), F32),
        pltpu.VMEM((3, 384, 256), BF),
        pltpu.VMEM((3, 512, 256), BF),
        pltpu.VMEM((3, 384, 256), BF),
        pltpu.VMEM((256, 256), BF),
        pltpu.VMEM((8, 128), F32),
        pltpu.VMEM((32, 128), F32),
        pltpu.VMEM((8, 128), F32),
        pltpu.VMEM((PAY, 128), F32),
        pltpu.VMEM((ngy, size, 128), F32),
        pltpu.VMEM((group, size, 128), F32),
        pltpu.VMEM((size, 128), F32),
        pltpu.VMEM((PAY, 128), F32),
        pltpu.VMEM((2, 40, 128), F32),
        pltpu.VMEM((2, 40, 128), F32),
        pltpu.VMEM((256, 512), BF),
        pltpu.VMEM((256, 512), BF),
        pltpu.VMEM((256, 3456), BF),
        pltpu.VMEM((3, 256, 1024), BF),
        pltpu.VMEM((2, 256, 512), F32),
        pltpu.VMEM((2, 48, 768), BF),
        pltpu.VMEM((3, 256, 1024), BF),
        pltpu.VMEM((3, 256, 1024), BF),
        pltpu.VMEM((CH, CH), F32),
        pltpu.VMEM((1, CH), F32),
        pltpu.VMEM((3, 3, MD, RK), F32),
        pltpu.VMEM((3, CH, RK), F32),
        pltpu.VMEM((3, CH, RK), F32),
        pltpu.SemaphoreType.DMA((len(NAMES),)),
        pltpu.SemaphoreType.DMA((12,)),
        pltpu.SemaphoreType.DMA((33,)),
        pltpu.SemaphoreType.DMA((33,)),
        pltpu.SemaphoreType.DMA((2 * ngy + group,)),
        pltpu.SemaphoreType.DMA((2 * ngy + group,)),
    ]

    def per_device(features, cotangent, skip_weight, bias_vector, mode_factors, in_factors, out_factors):
        tables = [jnp.asarray(TABLES[n]) for n in NAMES]
        result, red = pl.pallas_call(
            lambda *refs: layer_kernel(sizes, *refs),
            name="layer",
            out_shape=(jax.ShapeDtypeStruct((576, 768), F32), jax.ShapeDtypeStruct((PAY, 128), F32)),
            in_specs=[any_spec] * (7 + len(NAMES)),
            out_specs=(any_spec, any_spec),
            scratch_shapes=scratch,
            compiler_params=pltpu.CompilerParams(
                collective_id=0, has_side_effects=True, vmem_limit_bytes=60 * 1024 * 1024
            ),
            cost_estimate=pl.CostEstimate(flops=32 * 10**9, bytes_accessed=20 * 10**6, transcendentals=442368),
        )(
            features.reshape(576, 768),
            cotangent.reshape(576, 768),
            skip_weight,
            bias_vector.reshape(1, CH),
            mode_factors,
            in_factors,
            jnp.swapaxes(out_factors, 1, 2),
            *tables,
        )
        outs = pl.pallas_call(
            unpack_kernel,
            name="unpack",
            out_shape=(
                jax.ShapeDtypeStruct((576, 768), F32),
                jax.ShapeDtypeStruct((CH, CH), F32),
                jax.ShapeDtypeStruct((1, CH), F32),
                jax.ShapeDtypeStruct((3, 3, MD, RK), F32),
                jax.ShapeDtypeStruct((3, CH, RK), F32),
                jax.ShapeDtypeStruct((3, CH, RK), F32),
            ),
            in_specs=[any_spec] * 2,
            out_specs=(any_spec,) * 6,
            scratch_shapes=[
                pltpu.VMEM((PAY, 128), F32),
                pltpu.VMEM((576, 768), F32),
                pltpu.VMEM((CH, CH), F32),
                pltpu.VMEM((1, CH), F32),
                pltpu.VMEM((3, 3, MD, RK), F32),
                pltpu.VMEM((3, CH, RK), F32),
                pltpu.VMEM((3, CH, RK), F32),
                pltpu.SemaphoreType.DMA((18,)),
            ],
        )(result, red)
        return (outs[0].reshape(NP, NP, NP * CH), outs[1], outs[2].reshape(CH), outs[3], outs[4], jnp.swapaxes(outs[5], 1, 2))

    placed = (P("gx", "gy", "gz"), P("gx", "gy", "gz"), P(), P(), P(), P(), P())
    return jax.shard_map(
        per_device,
        mesh=mesh,
        in_specs=placed,
        out_specs=(P("gx", "gy", "gz"), P(), P(), P(), P(), P()),
        check_vma=False,
    )
```
